32 devices in a mesh: dp: 8 (over z, y), seq: 4 (over x, core).
Axes of the slice: x: 2, y: 2, z: 4, core: 2. Of those that a mesh axis runs over, the one named last changes fastest.
Arguments:
- tokens: bfloat16 [16, 512, 768], P('dp', 'seq'), may hold values from -6 to 6
- lengths: int32 [8, 2], P('dp'), may hold values from 1 to 512, 640 in all within a row
- cotangent: bfloat16 [16, 512, 768], P('dp', 'seq'), may hold values from -6 to 6
- w_qkv: bfloat16 [768, 2304], replicated, may hold values from -0.21875 to 0.21875
- b_query: float32 [768], replicated, may hold values from -4 to 4
- b_value: float32 [768], replicated, may hold values from -3 to 3
- w_out: bfloat16 [768, 768], replicated, may hold values from -1.75 to 1.75
- b_out: float32 [768], replicated, may hold values from -3 to 3
- first_gain: float32 [768], replicated, may hold values from 0.5 to 1.5
- first_shift: float32 [768], replicated, may hold values from -3 to 3
- w_up: bfloat16 [768, 3072], replicated, may hold values from -0.21875 to 0.21875
- b_up: float32 [3072], replicated, may hold values from -3 to 3
- w_down: bfloat16 [3072, 768], replicated, may hold values from -0.109375 to 0.109375
- b_down: float32 [768], replicated, may hold values from -3 to 3
- second_gain: float32 [768], replicated, may hold values from 0.5 to 1.5
- second_shift: float32 [768], replicated, may hold values from -3 to 3
Outputs:
- output_tokens: bfloat16 [16, 512, 768], P('dp', 'seq')
- grad_tokens: bfloat16 [16, 512, 768], P('dp', 'seq')
- grad_w_qkv: float32 [768, 2304], P('dp', 'seq')
- grad_w_out: float32 [768, 768], P('dp', 'seq')
- grad_w_up: float32 [768, 3072], P('dp', 'seq')
- grad_w_down: float32 [3072, 768], P('dp', 'seq')
- grad_b_query: float32 [768], replicated
- grad_b_value: float32 [768], replicated
- grad_b_out: float32 [768], replicated
- grad_first_gain: float32 [768], replicated
- grad_first_shift: float32 [768], replicated
- grad_b_up: float32 [3072], replicated
- grad_b_down: float32 [768], replicated
- grad_second_gain: float32 [768], replicated
- grad_second_shift: float32 [768], replicated
The draws below stay inside these ranges and needn't reach their ends.
Inputs may be any that keep to these rules, and one draw needn't show every extreme that they name: In each row of lengths the 2 lengths sum to 640.
All inputs are finite; a program needn't handle non-finite values.
Results may differ from the reference program's by a relative error of at most 0.015.
Values may be sent and summed in bfloat16 or wider, within the bound.
A program may use at most 128 MiB of HBM per device.

```python
import math
import jax
import jax.numpy as jnp
import numpy as np
from jax import lax

D = 768
HEADS = 12
HEAD_DIM = 64
FF = 3072
SEQ_LEN = 512
SEQS = 2
GROUPS = 8
SEQUENCES = 16


def spiked(array, stream_key, source, target, blocks, factor):
    def block_of(axis_at):
        return (jnp.arange(array.shape[axis_at]) // (array.shape[axis_at] // blocks)).reshape((-1,) + (1,) * (array.ndim - 1 - axis_at))

    one_side = jax.random.permutation(stream_key, blocks)[block_of(target)]
    other_side = (block_of(target) + blocks // 2) % blocks
    return jnp.where((block_of(source) == one_side) | (block_of(source) == other_side), factor * array, array)


def block_levels(rng, extent, pieces, low, largest):
    loudness = 1.0
    for position, parts in pieces:
        steps = jax.random.uniform(jax.random.fold_in(jax.random.fold_in(rng, 6), position), (parts,), jnp.float32, low / len(pieces), largest / len(pieces))
        loudness = loudness * jnp.repeat(jnp.exp(steps), extent[position] // parts).reshape((-1,) + (1,) * (len(extent) - 1 - position))
    return loudness


def profile(number_of, total, most, skew):
    weights = [(1 << 20) // math.isqrt(standing ** skew) + 1 for standing in range(2, number_of + 1)]
    spare, counts = total - most - (number_of - 1), [1] * (number_of - 1)
    while spare > 0:
        free = [i for i in range(number_of - 1) if counts[i] < most]
        whole, budget = sum([weights[i] for i in free]), spare
        for i in free:
            more = min(most - counts[i], max(1, budget * weights[i] // whole), spare)
            counts[i] = counts[i] + more
            spare = spare - more
    return np.array([most] + counts)


def uneven_parts(own_key, number_of, total, most, skew):
    if number_of == 2:
        one = jax.random.randint(own_key, (), max(1, total - most), min(most, total - 1) + 1)
        return jnp.stack([one, total - one])
    tallies = jnp.asarray(profile(number_of, total, most, skew), jnp.int32)
    pairs = (number_of - 1) // 2
    source_of, taker = tallies[1:1 + 2 * pairs:2], tallies[2:2 + 2 * pairs:2]
    slack = jnp.minimum(source_of - 1, most - taker)
    passed = jax.random.randint(jax.random.fold_in(own_key, 1), (pairs,), 0, 1 << 20) % (slack + 1)
    tallies = tallies.at[1:1 + 2 * pairs:2].set(source_of - passed).at[2:2 + 2 * pairs:2].set(taker + passed)
    return tallies[jax.random.permutation(jax.random.fold_in(own_key, 2), number_of)]


def normal_values(rng, dims, width, bound, split=(), held_as=jnp.bfloat16):
    array = jax.random.normal(rng, dims, jnp.float32) * width
    if len(split) > 0:
        array = block_levels(rng, dims, split, -0.22, 0.18) * array
    return jnp.clip(array, min=-bound, max=bound).astype(held_as)


def noise_with(rng, shape, scale, bound, pieces, heavy, kind=jnp.bfloat16):
    values = scale * jax.random.normal(rng, shape, jnp.float32)
    if pieces:
        values = values * block_levels(rng, shape, pieces, -0.22, 0.18)
    return jnp.clip(spiked(values, jax.random.fold_in(rng, 3), *heavy), -bound, bound).astype(kind)


def setup_inputs(seed: int = 0) -> dict:
    arg_keys = jax.random.split(jax.random.key(seed), 17)
    tokens = normal_values(arg_keys[0], (SEQUENCES, SEQ_LEN, D), 1.0, 6.0, ((0, 8), (1, 4)))
    lengths = jax.vmap(lambda own: uneven_parts(own, SEQS, SEQS * SEQ_LEN * 5 // 8, SEQ_LEN, 1))(jax.random.split(arg_keys[1], GROUPS)).reshape((GROUPS, SEQS)).astype(jnp.int32)
    cotangent = noise_with(arg_keys[2], (SEQUENCES, SEQ_LEN, D), 1.0, 6.0, ((0, 8), (1, 4)), (0, 2, 8, 2.0))
    w_qkv = normal_values(arg_keys[3], (D, 3 * D), D ** -0.5, 0.21875)
    b_query = normal_values(arg_keys[4], (D,), 1.0, 4.0, (), jnp.float32)
    b_value = normal_values(arg_keys[5], (D,), 0.5, 3.0, (), jnp.float32)
    w_out = normal_values(arg_keys[6], (D, D), (D // 64) ** -0.5, 1.75)
    b_out = normal_values(arg_keys[7], (D,), 0.5, 3.0, (), jnp.float32)
    first_gain = jnp.clip(1.0 + 0.1 * jax.random.normal(arg_keys[8], (D,), jnp.float32), 0.5, 1.5)
    first_shift = normal_values(arg_keys[9], (D,), 0.5, 3.0, (), jnp.float32)
    w_up = normal_values(arg_keys[10], (D, FF), D ** -0.5, 0.21875)
    b_up = normal_values(arg_keys[11], (FF,), 0.5, 3.0, (), jnp.float32)
    w_down = normal_values(arg_keys[12], (FF, D), FF ** -0.5, 0.109375)
    b_down = normal_values(arg_keys[13], (D,), 0.5, 3.0, (), jnp.float32)
    second_gain = jnp.clip(1.0 + 0.1 * jax.random.normal(arg_keys[14], (D,), jnp.float32), 0.5, 1.5)
    second_shift = normal_values(arg_keys[15], (D,), 0.5, 3.0, (), jnp.float32)
    return dict(tokens=tokens, lengths=lengths, cotangent=cotangent, w_qkv=w_qkv, b_query=b_query, b_value=b_value, w_out=w_out, b_out=b_out, first_gain=first_gain, first_shift=first_shift, w_up=w_up, b_up=b_up, w_down=w_down, b_down=b_down, second_gain=second_gain, second_shift=second_shift)


EPSILON = 1e-05
FULL_ACCURACY = lax.Precision.HIGHEST

@jax.custom_vjp
def low(v):
    return lax.optimization_barrier(v.astype(jnp.bfloat16)).astype(jnp.float32)

@jax.custom_vjp
def low_back(v):
    return v

def reduced_saved_copy(v):
    return (low(v), None)

def low_pass(kept, grad):
    return (grad,)

def back_keep(v):
    return (v, None)

def back_low(kept, grad):
    return (low(grad),)
low.defvjp(reduced_saved_copy, low_pass)
low_back.defvjp(back_keep, back_low)

def rounded_both(value):
    return low_back(low(value))

def layer_norm(value_rows, gain, shift):
    center = value_rows - lax.optimization_barrier(jnp.mean(value_rows, axis=-1, keepdims=True))
    spread = lax.optimization_barrier(jnp.mean(center * center, axis=-1, keepdims=True))
    return center * lax.rsqrt(spread + EPSILON) * gain + shift

def project(value_rows, weight_matrix):
    return jnp.einsum('yrf,fg->yrg', value_rows, weight_matrix, precision=FULL_ACCURACY)

def attend_sequence(inputs):
    queries, key_block, value_block, length = inputs
    scores = jnp.einsum('qhd,khd->hqk', queries, key_block, precision=FULL_ACCURACY) * HEAD_DIM ** (-0.5)
    scores = low_back(scores)
    usable = jnp.arange(SEQ_LEN, dtype=jnp.int32) < length
    scores = jnp.where(usable[None, None, :], scores, -1e+30)
    weight_tensors = low(jax.nn.softmax(scores, axis=-1))
    return jnp.einsum('hqk,khd->qhd', weight_tensors, value_block, precision=FULL_ACCURACY)

def encoder_layer(params, inputs, group_lengths):
    w_qkv, b_query, b_value, w_out, b_out, first_gain, first_shift, w_up, b_up, w_down, b_down, second_gain, second_shift = params
    joined_bias = jnp.concatenate([b_query, jnp.zeros_like(b_query), b_value])
    mixed = rounded_both(project(inputs, w_qkv) + joined_bias)
    shaped = mixed.reshape(SEQS, SEQ_LEN, 3, HEADS, HEAD_DIM)
    context = lax.map(jax.checkpoint(attend_sequence), (shaped[:, :, 0], shaped[:, :, 1], shaped[:, :, 2], group_lengths))
    context = rounded_both(context.reshape(SEQS, SEQ_LEN, D))
    branch = low_back(project(context, w_out) + b_out)
    hidden = layer_norm(inputs + branch, first_gain, first_shift)
    preactivation_input = low_back(project(low(hidden), w_up) + b_up)
    active = low(jax.nn.gelu(preactivation_input, approximate=False))
    ffn_out = low_back(project(active, w_down) + b_down)
    live = jnp.arange(SEQ_LEN, dtype=jnp.int32)[None, :] < group_lengths[:, None]
    return layer_norm(hidden + ffn_out, second_gain, second_shift) * live[:, :, None].astype(inputs.dtype)

def reference(tokens, lengths, cotangent, w_qkv, b_query, b_value, w_out, b_out, first_gain, first_shift, w_up, b_up, w_down, b_down, second_gain, second_shift):
    params = tuple((item.astype(jnp.float32) for item in (w_qkv, b_query, b_value, w_out, b_out, first_gain, first_shift, w_up, b_up, w_down, b_down, second_gain, second_shift)))
    grouped = tokens.reshape(GROUPS, SEQS, SEQ_LEN, D)
    grouped_cot = cotangent.reshape(GROUPS, SEQS, SEQ_LEN, D)

    def one_group(totals, inputs):
        group_tokens, group_cot, group_lengths = inputs

        def forward(weight_tensors, value_rows):
            return encoder_layer(weight_tensors, value_rows, group_lengths)
        result, pullback = jax.vjp(forward, params, group_tokens.astype(jnp.float32))
        weight_grads, token_grads = pullback(group_cot.astype(jnp.float32))
        totals = jax.tree.map(jnp.add, totals, weight_grads)
        return (totals, (result.astype(jnp.bfloat16), token_grads.astype(jnp.bfloat16)))
    initial = jax.tree.map(jnp.zeros_like, params)
    totals, (outputs, grads) = lax.scan(one_group, initial, (grouped, grouped_cot, lengths))
    return (outputs.reshape(SEQUENCES, SEQ_LEN, D), grads.reshape(SEQUENCES, SEQ_LEN, D), totals[0], totals[3], totals[7], totals[9], totals[1], totals[2], totals[4], totals[5], totals[6], totals[8], totals[10], totals[11], totals[12])
```

```python
import functools

import jax
import jax.numpy as jnp
from jax import lax
from jax.experimental import pallas as pl
from jax.experimental.pallas import tpu as pltpu
from jax.sharding import PartitionSpec as P

MESH_ID = pl.DeviceIdType.MESH
BF16 = jnp.bfloat16
F32 = jnp.float32

HEAD_DIM = 64


EPSILON = 1e-05
ROOT_HALF = 0.7071067811865476
INV_ROOT_TWO_PI = 0.3989422804014327


def contract_rows(left, right):
    return lax.dot_general(
        left, right, (((0,), (0,)), ((), ())), preferred_element_type=jnp.float32
    )


def times_transposed(left, weight_matrix):
    return lax.dot_general(
        left, weight_matrix, (((1,), (1,)), ((), ())), preferred_element_type=jnp.float32
    )


def normalize(value_rows):
    center = value_rows - jnp.mean(value_rows, axis=-1, keepdims=True)
    inverse_root = lax.rsqrt(jnp.mean(center * center, axis=-1, keepdims=True) + EPSILON)
    return (center * inverse_root, inverse_root)


def norm_backward(grad_out, normed, inverse_root, gain):
    scaled = grad_out * gain
    return inverse_root * (
        scaled
        - jnp.mean(scaled, axis=-1, keepdims=True)
        - normed * jnp.mean(scaled * normed, axis=-1, keepdims=True)
    )


def attention_forward_pass(inputs):
    queries, key_block, value_block, key_valid = inputs
    head_scale = queries.shape[-1] ** (-0.5)
    scores = (
        jnp.einsum("qhd,khd->hqk", queries, key_block, preferred_element_type=jnp.float32)
        * head_scale
    )
    scores = jnp.where(key_valid[None, None, :], scores, -1e30)
    highest = jnp.max(scores, axis=-1, keepdims=True)
    exponent = jnp.exp(scores - highest)
    row_total = jnp.sum(exponent, axis=-1, keepdims=True)
    weight_tensors = (exponent / row_total).astype(jnp.bfloat16)
    context = jnp.einsum(
        "hqk,khd->qhd", weight_tensors, value_block, preferred_element_type=jnp.float32
    )
    return (context.astype(jnp.bfloat16), (highest + jnp.log(row_total))[..., 0])


def attend_backward(inputs):
    queries, key_block, value_block, key_valid, log_total, grad_context = inputs
    head_scale = queries.shape[-1] ** (-0.5)
    scores = (
        jnp.einsum("qhd,khd->hqk", queries, key_block, preferred_element_type=jnp.float32)
        * head_scale
    )
    scores = jnp.where(key_valid[None, None, :], scores, -1e30)
    probs = jnp.exp(scores - log_total[..., None])
    grad_probs = jnp.einsum(
        "qhd,khd->hqk", grad_context, value_block, preferred_element_type=jnp.float32
    )
    row_inner = jnp.sum(probs * grad_probs, axis=-1, keepdims=True)
    grad_scores = (probs * (grad_probs - row_inner)).astype(jnp.bfloat16)
    probs_low = probs.astype(jnp.bfloat16)
    grad_queries = (
        jnp.einsum("hqk,khd->qhd", grad_scores, key_block, preferred_element_type=jnp.float32)
        * head_scale
    )
    grad_keys = (
        jnp.einsum("hqk,qhd->khd", grad_scores, queries, preferred_element_type=jnp.float32)
        * head_scale
    )
    grad_values = jnp.einsum(
        "hqk,qhd->khd", probs_low, grad_context, preferred_element_type=jnp.float32
    )
    return jnp.stack([grad_queries, grad_keys, grad_values], axis=1).astype(jnp.bfloat16)


DOWN, UP, QKV = 0, 1, 2
CHUNKS = tuple((m, k) for k in (1, 2, 3, 0) for m in (DOWN, UP)) + tuple((QKV, k) for k in (1, 2, 3, 0))
X_FIRST = {(UP, 0), (UP, 1), (UP, 2), (UP, 3), (QKV, 2), (QKV, 0)}


def place():
    row, lane = lax.axis_index("dp"), lax.axis_index("seq")
    return row // 2, row % 2, lane // 2, lane % 2


def device(z, y, x, core):
    return (z * 2 + y, x * 2 + core)


def remote(source, target, send, receive, where):
    return pltpu.make_async_remote_copy(
        src_ref=source,
        dst_ref=target,
        send_sem=send,
        recv_sem=receive,
        device_id=where,
        device_id_type=MESH_ID,
    )


def grad_kernel(
    hid_ref, dpre_ref, act_ref, dffn_ref, tok_ref, dqkv_ref, ctx_ref, dbr_ref, vec_ref,
    down_out, up_out, qkv_out, vec_out,
    act, dpre, dffn_t, hid_t, tok_t, ctx_t, dqkv, dbr,
    sums_0, sums_1, sums_2, in1_0, in1_1, in1_2, in2_0, in2_1, in2_2, in3_0, in3_1, in3_2,
    vec_mine, vec_in,
    core_send, core_recv, send1, recv1, send2, recv2, send3, recv3, vec_send, vec_recv,
):
    z, y, x, core = place()
    sums, in1, in2, in3 = (sums_0, sums_1, sums_2), (in1_0, in1_1, in1_2), (in2_0, in2_1, in2_2), (in3_0, in3_1, in3_2)
    at_core = device(z, y, x, 1 - core)
    at_x = device(z, y, 1 - x, core)
    at_y = device(z, 1 - y, x, core)
    at_z = [device((z + k) % 4, y, x, core) for k in (1, 2, 3)]
    barrier = pltpu.get_barrier_semaphore()
    for where in [at_core, at_x, at_y] + at_z:
        pl.semaphore_signal(barrier, inc=1, device_id=where, device_id_type=MESH_ID)
    pl.semaphore_wait(barrier, 6)

    R = 256
    core_copies = []

    def to_core(source, target):
        n = len(core_copies)
        copy = remote(source, target, core_send.at[n], core_recv.at[n], at_core)
        copy.start()
        core_copies.append(copy)
        return copy

    act_copies = []
    for t in range(4):
        act[t, 0:R, :] = act_ref[:, 768 * t : 768 * (t + 1)]
        act_copies.append(to_core(act.at[t, pl.ds(0, R)], act.at[t, pl.ds(R, R)]))
    dffn_all = dffn_ref[...].T
    for j in range(4):
        dffn_t[j, :, 0:R] = dffn_all[192 * j : 192 * (j + 1), :]
    for j in (0, 2):
        there = j + 1 - core
        act_copies.append(to_core(dffn_t.at[there, :, pl.ds(0, R)], dffn_t.at[there, :, pl.ds(R, R)]))
    hid_t[:, 0:R] = hid_ref[...].T
    up_copies = [to_core(hid_t.at[:, pl.ds(0, R)], hid_t.at[:, pl.ds(R, R)])]
    for t in range(4):
        dpre[t, 0:R, :] = dpre_ref[:, 768 * t : 768 * (t + 1)]
    for j in (0, 2):
        there = j + 1 - core
        up_copies.append(to_core(dpre.at[there, pl.ds(0, R)], dpre.at[there, pl.ds(R, R)]))
    tok_t[:, 0:R] = tok_ref[...].T
    ctx_t[:, 0:R] = ctx_ref[...].T
    qkv_copies = [
        to_core(tok_t.at[:, pl.ds(0, R)], tok_t.at[:, pl.ds(R, R)]),
        to_core(ctx_t.at[:, pl.ds(0, R)], ctx_t.at[:, pl.ds(R, R)]),
    ]
    for j in range(4):
        dqkv[j, 0:R, :] = jnp.concatenate(
            [dqkv_ref[:, 576 * j : 576 * (j + 1)], jnp.zeros((R, 64), BF16)], axis=1
        )
        dbr[j, 0:R, :] = jnp.concatenate(
            [jnp.zeros((R, 64), BF16), dbr_ref[:, 192 * j : 192 * (j + 1)]], axis=1
        )
    for j in (0, 2):
        there = j + 1 - core
        qkv_copies.append(to_core(dqkv.at[there, pl.ds(0, R)], dqkv.at[there, pl.ds(R, R)]))
        qkv_copies.append(to_core(dbr.at[there, pl.ds(0, R)], dbr.at[there, pl.ds(R, R)]))

    def first(m, k):
        zk = (z + k) % 4
        if (m, k) in X_FIRST:
            return remote(sums[m].at[1 - x, zk], in1[m].at[zk], send1.at[m, k], recv1.at[m, k], at_x)
        return remote(sums[m].at[:, zk, 1 - y], in1[m].at[zk], send1.at[m, k], recv1.at[m, k], at_y)

    def second(m, k):
        zk = (z + k) % 4
        if (m, k) in X_FIRST:
            return remote(sums[m].at[x, zk, 1 - y], in2[m].at[zk], send2.at[m, k], recv2.at[m, k], at_y)
        return remote(sums[m].at[1 - x, zk, y], in2[m].at[zk], send2.at[m, k], recv2.at[m, k], at_x)

    def third(m, k):
        zk = (z + k) % 4
        return remote(sums[m].at[x, zk, y], in3[m].at[k - 1], send3.at[m, k], recv3.at[m, k], at_z[k - 1])

    def add_first(m, k):
        zk = (z + k) % 4
        if (m, k) in X_FIRST:
            sums[m][x, zk] = sums[m][x, zk] + in1[m][zk]
        else:
            for b in range(2):
                sums[m][b, zk, y] = sums[m][b, zk, y] + in1[m][zk, b]

    def add_second(m, k):
        zk = (z + k) % 4
        sums[m][x, zk, y] = sums[m][x, zk, y] + in2[m][zk]

    vec_mine[0] = vec_ref[...]
    vec_steps = [remote(vec_mine.at[s], vec_in.at[s], vec_send.at[s], vec_recv.at[s], w) for s, w in enumerate((at_core, at_x, at_y))]
    vec_steps[0].start()

    for copy in act_copies:
        copy.wait_recv()
    left = jnp.concatenate([dffn_t[core], dffn_t[2 + core]], axis=0)
    for t in range(4):
        part = jnp.dot(left, act[t], preferred_element_type=F32).astype(BF16)
        for b in range(2):
            for h in range(2):
                sums_0[b, t, h] = part[192 * b : 192 * (b + 1), 384 * h : 384 * (h + 1)]
    for k in (1, 2, 3, 0):
        first(DOWN, k).start()
    for copy in up_copies:
        copy.wait_recv()
    for b in range(2):
        for n in range(3):
            part = jnp.dot(hid_t[...], dpre[2 * b + core, :, 256 * n : 256 * (n + 1)], preferred_element_type=F32).astype(BF16)
            sums_1[b, :, :, :, 256 * n : 256 * (n + 1)] = part.reshape(4, 2, 96, 256)
    for k in (1, 2, 3, 0):
        first(UP, k).start()
    vec_steps[0].wait_recv()
    vec_mine[1] = vec_mine[0] + vec_in[0]
    vec_steps[1].start()
    for copy in qkv_copies:
        copy.wait_recv()
    for b in range(2):
        one = jnp.dot(tok_t[...], dqkv[2 * b + core], preferred_element_type=F32)
        two = jnp.dot(ctx_t[...], dbr[2 * b + core], preferred_element_type=F32)
        part = jnp.concatenate([one[:, 0:512], one[:, 512:640] + two[:, 0:128], two[:, 128:256]], axis=1).astype(BF16)
        sums_2[b] = part.reshape(4, 2, 96, 768)
    for k in (1, 2, 3, 0):
        first(QKV, k).start()
    vec_steps[1].wait_recv()
    vec_mine[2] = vec_mine[1] + vec_in[1]
    vec_steps[2].start()

    vec_z = [
        remote(vec_mine.at[3], vec_in.at[3 + z], vec_send.at[2 + k], vec_recv.at[2 + k], at_z[k - 1])
        for k in (1, 2, 3)
    ]
    lag = 2
    for step in range(len(CHUNKS) + lag):
        if step < len(CHUNKS):
            m, k = CHUNKS[step]
            first(m, k).wait_recv()
            add_first(m, k)
            second(m, k).start()
        if step >= lag:
            m, k = CHUNKS[step - lag]
            second(m, k).wait_recv()
            add_second(m, k)
            if k:
                third(m, k).start()
        if step == 2:
            vec_steps[2].wait_recv()
            vec_mine[3] = vec_mine[2] + vec_in[2]
            for copy in vec_z:
                copy.start()
    for copy in vec_z:
        copy.wait_recv()
    vec_in[3 + z] = vec_mine[3]
    vec_out[...] = (vec_in[3] + vec_in[4]) + (vec_in[5] + vec_in[6])
    for m, out in ((DOWN, down_out), (UP, up_out), (QKV, qkv_out)):
        for k in (1, 2, 3):
            third(m, k).wait_recv()
        total = sums[m][x, z, y].astype(F32)
        for k in range(3):
            total = total + in3[m][k].astype(F32)
        out[...] = total
    for copy in core_copies + vec_steps + vec_z:
        copy.wait_send()
    for m, k in CHUNKS:
        first(m, k).wait_send()
        second(m, k).wait_send()
        if k:
            third(m, k).wait_send()


def reduce_grads(hidden_low, d_pre, active, d_ffn, tokens, d_qkv, context, d_branch, vectors):
    V = pl.BlockSpec(memory_space=pltpu.VMEM)
    blocks = {DOWN: (192, 384), UP: (96, 768), QKV: (96, 768)}
    dma = pltpu.SemaphoreType.DMA
    return pl.pallas_call(
        grad_kernel,
        name="grads",
        out_shape=(
            jax.ShapeDtypeStruct((192, 384), F32),
            jax.ShapeDtypeStruct((96, 768), F32),
            jax.ShapeDtypeStruct((96, 768), F32),
            jax.ShapeDtypeStruct((16, 768), F32),
        ),
        in_specs=[V] * 9,
        out_specs=(V,) * 4,
        scratch_shapes=[
            pltpu.VMEM((4, 512, 768), BF16),
            pltpu.VMEM((4, 512, 768), BF16),
            pltpu.VMEM((4, 192, 512), BF16),
            pltpu.VMEM((768, 512), BF16),
            pltpu.VMEM((768, 512), BF16),
            pltpu.VMEM((768, 512), BF16),
            pltpu.VMEM((4, 512, 640), BF16),
            pltpu.VMEM((4, 512, 256), BF16),
        ]
        + [pltpu.VMEM((2, 4, 2) + blocks[m], BF16) for m in range(3)]
        + [pltpu.VMEM((4, 2) + blocks[m], BF16) for m in range(3)]
        + [pltpu.VMEM((4,) + blocks[m], BF16) for m in range(3)]
        + [pltpu.VMEM((3,) + blocks[m], BF16) for m in range(3)]
        + [pltpu.VMEM((4, 16, 768), F32), pltpu.VMEM((7, 16, 768), F32)]
        + [dma((16,)), dma((16,))]
        + [dma((3, 4))] * 6
        + [dma((6,)), dma((6,))],
        compiler_params=pltpu.CompilerParams(
            collective_id=1, has_side_effects=True, vmem_limit_bytes=60 * 1024 * 1024
        ),
    )(hidden_low, d_pre, active, d_ffn, tokens, d_qkv, context, d_branch, vectors)


def local_any(
    tokens,
    lengths,
    cotangent,
    w_qkv,
    b_query,
    b_value,
    w_out,
    b_out,
    first_gain,
    first_shift,
    w_up,
    b_up,
    w_down,
    b_down,
    second_gain,
    second_shift,
):
    lane_count = lax.axis_size("seq")
    seq_count, part_len, model_width = tokens.shape
    full_len = part_len * lane_count
    lane_width = model_width // lane_count
    head_size = HEAD_DIM
    heads_here = lane_width // head_size
    row_count = seq_count * part_len
    offset = lax.axis_index("seq") * part_len
    places = offset + jnp.arange(part_len, dtype=jnp.int32)
    length_row = lengths[0]
    row_live = (places[None, :] < length_row[:, None]).astype(jnp.float32).reshape(row_count, 1)
    key_valid = jnp.arange(full_len, dtype=jnp.int32)[None, :] < length_row[:, None]
    joined_bias = jnp.concatenate([b_query, jnp.zeros_like(b_query), b_value])
    tokens_flat = tokens.reshape(row_count, model_width)
    mixed = jnp.dot(tokens_flat, w_qkv, preferred_element_type=jnp.float32) + joined_bias
    qkv_heads = lax.all_to_all(
        mixed.astype(jnp.bfloat16).reshape(seq_count, part_len, 3, lane_count, lane_width),
        "seq",
        split_axis=3,
        concat_axis=1,
        tiled=True,
    )
    qkv_heads = qkv_heads.reshape(seq_count, full_len, 3, heads_here, head_size)
    context_heads, log_total = lax.map(
        attention_forward_pass,
        (qkv_heads[:, :, 0], qkv_heads[:, :, 1], qkv_heads[:, :, 2], key_valid),
    )
    context_heads = context_heads.reshape(seq_count, full_len, 1, lane_width)
    context_token_rows = lax.all_to_all(
        context_heads, "seq", split_axis=1, concat_axis=2, tiled=True
    ).reshape(row_count, model_width)
    branch = jnp.dot(context_token_rows, w_out, preferred_element_type=jnp.float32) + b_out
    normed_one, inverse_one = normalize(tokens_flat.astype(jnp.float32) + branch)
    hidden = normed_one * first_gain + first_shift
    hidden_low = hidden.astype(jnp.bfloat16)
    preactivation_input = jnp.dot(hidden_low, w_up, preferred_element_type=jnp.float32) + b_up
    active = jax.nn.gelu(preactivation_input, approximate=False).astype(jnp.bfloat16)
    ffn_out = jnp.dot(active, w_down, preferred_element_type=jnp.float32) + b_down
    normed_two, inverse_two = normalize(hidden + ffn_out)
    output_rows = (normed_two * second_gain + second_shift) * row_live
    output_tokens = output_rows.astype(jnp.bfloat16).reshape(seq_count, part_len, model_width)
    grad_out = cotangent.reshape(row_count, model_width).astype(jnp.float32) * row_live
    grad_second_gain = jnp.sum(grad_out * normed_two, axis=0)
    grad_second_shift = jnp.sum(grad_out, axis=0)
    d_sum_two = norm_backward(grad_out, normed_two, inverse_two, second_gain)
    d_ffn = d_sum_two.astype(jnp.bfloat16)
    grad_b_down = jnp.sum(d_ffn.astype(jnp.float32), axis=0)
    grad_w_down = contract_rows(active, d_ffn)
    d_active = times_transposed(d_ffn, w_down)
    gelu_slope = (
        0.5 * (1.0 + lax.erf(preactivation_input * ROOT_HALF))
        + preactivation_input
        * jnp.exp(-0.5 * preactivation_input * preactivation_input)
        * INV_ROOT_TWO_PI
    )
    d_pre = (d_active * gelu_slope).astype(jnp.bfloat16)
    grad_b_up = jnp.sum(d_pre.astype(jnp.float32), axis=0)
    grad_w_up = contract_rows(hidden_low, d_pre)
    d_hidden = d_sum_two + times_transposed(d_pre, w_up)
    grad_first_gain = jnp.sum(d_hidden * normed_one, axis=0)
    grad_first_shift = jnp.sum(d_hidden, axis=0)
    d_sum_one = norm_backward(d_hidden, normed_one, inverse_one, first_gain)
    d_branch = d_sum_one.astype(jnp.bfloat16)
    grad_b_out = jnp.sum(d_branch.astype(jnp.float32), axis=0)
    grad_w_out = contract_rows(context_token_rows, d_branch)
    d_context = times_transposed(d_branch, w_out).astype(jnp.bfloat16)
    d_context = d_context.reshape(seq_count, part_len, lane_count, lane_width)
    d_context_heads = lax.all_to_all(d_context, "seq", split_axis=2, concat_axis=1, tiled=True)
    d_context_heads = d_context_heads.reshape(seq_count, full_len, heads_here, head_size)
    d_qkv_heads = lax.map(
        attend_backward,
        (
            qkv_heads[:, :, 0],
            qkv_heads[:, :, 1],
            qkv_heads[:, :, 2],
            key_valid,
            log_total,
            d_context_heads,
        ),
    )
    d_qkv_heads = d_qkv_heads.reshape(seq_count, full_len, 3, 1, lane_width)
    d_qkv = lax.all_to_all(d_qkv_heads, "seq", split_axis=1, concat_axis=3, tiled=True).reshape(
        row_count, 3 * model_width
    )
    d_qkv_wide = d_qkv.astype(jnp.float32)
    grad_b_query = jnp.sum(d_qkv_wide[:, :model_width], axis=0)
    grad_b_value = jnp.sum(d_qkv_wide[:, 2 * model_width :], axis=0)
    grad_w_qkv = contract_rows(tokens_flat, d_qkv)
    grad_rows = d_sum_one + times_transposed(d_qkv, w_qkv)
    grad_tokens = grad_rows.astype(jnp.bfloat16).reshape(seq_count, part_len, model_width)
    matrices = (grad_w_qkv, grad_w_out, grad_w_up, grad_w_down)
    halfway = (
        lax.psum_scatter(matrices[0], "dp", scatter_dimension=0, tiled=True),
        lax.psum_scatter(matrices[1], "dp", scatter_dimension=0, tiled=True),
        lax.psum_scatter(matrices[2], "dp", scatter_dimension=0, tiled=True),
        lax.psum_scatter(matrices[3], "dp", scatter_dimension=0, tiled=True),
    )
    matrices = (
        lax.psum_scatter(
            halfway[0].astype(jnp.bfloat16), "seq", scatter_dimension=1, tiled=True
        ).astype(jnp.float32),
        lax.psum_scatter(
            halfway[1].astype(jnp.bfloat16), "seq", scatter_dimension=1, tiled=True
        ).astype(jnp.float32),
        lax.psum_scatter(
            halfway[2].astype(jnp.bfloat16), "seq", scatter_dimension=1, tiled=True
        ).astype(jnp.float32),
        lax.psum_scatter(
            halfway[3].astype(jnp.bfloat16), "seq", scatter_dimension=1, tiled=True
        ).astype(jnp.float32),
    )
    vectors = lax.psum(
        (
            grad_b_query,
            grad_b_value,
            grad_b_out,
            grad_first_gain,
            grad_first_shift,
            grad_b_up,
            grad_b_down,
            grad_second_gain,
            grad_second_shift,
        ),
        ("dp", "seq"),
    )
    return (
        output_tokens,
        grad_tokens,
        matrices[0],
        matrices[1],
        matrices[2],
        matrices[3],
        vectors[0],
        vectors[1],
        vectors[2],
        vectors[3],
        vectors[4],
        vectors[5],
        vectors[6],
        vectors[7],
        vectors[8],
    )


def local(
    tokens,
    lengths,
    cotangent,
    w_qkv,
    b_query,
    b_value,
    w_out,
    b_out,
    first_gain,
    first_shift,
    w_up,
    b_up,
    w_down,
    b_down,
    second_gain,
    second_shift,
):
    lane_count = lax.axis_size("seq")
    seq_count, part_len, model_width = tokens.shape
    full_len = part_len * lane_count
    lane_width = model_width // lane_count
    head_size = HEAD_DIM
    heads_here = lane_width // head_size
    row_count = seq_count * part_len
    offset = lax.axis_index("seq") * part_len
    places = offset + jnp.arange(part_len, dtype=jnp.int32)
    length_row = lengths[0]
    row_live = (places[None, :] < length_row[:, None]).astype(jnp.float32).reshape(row_count, 1)
    key_valid = jnp.arange(full_len, dtype=jnp.int32)[None, :] < length_row[:, None]
    joined_bias = jnp.concatenate([b_query, jnp.zeros_like(b_query), b_value])
    tokens_flat = tokens.reshape(row_count, model_width)
    mixed = jnp.dot(tokens_flat, w_qkv, preferred_element_type=jnp.float32) + joined_bias
    qkv_heads = lax.all_to_all(
        mixed.astype(jnp.bfloat16).reshape(seq_count, part_len, 3, lane_count, lane_width),
        "seq",
        split_axis=3,
        concat_axis=1,
        tiled=True,
    )
    qkv_heads = qkv_heads.reshape(seq_count, full_len, 3, heads_here, head_size)
    context_heads, log_total = lax.map(
        attention_forward_pass,
        (qkv_heads[:, :, 0], qkv_heads[:, :, 1], qkv_heads[:, :, 2], key_valid),
    )
    context_heads = context_heads.reshape(seq_count, full_len, 1, lane_width)
    context_token_rows = lax.all_to_all(
        context_heads, "seq", split_axis=1, concat_axis=2, tiled=True
    ).reshape(row_count, model_width)
    branch = jnp.dot(context_token_rows, w_out, preferred_element_type=jnp.float32) + b_out
    normed_one, inverse_one = normalize(tokens_flat.astype(jnp.float32) + branch)
    hidden = normed_one * first_gain + first_shift
    hidden_low = hidden.astype(jnp.bfloat16)
    preactivation_input = jnp.dot(hidden_low, w_up, preferred_element_type=jnp.float32) + b_up
    active = jax.nn.gelu(preactivation_input, approximate=False).astype(jnp.bfloat16)
    ffn_out = jnp.dot(active, w_down, preferred_element_type=jnp.float32) + b_down
    normed_two, inverse_two = normalize(hidden + ffn_out)
    output_rows = (normed_two * second_gain + second_shift) * row_live
    output_tokens = output_rows.astype(jnp.bfloat16).reshape(seq_count, part_len, model_width)
    grad_out = cotangent.reshape(row_count, model_width).astype(jnp.float32) * row_live
    grad_second_gain = jnp.sum(grad_out * normed_two, axis=0)
    grad_second_shift = jnp.sum(grad_out, axis=0)
    d_sum_two = norm_backward(grad_out, normed_two, inverse_two, second_gain)
    d_ffn = d_sum_two.astype(jnp.bfloat16)
    grad_b_down = jnp.sum(d_ffn.astype(jnp.float32), axis=0)
    d_active = times_transposed(d_ffn, w_down)
    gelu_slope = (
        0.5 * (1.0 + lax.erf(preactivation_input * ROOT_HALF))
        + preactivation_input
        * jnp.exp(-0.5 * preactivation_input * preactivation_input)
        * INV_ROOT_TWO_PI
    )
    d_pre = (d_active * gelu_slope).astype(jnp.bfloat16)
    grad_b_up = jnp.sum(d_pre.astype(jnp.float32), axis=0)
    d_hidden = d_sum_two + times_transposed(d_pre, w_up)
    grad_first_gain = jnp.sum(d_hidden * normed_one, axis=0)
    grad_first_shift = jnp.sum(d_hidden, axis=0)
    d_sum_one = norm_backward(d_hidden, normed_one, inverse_one, first_gain)
    d_branch = d_sum_one.astype(jnp.bfloat16)
    grad_b_out = jnp.sum(d_branch.astype(jnp.float32), axis=0)
    d_context = times_transposed(d_branch, w_out).astype(jnp.bfloat16)
    d_context = d_context.reshape(seq_count, part_len, lane_count, lane_width)
    d_context_heads = lax.all_to_all(d_context, "seq", split_axis=2, concat_axis=1, tiled=True)
    d_context_heads = d_context_heads.reshape(seq_count, full_len, heads_here, head_size)
    d_qkv_heads = lax.map(
        attend_backward,
        (
            qkv_heads[:, :, 0],
            qkv_heads[:, :, 1],
            qkv_heads[:, :, 2],
            key_valid,
            log_total,
            d_context_heads,
        ),
    )
    d_qkv_heads = d_qkv_heads.reshape(seq_count, full_len, 3, 1, lane_width)
    d_qkv = lax.all_to_all(d_qkv_heads, "seq", split_axis=1, concat_axis=3, tiled=True).reshape(
        row_count, 3 * model_width
    )
    d_qkv_wide = d_qkv.astype(jnp.float32)
    grad_b_query = jnp.sum(d_qkv_wide[:, :model_width], axis=0)
    grad_b_value = jnp.sum(d_qkv_wide[:, 2 * model_width :], axis=0)
    grad_rows = d_sum_one + times_transposed(d_qkv, w_qkv)
    grad_tokens = grad_rows.astype(jnp.bfloat16).reshape(seq_count, part_len, model_width)
    vectors = jnp.concatenate(
        [
            grad_b_query,
            grad_b_value,
            grad_b_out,
            grad_first_gain,
            grad_first_shift,
            grad_b_down,
            grad_second_gain,
            grad_second_shift,
            grad_b_up,
            jnp.zeros((4 * model_width,), jnp.float32),
        ]
    ).reshape(16, model_width)
    down, up, joined, vectors = reduce_grads(
        hidden_low, d_pre, active, d_ffn, tokens_flat, d_qkv, context_token_rows, d_branch, vectors
    )
    return (
        output_tokens,
        grad_tokens,
        joined[:, :576],
        joined[:, 576:],
        up,
        down.T,
        vectors[0],
        vectors[1],
        vectors[2],
        vectors[3],
        vectors[4],
        vectors[8:12].reshape(-1),
        vectors[5],
        vectors[6],
        vectors[7],
    )


def solution(mesh):
    in_specs = (
        P("dp", "seq", None),
        P("dp", None),
        P("dp", "seq", None),
        P(),
        P(),
        P(),
        P(),
        P(),
        P(),
        P(),
        P(),
        P(),
        P(),
        P(),
        P(),
        P(),
    )
    out_specs = (
        P("dp", "seq", None),
        P("dp", "seq", None),
        P("dp", "seq"),
        P("dp", "seq"),
        P("dp", "seq"),
        P("dp", "seq"),
        P(),
        P(),
        P(),
        P(),
        P(),
        P(),
        P(),
        P(),
        P(),
    )
    return jax.shard_map(
        local if dict(mesh.shape) == {"dp": 8, "seq": 4} else local_any, mesh=mesh, in_specs=in_specs, out_specs=out_specs, check_vma=False)
```

```python
import functools

import jax
import jax.numpy as jnp
from jax import lax
from jax.experimental import pallas as pl
from jax.experimental.pallas import tpu as pltpu
from jax.sharding import PartitionSpec as P

MESH_ID = pl.DeviceIdType.MESH
BF16 = jnp.bfloat16
F32 = jnp.float32

HEAD_DIM = 64


EPSILON = 1e-05
ROOT_HALF = 0.7071067811865476
INV_ROOT_TWO_PI = 0.3989422804014327


def contract_rows(left, right):
    return lax.dot_general(
        left, right, (((0,), (0,)), ((), ())), preferred_element_type=jnp.float32
    )


def times_transposed(left, weight_matrix):
    return lax.dot_general(
        left, weight_matrix, (((1,), (1,)), ((), ())), preferred_element_type=jnp.float32
    )


def normalize(value_rows):
    center = value_rows - jnp.mean(value_rows, axis=-1, keepdims=True)
    inverse_root = lax.rsqrt(jnp.mean(center * center, axis=-1, keepdims=True) + EPSILON)
    return (center * inverse_root, inverse_root)


def norm_backward(grad_out, normed, inverse_root, gain):
    scaled = grad_out * gain
    return inverse_root * (
        scaled
        - jnp.mean(scaled, axis=-1, keepdims=True)
        - normed * jnp.mean(scaled * normed, axis=-1, keepdims=True)
    )


def attention_forward_pass(inputs):
    queries, key_block, value_block, key_valid = inputs
    head_scale = queries.shape[-1] ** (-0.5)
    scores = (
        jnp.einsum("qhd,khd->hqk", queries, key_block, preferred_element_type=jnp.float32)
        * head_scale
    )
    scores = jnp.where(key_valid[None, None, :], scores, -1e30)
    highest = jnp.max(scores, axis=-1, keepdims=True)
    exponent = jnp.exp(scores - highest)
    row_total = jnp.sum(exponent, axis=-1, keepdims=True)
    weight_tensors = (exponent / row_total).astype(jnp.bfloat16)
    context = jnp.einsum(
        "hqk,khd->qhd", weight_tensors, value_block, preferred_element_type=jnp.float32
    )
    return (context.astype(jnp.bfloat16), (highest + jnp.log(row_total))[..., 0])


def attend_backward(inputs):
    queries, key_block, value_block, key_valid, log_total, grad_context = inputs
    head_scale = queries.shape[-1] ** (-0.5)
    scores = (
        jnp.einsum("qhd,khd->hqk", queries, key_block, preferred_element_type=jnp.float32)
        * head_scale
    )
    scores = jnp.where(key_valid[None, None, :], scores, -1e30)
    probs = jnp.exp(scores - log_total[..., None])
    grad_probs = jnp.einsum(
        "qhd,khd->hqk", grad_context, value_block, preferred_element_type=jnp.float32
    )
    row_inner = jnp.sum(probs * grad_probs, axis=-1, keepdims=True)
    grad_scores = (probs * (grad_probs - row_inner)).astype(jnp.bfloat16)
    probs_low = probs.astype(jnp.bfloat16)
    grad_queries = (
        jnp.einsum("hqk,khd->qhd", grad_scores, key_block, preferred_element_type=jnp.float32)
        * head_scale
    )
    grad_keys = (
        jnp.einsum("hqk,qhd->khd", grad_scores, queries, preferred_element_type=jnp.float32)
        * head_scale
    )
    grad_values = jnp.einsum(
        "hqk,qhd->khd", probs_low, grad_context, preferred_element_type=jnp.float32
    )
    return jnp.stack([grad_queries, grad_keys, grad_values], axis=1).astype(jnp.bfloat16)


def local_any(
    tokens,
    lengths,
    cotangent,
    w_qkv,
    b_query,
    b_value,
    w_out,
    b_out,
    first_gain,
    first_shift,
    w_up,
    b_up,
    w_down,
    b_down,
    second_gain,
    second_shift,
):
    lane_count = lax.axis_size("seq")
    seq_count, part_len, model_width = tokens.shape
    full_len = part_len * lane_count
    lane_width = model_width // lane_count
    head_size = HEAD_DIM
    heads_here = lane_width // head_size
    row_count = seq_count * part_len
    offset = lax.axis_index("seq") * part_len
    places = offset + jnp.arange(part_len, dtype=jnp.int32)
    length_row = lengths[0]
    row_live = (places[None, :] < length_row[:, None]).astype(jnp.float32).reshape(row_count, 1)
    key_valid = jnp.arange(full_len, dtype=jnp.int32)[None, :] < length_row[:, None]
    joined_bias = jnp.concatenate([b_query, jnp.zeros_like(b_query), b_value])
    tokens_flat = tokens.reshape(row_count, model_width)
    mixed = jnp.dot(tokens_flat, w_qkv, preferred_element_type=jnp.float32) + joined_bias
    qkv_heads = lax.all_to_all(
        mixed.astype(jnp.bfloat16).reshape(seq_count, part_len, 3, lane_count, lane_width),
        "seq",
        split_axis=3,
        concat_axis=1,
        tiled=True,
    )
    qkv_heads = qkv_heads.reshape(seq_count, full_len, 3, heads_here, head_size)
    context_heads, log_total = lax.map(
        attention_forward_pass,
        (qkv_heads[:, :, 0], qkv_heads[:, :, 1], qkv_heads[:, :, 2], key_valid),
    )
    context_heads = context_heads.reshape(seq_count, full_len, 1, lane_width)
    context_token_rows = lax.all_to_all(
        context_heads, "seq", split_axis=1, concat_axis=2, tiled=True
    ).reshape(row_count, model_width)
    branch = jnp.dot(context_token_rows, w_out, preferred_element_type=jnp.float32) + b_out
    normed_one, inverse_one = normalize(tokens_flat.astype(jnp.float32) + branch)
    hidden = normed_one * first_gain + first_shift
    hidden_low = hidden.astype(jnp.bfloat16)
    preactivation_input = jnp.dot(hidden_low, w_up, preferred_element_type=jnp.float32) + b_up
    active = jax.nn.gelu(preactivation_input, approximate=False).astype(jnp.bfloat16)
    ffn_out = jnp.dot(active, w_down, preferred_element_type=jnp.float32) + b_down
    normed_two, inverse_two = normalize(hidden + ffn_out)
    output_rows = (normed_two * second_gain + second_shift) * row_live
    output_tokens = output_rows.astype(jnp.bfloat16).reshape(seq_count, part_len, model_width)
    grad_out = cotangent.reshape(row_count, model_width).astype(jnp.float32) * row_live
    grad_second_gain = jnp.sum(grad_out * normed_two, axis=0)
    grad_second_shift = jnp.sum(grad_out, axis=0)
    d_sum_two = norm_backward(grad_out, normed_two, inverse_two, second_gain)
    d_ffn = d_sum_two.astype(jnp.bfloat16)
    grad_b_down = jnp.sum(d_ffn.astype(jnp.float32), axis=0)
    grad_w_down = contract_rows(active, d_ffn)
    d_active = times_transposed(d_ffn, w_down)
    gelu_slope = (
        0.5 * (1.0 + lax.erf(preactivation_input * ROOT_HALF))
        + preactivation_input
        * jnp.exp(-0.5 * preactivation_input * preactivation_input)
        * INV_ROOT_TWO_PI
    )
    d_pre = (d_active * gelu_slope).astype(jnp.bfloat16)
    grad_b_up = jnp.sum(d_pre.astype(jnp.float32), axis=0)
    grad_w_up = contract_rows(hidden_low, d_pre)
    d_hidden = d_sum_two + times_transposed(d_pre, w_up)
    grad_first_gain = jnp.sum(d_hidden * normed_one, axis=0)
    grad_first_shift = jnp.sum(d_hidden, axis=0)
    d_sum_one = norm_backward(d_hidden, normed_one, inverse_one, first_gain)
    d_branch = d_sum_one.astype(jnp.bfloat16)
    grad_b_out = jnp.sum(d_branch.astype(jnp.float32), axis=0)
    grad_w_out = contract_rows(context_token_rows, d_branch)
    d_context = times_transposed(d_branch, w_out).astype(jnp.bfloat16)
    d_context = d_context.reshape(seq_count, part_len, lane_count, lane_width)
    d_context_heads = lax.all_to_all(d_context, "seq", split_axis=2, concat_axis=1, tiled=True)
    d_context_heads = d_context_heads.reshape(seq_count, full_len, heads_here, head_size)
    d_qkv_heads = lax.map(
        attend_backward,
        (
            qkv_heads[:, :, 0],
            qkv_heads[:, :, 1],
            qkv_heads[:, :, 2],
            key_valid,
            log_total,
            d_context_heads,
        ),
    )
    d_qkv_heads = d_qkv_heads.reshape(seq_count, full_len, 3, 1, lane_width)
    d_qkv = lax.all_to_all(d_qkv_heads, "seq", split_axis=1, concat_axis=3, tiled=True).reshape(
        row_count, 3 * model_width
    )
    d_qkv_wide = d_qkv.astype(jnp.float32)
    grad_b_query = jnp.sum(d_qkv_wide[:, :model_width], axis=0)
    grad_b_value = jnp.sum(d_qkv_wide[:, 2 * model_width :], axis=0)
    grad_w_qkv = contract_rows(tokens_flat, d_qkv)
    grad_rows = d_sum_one + times_transposed(d_qkv, w_qkv)
    grad_tokens = grad_rows.astype(jnp.bfloat16).reshape(seq_count, part_len, model_width)
    matrices = (grad_w_qkv, grad_w_out, grad_w_up, grad_w_down)
    halfway = (
        lax.psum_scatter(matrices[0], "dp", scatter_dimension=0, tiled=True),
        lax.psum_scatter(matrices[1], "dp", scatter_dimension=0, tiled=True),
        lax.psum_scatter(matrices[2], "dp", scatter_dimension=0, tiled=True),
        lax.psum_scatter(matrices[3], "dp", scatter_dimension=0, tiled=True),
    )
    matrices = (
        lax.psum_scatter(
            halfway[0].astype(jnp.bfloat16), "seq", scatter_dimension=1, tiled=True
        ).astype(jnp.float32),
        lax.psum_scatter(
            halfway[1].astype(jnp.bfloat16), "seq", scatter_dimension=1, tiled=True
        ).astype(jnp.float32),
        lax.psum_scatter(
            halfway[2].astype(jnp.bfloat16), "seq", scatter_dimension=1, tiled=True
        ).astype(jnp.float32),
        lax.psum_scatter(
            halfway[3].astype(jnp.bfloat16), "seq", scatter_dimension=1, tiled=True
        ).astype(jnp.float32),
    )
    vectors = lax.psum(
        (
            grad_b_query,
            grad_b_value,
            grad_b_out,
            grad_first_gain,
            grad_first_shift,
            grad_b_up,
            grad_b_down,
            grad_second_gain,
            grad_second_shift,
        ),
        ("dp", "seq"),
    )
    return (
        output_tokens,
        grad_tokens,
        matrices[0],
        matrices[1],
        matrices[2],
        matrices[3],
        vectors[0],
        vectors[1],
        vectors[2],
        vectors[3],
        vectors[4],
        vectors[5],
        vectors[6],
        vectors[7],
        vectors[8],
    )


DOWN, UP, QKV = 0, 1, 2
ORDER = (1, 2, 3, 0)
CHUNKS = tuple((m, k) for k in ORDER for m in (DOWN, UP)) + tuple((QKV, k) for k in ORDER)
X_FIRST = {(UP, 0), (UP, 1), (UP, 2), (UP, 3), (QKV, 2), (QKV, 0)}
BLOCKS = ((192, 384), (96, 768), (96, 768))

B_QUERY, B_VALUE, B_OUT, FIRST_GAIN, FIRST_SHIFT, B_DOWN, SECOND_GAIN, SECOND_SHIFT, B_UP = range(9)

ROWS = 256
PART = 128
WIDTH = 768
STEP = 32


def place():
    row, lane = lax.axis_index("dp"), lax.axis_index("seq")
    return row // 2, row % 2, lane // 2, lane % 2


def device(z, y, x, core):
    return (z * 2 + y, x * 2 + core)


def remote(source, target, send, receive, where):
    return pltpu.make_async_remote_copy(
        src_ref=source,
        dst_ref=target,
        send_sem=send,
        recv_sem=receive,
        device_id=where,
        device_id_type=MESH_ID,
    )


def dot(left, right):
    return jnp.dot(left, right, preferred_element_type=F32)


def dot_t(left, right):
    return lax.dot_general(left, right, (((1,), (1,)), ((), ())), preferred_element_type=F32)


def fold(rows):
    return jnp.sum(rows.reshape(rows.shape[0] // 8, 8, rows.shape[1]), axis=0)


def mean(rows):
    return jnp.sum(rows, axis=-1, keepdims=True) * (1.0 / WIDTH)


def layer_kernel(
    tokens_in, lengths_in, cot_in, w_qkv_in, w_out_in, w_up_in, w_down_in,
    b_query_in, b_value_in, b_out_in, first_gain_in, first_shift_in, b_up_in, b_down_in, second_gain_in, second_shift_in,
    tokens_out, grad_out, down_out, up_out, qkv_out, vec_out,
    w_qkv, w_out, w_up, w_down, par, tok, cot, q3, k3, v3, bias, probs, hidden, xhat, rstd, low, slope, wide, total,
    dsum, dctx3, dkv_own, dkv_send, dkv_in, dq_t, dqkv_flat, out_rows, grad_rows,
    act, dpre, dffn_t, hid_t, tok_t, ctx_t, dqkv, dbr,
    sums_0, sums_1, sums_2, in1_0, in1_1, in1_2, in2_0, in2_1, in2_2, in3_0, in3_1, in3_2,
    vec_mine, vec_in,
    load, ex_send, ex_recv, core_send, core_recv, act_send, act_recv,
    send1, recv1, send2, recv2, send3, recv3, vec_send, vec_recv,
):
    z, y, x, core = place()
    sums, in1, in2, in3 = (sums_0, sums_1, sums_2), (in1_0, in1_1, in1_2), (in2_0, in2_1, in2_2), (in3_0, in3_1, in3_2)
    at_core = device(z, y, x, 1 - core)
    at_x = device(z, y, 1 - x, core)
    at_y = device(z, 1 - y, x, core)
    at_z = [device((z + k) % 4, y, x, core) for k in (1, 2, 3)]

    loads = [pltpu.make_async_copy(tokens_in.at[x], tok.at[pl.ds(0, PART)], load.at[0])]
    for n, s in enumerate((1, 2, 0)):
        loads.append(
            pltpu.make_async_copy(
                w_qkv_in.at[:, pl.ds(WIDTH * s, WIDTH)], w_qkv.at[:, pl.ds(WIDTH * s, WIDTH)], load.at[1 + n]
            )
        )
    loads.append(pltpu.make_async_copy(cot_in.at[x], cot.at[pl.ds(0, PART)], load.at[4]))
    loads.append(pltpu.make_async_copy(w_out_in, w_out, load.at[5]))
    for t in range(4):
        loads.append(pltpu.make_async_copy(w_up_in.at[:, pl.ds(WIDTH * t, WIDTH)], w_up.at[t], load.at[6 + t]))
    for t in range(4):
        loads.append(pltpu.make_async_copy(w_down_in.at[pl.ds(WIDTH * t, WIDTH)], w_down.at[t], load.at[10 + t]))
    for copy in loads:
        copy.start()

    barrier = pltpu.get_barrier_semaphore()
    for where in [at_core, at_x, at_y] + at_z:
        pl.semaphore_signal(barrier, inc=1, device_id=where, device_id_type=MESH_ID)
    pl.semaphore_wait(barrier, 6)

    get_tok = remote(tokens_in.at[1 - x], tok.at[pl.ds(PART, PART)], ex_send.at[0], ex_recv.at[0], at_x)
    get_cot = remote(cot_in.at[1 - x], cot.at[pl.ds(PART, PART)], ex_send.at[1], ex_recv.at[1], at_x)
    get_tok.start()
    get_cot.start()

    core_copies = []

    def to_core(source, target):
        n = len(core_copies)
        copy = remote(source, target, core_send.at[n], core_recv.at[n], at_core)
        copy.start()
        core_copies.append(copy)
        return copy

    for row, ref in (
        (B_QUERY, b_query_in), (B_VALUE, b_value_in), (B_OUT, b_out_in), (FIRST_GAIN, first_gain_in), (FIRST_SHIFT, first_shift_in),
        (B_DOWN, b_down_in), (SECOND_GAIN, second_gain_in), (SECOND_SHIFT, second_shift_in),
    ):
        par[row : row + 1, :] = ref[...].reshape(1, WIDTH)
    for t in range(4):
        par[B_UP + t : B_UP + t + 1, :] = b_up_in[WIDTH * t : WIDTH * (t + 1)].reshape(1, WIDTH)
    vec_mine[0] = jnp.zeros((16, WIDTH), F32)
    length = lengths_in[0, x]
    mine, across = 2 * x + core, 2 * (1 - x) + core
    theirs, theirs_across = 2 * x + 1 - core, 2 * (1 - x) + 1 - core

    def positions(shape, starts):
        n = lax.broadcasted_iota(jnp.int32, shape, 0)
        first = starts[-1] * PART
        for b in range(len(starts) - 2, -1, -1):
            first = jnp.where(n < PART * (b + 1), starts[b] * PART, first)
        return first + n % PART

    bias[...] = jnp.where(positions((512, ROWS), (mine, across, theirs, theirs_across)) < length, 0.0, -1e30)

    kv_copies = []
    for b in range(2):
        rows = slice(PART * b, PART * (b + 1))
        if b == 0:
            loads[0].wait()
        else:
            get_tok.wait_recv()
        for n, s in enumerate((1, 2, 0)):
            if b == 0:
                loads[1 + n].wait()
            part = dot(tok[rows, :], w_qkv[:, WIDTH * s : WIDTH * (s + 1)])
            if s == 0:
                part = part + par[B_QUERY : B_QUERY + 1, :]
            if s == 2:
                part = part + par[B_VALUE : B_VALUE + 1, :]
            part = part.astype(BF16)
            if s == 0:
                part = part * jnp.asarray(0.125, BF16)
            held = (q3, k3, v3)[s]
            for j in range(6):
                held[j, rows, :] = part[:, 128 * j : 128 * (j + 1)]
            if s:
                kv_copies.append(
                    to_core(held.at[:, pl.ds(PART * b, PART)], held.at[:, pl.ds(ROWS + PART * b, PART)])
                )
    tok_t[:, 0:ROWS] = tok[...].T
    qkv_copies = [to_core(tok_t.at[:, pl.ds(0, ROWS)], tok_t.at[:, pl.ds(ROWS, ROWS)])]
    for copy in kv_copies:
        copy.wait_recv()

    low_half = lax.broadcasted_iota(jnp.int32, (ROWS, 128), 1) < 64

    def half_of(pair, h):
        zeros = jnp.zeros_like(pair)
        return jnp.where(low_half, pair, zeros) if h == 0 else jnp.where(low_half, zeros, pair)

    def attend(j, _):
        queries, keys = q3[j], k3[j]
        values_t = v3[j].T
        for h in range(2):
            scores = dot_t(keys, half_of(queries, h)) + bias[...]
            exponent = jnp.exp(scores - jnp.max(scores, axis=0, keepdims=True))
            weight = (exponent * (1.0 / jnp.sum(exponent, axis=0, keepdims=True))).astype(BF16)
            probs[2 * j + h] = weight
            ctx_t[pl.ds(pl.multiple_of(128 * j + 64 * h, 64), 64), 0:ROWS] = dot(values_t[64 * h : 64 * (h + 1)], weight).astype(BF16)
        return 0

    lax.fori_loop(0, 6, attend, 0)
    qkv_copies.append(to_core(ctx_t.at[:, pl.ds(0, ROWS)], ctx_t.at[:, pl.ds(ROWS, ROWS)]))

    loads[5].wait()
    wide[...] = dot(ctx_t[:, 0:ROWS].T, w_out[...])

    def first_norm(r, _):
        rows = pl.ds(pl.multiple_of(STEP * r, STEP), STEP)
        value = tok[rows, :].astype(F32) + wide[rows, :] + par[B_OUT : B_OUT + 1, :]
        center = value - mean(value)
        root = lax.rsqrt(mean(center * center) + EPSILON)
        normed = center * root
        out = normed * par[FIRST_GAIN : FIRST_GAIN + 1, :] + par[FIRST_SHIFT : FIRST_SHIFT + 1, :]
        xhat[rows, :] = normed
        rstd[rows, :] = root
        hidden[rows, :] = out
        low[rows, :] = out.astype(BF16)
        return 0

    lax.fori_loop(0, ROWS // STEP, first_norm, 0)
    hid_t[:, 0:ROWS] = low[...].T
    up_copies = [to_core(hid_t.at[:, pl.ds(0, ROWS)], hid_t.at[:, pl.ds(ROWS, ROWS)])]

    for n in range(6, 14):
        loads[n].wait()
    total[...] = jnp.zeros_like(total)

    def act_copy(t):
        return remote(act.at[t, pl.ds(0, ROWS)], act.at[t, pl.ds(ROWS, ROWS)], act_send.at[t], act_recv.at[t], at_core)

    def feed(t, _):
        wide[...] = dot(low[...], w_up[t])

        def gelu(r, _):
            rows = pl.ds(pl.multiple_of(STEP * r, STEP), STEP)
            u = wide[rows, :] + par[pl.ds(B_UP + t, 1), :]
            phi = 0.5 * (1.0 + lax.erf(u * ROOT_HALF))
            act[t, rows, :] = (u * phi).astype(BF16)
            slope[t, rows, :] = phi + u * jnp.exp(-0.5 * u * u) * INV_ROOT_TWO_PI
            return 0

        lax.fori_loop(0, ROWS // STEP, gelu, 0)
        act_copy(t).start()
        total[...] += dot(act[t, 0:ROWS, :], w_down[t])
        return 0

    lax.fori_loop(0, 4, feed, 0)

    loads[4].wait()
    get_cot.wait_recv()

    def second_norm(r, carry):
        rows = pl.ds(pl.multiple_of(STEP * r, STEP), STEP)
        value = hidden[rows, :] + (total[rows, :] + par[B_DOWN : B_DOWN + 1, :])
        center = value - mean(value)
        root = lax.rsqrt(mean(center * center) + EPSILON)
        normed = center * root
        n = lax.broadcasted_iota(jnp.int32, (STEP, 1), 0) + STEP * r
        live = jnp.where(jnp.where(n < PART, mine * PART + n, across * PART + n - PART) < length, 1.0, 0.0)
        out = (normed * par[SECOND_GAIN : SECOND_GAIN + 1, :] + par[SECOND_SHIFT : SECOND_SHIFT + 1, :]) * live
        out_rows[rows, :] = out.astype(BF16)
        grad = cot[rows, :].astype(F32) * live
        e = grad * par[SECOND_GAIN : SECOND_GAIN + 1, :]
        d = root * (e - mean(e) - normed * mean(e * normed))
        dsum[rows, :] = d
        d_low = d.astype(BF16)
        low[rows, :] = d_low
        gain, shift, down = carry
        return gain + fold(grad * normed), shift + fold(grad), down + fold(d_low.astype(F32))

    zero = jnp.zeros((8, WIDTH), F32)
    gain, shift, down = lax.fori_loop(0, ROWS // STEP, second_norm, (zero, zero, zero))

    def put(row, partial):
        vec_mine[0, row : row + 1, :] = jnp.sum(partial, axis=0, keepdims=True)

    put(SECOND_GAIN, gain)
    put(SECOND_SHIFT, shift)
    put(B_DOWN, down)
    out_local = pltpu.make_async_copy(out_rows.at[pl.ds(0, PART)], tokens_out.at[x], load.at[14])
    out_across = remote(out_rows.at[pl.ds(PART, PART)], tokens_out.at[x], ex_send.at[2], ex_recv.at[2], at_x)
    out_local.start()
    out_across.start()
    dffn_all = low[...].T
    for j in range(4):
        dffn_t[j, :, 0:ROWS] = dffn_all[192 * j : 192 * (j + 1), :]
    down_copies = []
    for j in (0, 2):
        there = j + 1 - core
        down_copies.append(to_core(dffn_t.at[there, :, pl.ds(0, ROWS)], dffn_t.at[there, :, pl.ds(ROWS, ROWS)]))

    def first(m, k):
        zk = (z + k) % 4
        if (m, k) in X_FIRST:
            return remote(sums[m].at[1 - x, zk], in1[m].at[zk], send1.at[m, k], recv1.at[m, k], at_x)
        return remote(sums[m].at[:, zk, 1 - y], in1[m].at[zk], send1.at[m, k], recv1.at[m, k], at_y)

    def second(m, k):
        zk = (z + k) % 4
        if (m, k) in X_FIRST:
            return remote(sums[m].at[x, zk, 1 - y], in2[m].at[zk], send2.at[m, k], recv2.at[m, k], at_y)
        return remote(sums[m].at[1 - x, zk, y], in2[m].at[zk], send2.at[m, k], recv2.at[m, k], at_x)

    def third(m, k):
        zk = (z + k) % 4
        return remote(sums[m].at[x, zk, y], in3[m].at[k - 1], send3.at[m, k], recv3.at[m, k], at_z[k - 1])

    def add_first(m, k):
        zk = (z + k) % 4
        if (m, k) in X_FIRST:
            sums[m][x, zk] = sums[m][x, zk] + in1[m][zk]
        else:
            for b in range(2):
                sums[m][b, zk, y] = sums[m][b, zk, y] + in1[m][zk, b]

    def add_second(m, k):
        zk = (z + k) % 4
        sums[m][x, zk, y] = sums[m][x, zk, y] + in2[m][zk]

    lag = 2
    done = [0]

    def advance(steps):
        for step in range(done[0], min(done[0] + steps, len(CHUNKS) + lag)):
            if step < len(CHUNKS):
                m, k = CHUNKS[step]
                first(m, k).wait_recv()
                add_first(m, k)
                second(m, k).start()
            if step >= lag:
                m, k = CHUNKS[step - lag]
                second(m, k).wait_recv()
                add_second(m, k)
                if k:
                    third(m, k).start()
        done[0] += steps

    total[...] = dsum[...]

    def feed_back(t, _):
        wide[...] = dot_t(low[...], w_down[t])

        def times_slope(r, carry):
            rows = pl.ds(pl.multiple_of(STEP * r, STEP), STEP)
            d = (wide[rows, :] * slope[t, rows, :]).astype(BF16)
            dpre[t, rows, :] = d
            return carry + fold(d.astype(F32))

        partial = lax.fori_loop(0, ROWS // STEP, times_slope, zero)
        vec_mine[0, pl.ds(B_UP + t, 1), :] = jnp.sum(partial, axis=0, keepdims=True)
        total[...] += dot_t(dpre[t, 0:ROWS, :], w_up[t])
        return 0

    lax.fori_loop(0, 4, feed_back, 0)
    for j in (0, 2):
        there = j + 1 - core
        up_copies.append(to_core(dpre.at[there, pl.ds(0, ROWS)], dpre.at[there, pl.ds(ROWS, ROWS)]))

    for t in range(4):
        act_copy(t).wait_recv()
    for copy in down_copies:
        copy.wait_recv()
    left = jnp.concatenate([dffn_t[core], dffn_t[2 + core]], axis=0)
    for t in range(4):
        part = dot(left, act[t]).astype(BF16)
        for b in range(2):
            for h in range(2):
                sums_0[b, t, h] = part[192 * b : 192 * (b + 1), 384 * h : 384 * (h + 1)]
    for k in ORDER:
        first(DOWN, k).start()
    for copy in up_copies:
        copy.wait_recv()
    for b in range(2):
        for n in range(3):
            part = dot(hid_t[...], dpre[2 * b + core, :, 256 * n : 256 * (n + 1)]).astype(BF16)
            sums_1[b, :, :, :, 256 * n : 256 * (n + 1)] = part.reshape(4, 2, 96, 256)
    for k in ORDER:
        first(UP, k).start()

    def first_norm_back(r, carry):
        rows = pl.ds(pl.multiple_of(STEP * r, STEP), STEP)
        d_hidden, normed = total[rows, :], xhat[rows, :]
        e = d_hidden * par[FIRST_GAIN : FIRST_GAIN + 1, :]
        d = rstd[rows, :] * (e - mean(e) - normed * mean(e * normed))
        dsum[rows, :] = d
        d_low = d.astype(BF16)
        low[rows, :] = d_low
        gain, shift, out = carry
        return gain + fold(d_hidden * normed), shift + fold(d_hidden), out + fold(d_low.astype(F32))

    gain, shift, out = lax.fori_loop(0, ROWS // STEP, first_norm_back, (zero, zero, zero))
    put(FIRST_GAIN, gain)
    put(FIRST_SHIFT, shift)
    put(B_OUT, out)
    for j in range(4):
        dbr[j, 0:ROWS, :] = jnp.concatenate([jnp.zeros((ROWS, 64), BF16), low[:, 192 * j : 192 * (j + 1)]], axis=1)
    for j in (0, 2):
        there = j + 1 - core
        qkv_copies.append(to_core(dbr.at[there, pl.ds(0, ROWS)], dbr.at[there, pl.ds(ROWS, ROWS)]))
    d_context = dot_t(low[...], w_out[...]).astype(BF16)
    for j in range(6):
        dctx3[j] = d_context[:, 128 * j : 128 * (j + 1)]

    def attend_back(j, _):
        queries, keys, values, d_ctx = q3[j], k3[j], v3[j], dctx3[j]
        keys_t = keys.T
        d_keys = jnp.zeros((512, 128), F32)
        d_values = jnp.zeros((512, 128), F32)
        for h in range(2):
            d_head = half_of(d_ctx, h)
            weight = probs[2 * j + h]
            d_probs = dot_t(values, d_head)
            d_values = d_values + dot(weight, d_head)
            wide_weight = weight.astype(F32)
            inner = jnp.sum(wide_weight * d_probs, axis=0, keepdims=True)
            d_scores = (wide_weight * (d_probs - inner)).astype(BF16)
            d_keys = d_keys + dot(d_scores, half_of(queries, h))
            dq_t[pl.ds(pl.multiple_of(128 * j + 64 * h, 64), 64), :] = (dot(keys_t[64 * h : 64 * (h + 1)], d_scores) * 0.125).astype(BF16)
        dkv_own[0, j] = d_keys[0:ROWS]
        dkv_own[1, j] = d_values[0:ROWS]
        dkv_send[0, j] = d_keys[ROWS:].astype(BF16)
        dkv_send[1, j] = d_values[ROWS:].astype(BF16)
        return 0

    lax.fori_loop(0, 3, attend_back, 0)
    back_copies = [to_core(dkv_send.at[:, pl.ds(0, 3)], dkv_in.at[:, pl.ds(0, 3)])]
    lax.fori_loop(3, 6, attend_back, 0)
    back_copies.append(to_core(dkv_send.at[:, pl.ds(3, 3)], dkv_in.at[:, pl.ds(3, 3)]))
    d_queries = dq_t[...].T
    dqkv_flat[:, 0:WIDTH] = d_queries
    put(B_QUERY, fold(d_queries.astype(F32)))
    for copy in back_copies:
        copy.wait_recv()
    for j in range(6):
        for s in range(2):
            d = (dkv_own[s, j] + dkv_in[s, j].astype(F32)).astype(BF16)
            dqkv_flat[:, WIDTH * (1 + s) + 128 * j : WIDTH * (1 + s) + 128 * (j + 1)] = d
            if s:
                vec_mine[0, B_VALUE : B_VALUE + 1, 128 * j : 128 * (j + 1)] = jnp.sum(d.astype(F32), axis=0, keepdims=True)
    for j in range(4):
        dqkv[j, 0:ROWS, :] = jnp.concatenate(
            [dqkv_flat[:, 576 * j : 576 * (j + 1)], jnp.zeros((ROWS, 64), BF16)], axis=1
        )
    for j in (0, 2):
        there = j + 1 - core
        qkv_copies.append(to_core(dqkv.at[there, pl.ds(0, ROWS)], dqkv.at[there, pl.ds(ROWS, ROWS)]))
    vec_steps = [
        remote(vec_mine.at[s], vec_in.at[s], vec_send.at[s], vec_recv.at[s], w) for s, w in enumerate((at_core, at_x, at_y))
    ]
    vec_steps[0].start()

    for copy in qkv_copies:
        copy.wait_recv()
    for b in range(2):
        one = dot(tok_t[...], dqkv[2 * b + core])
        two = dot(ctx_t[...], dbr[2 * b + core])
        part = jnp.concatenate([one[:, 0:512], one[:, 512:640] + two[:, 0:128], two[:, 128:256]], axis=1).astype(BF16)
        sums_2[b] = part.reshape(4, 2, 96, WIDTH)
    for k in ORDER:
        first(QKV, k).start()
    vec_steps[0].wait_recv()
    vec_mine[1] = vec_mine[0] + vec_in[0]
    vec_steps[1].start()
    grad_rows[...] = (dsum[...] + dot_t(dqkv_flat[...], w_qkv[...])).astype(BF16)
    grad_local = pltpu.make_async_copy(grad_rows.at[pl.ds(0, PART)], grad_out.at[x], load.at[15])
    grad_across = remote(grad_rows.at[pl.ds(PART, PART)], grad_out.at[x], ex_send.at[3], ex_recv.at[3], at_x)
    grad_local.start()
    grad_across.start()
    advance(2)
    vec_steps[1].wait_recv()
    vec_mine[2] = vec_mine[1] + vec_in[1]
    vec_steps[2].start()
    advance(2)
    vec_steps[2].wait_recv()
    vec_mine[3] = vec_mine[2] + vec_in[2]
    vec_z = [
        remote(vec_mine.at[3], vec_in.at[3 + z], vec_send.at[2 + k], vec_recv.at[2 + k], at_z[k - 1])
        for k in (1, 2, 3)
    ]
    for copy in vec_z:
        copy.start()
    vec_in[3 + z] = vec_mine[3]
    advance(len(CHUNKS))
    for copy in vec_z:
        copy.wait_recv()
    vec_out[...] = (vec_in[3] + vec_in[4]) + (vec_in[5] + vec_in[6])
    for m, out in ((DOWN, down_out), (UP, up_out), (QKV, qkv_out)):
        for k in (1, 2, 3):
            third(m, k).wait_recv()
        block = sums[m][x, z, y].astype(F32)
        for k in range(3):
            block = block + in3[m][k].astype(F32)
        out[...] = block

    out_across.wait_recv()
    grad_across.wait_recv()
    out_local.wait()
    grad_local.wait()
    for copy in [get_tok, get_cot, out_across, grad_across] + core_copies + vec_steps + vec_z:
        copy.wait_send()
    for t in range(4):
        act_copy(t).wait_send()
    for m, k in CHUNKS:
        first(m, k).wait_send()
        second(m, k).wait_send()
        if k:
            third(m, k).wait_send()


def local(
    tokens, lengths, cotangent, w_qkv, b_query, b_value, w_out, b_out, first_gain, first_shift, w_up, b_up, w_down, b_down,
    second_gain, second_shift,
):
    vmem = pl.BlockSpec(memory_space=pltpu.VMEM)
    hbm = pl.BlockSpec(memory_space=pl.ANY)
    dma = pltpu.SemaphoreType.DMA
    B, W = pltpu.VMEM, WIDTH
    scratch = [
        B((W, 3 * W), BF16), B((W, W), BF16), B((4, W, W), BF16), B((4, W, W), BF16), B((16, W), F32),
        B((ROWS, W), BF16), B((ROWS, W), BF16),
        B((6, ROWS, 128), BF16), B((6, 512, 128), BF16), B((6, 512, 128), BF16),
        B((512, ROWS), F32), B((12, 512, ROWS), BF16),
        B((ROWS, W), F32), B((ROWS, W), F32), B((ROWS, 1), F32), B((ROWS, W), BF16),
        B((4, ROWS, W), F32), B((ROWS, W), F32), B((ROWS, W), F32), B((ROWS, W), F32),
        B((6, ROWS, 128), BF16), B((2, 6, ROWS, 128), F32), B((2, 6, ROWS, 128), BF16), B((2, 6, ROWS, 128), BF16),
        B((W, ROWS), BF16), B((ROWS, 3 * W), BF16), B((ROWS, W), BF16), B((ROWS, W), BF16),
        B((4, 512, W), BF16), B((4, 512, W), BF16), B((4, 192, 512), BF16),
        B((W, 512), BF16), B((W, 512), BF16), B((W, 512), BF16), B((4, 512, 640), BF16), B((4, 512, 256), BF16),
    ]
    scratch += [B((2, 4, 2) + block, BF16) for block in BLOCKS]
    scratch += [B((4, 2) + block, BF16) for block in BLOCKS]
    scratch += [B((4,) + block, BF16) for block in BLOCKS]
    scratch += [B((3,) + block, BF16) for block in BLOCKS]
    scratch += [B((4, 16, W), F32), B((7, 16, W), F32)]
    scratch += [dma((16,)), dma((4,)), dma((4,)), dma((24,)), dma((24,)), dma((4,)), dma((4,))]
    scratch += [dma((3, 4))] * 6 + [dma((6,)), dma((6,))]
    out_tokens, grad_tokens, down, up, joined, vectors = pl.pallas_call(
        layer_kernel,
        name="layer",
        out_shape=(
            jax.ShapeDtypeStruct(tokens.shape, BF16),
            jax.ShapeDtypeStruct(tokens.shape, BF16),
            jax.ShapeDtypeStruct(BLOCKS[DOWN], F32),
            jax.ShapeDtypeStruct(BLOCKS[UP], F32),
            jax.ShapeDtypeStruct(BLOCKS[QKV], F32),
            jax.ShapeDtypeStruct((16, W), F32),
        ),
        in_specs=[hbm, pl.BlockSpec(memory_space=pltpu.SMEM)] + [hbm] * 5 + [vmem] * 9,
        out_specs=(hbm, hbm) + (vmem,) * 4,
        scratch_shapes=scratch,
        compiler_params=pltpu.CompilerParams(
            collective_id=1, has_side_effects=True, vmem_limit_bytes=63 * 1024 * 1024
        ),
    )(
        tokens, lengths, cotangent, w_qkv, w_out, w_up, w_down,
        b_query, b_value, b_out, first_gain, first_shift, b_up, b_down, second_gain, second_shift,
    )
    return (
        out_tokens, grad_tokens, joined[:, :576], joined[:, 576:], up, down.T,
        vectors[B_QUERY], vectors[B_VALUE], vectors[B_OUT], vectors[FIRST_GAIN], vectors[FIRST_SHIFT],
        vectors[B_UP : B_UP + 4].reshape(-1), vectors[B_DOWN], vectors[SECOND_GAIN], vectors[SECOND_SHIFT],
    )


def solution(mesh):
    in_specs = (
        P("dp", "seq", None),
        P("dp", None),
        P("dp", "seq", None),
        P(),
        P(),
        P(),
        P(),
        P(),
        P(),
        P(),
        P(),
        P(),
        P(),
        P(),
        P(),
        P(),
    )
    out_specs = (
        P("dp", "seq", None),
        P("dp", "seq", None),
        P("dp", "seq"),
        P("dp", "seq"),
        P("dp", "seq"),
        P("dp", "seq"),
        P(),
        P(),
        P(),
        P(),
        P(),
        P(),
        P(),
        P(),
        P(),
    )
    return jax.shard_map(
        local if dict(mesh.shape) == {"dp": 8, "seq": 4} else local_any, mesh=mesh, in_specs=in_specs, out_specs=out_specs, check_vma=False)
```

```python
import functools

import jax
import jax.numpy as jnp
from jax import lax
from jax.experimental import pallas as pl
from jax.experimental.pallas import tpu as pltpu
from jax.sharding import PartitionSpec as P

MESH_ID = pl.DeviceIdType.MESH
BF16 = jnp.bfloat16
F32 = jnp.float32

HEAD_DIM = 64


EPSILON = 1e-05
ROOT_HALF = 0.7071067811865476
INV_ROOT_TWO_PI = 0.3989422804014327


def contract_rows(left, right):
    return lax.dot_general(
        left, right, (((0,), (0,)), ((), ())), preferred_element_type=jnp.float32
    )


def times_transposed(left, weight_matrix):
    return lax.dot_general(
        left, weight_matrix, (((1,), (1,)), ((), ())), preferred_element_type=jnp.float32
    )


def normalize(value_rows):
    center = value_rows - jnp.mean(value_rows, axis=-1, keepdims=True)
    inverse_root = lax.rsqrt(jnp.mean(center * center, axis=-1, keepdims=True) + EPSILON)
    return (center * inverse_root, inverse_root)


def norm_backward(grad_out, normed, inverse_root, gain):
    scaled = grad_out * gain
    return inverse_root * (
        scaled
        - jnp.mean(scaled, axis=-1, keepdims=True)
        - normed * jnp.mean(scaled * normed, axis=-1, keepdims=True)
    )


def attention_forward_pass(inputs):
    queries, key_block, value_block, key_valid = inputs
    head_scale = queries.shape[-1] ** (-0.5)
    scores = (
        jnp.einsum("qhd,khd->hqk", queries, key_block, preferred_element_type=jnp.float32)
        * head_scale
    )
    scores = jnp.where(key_valid[None, None, :], scores, -1e30)
    highest = jnp.max(scores, axis=-1, keepdims=True)
    exponent = jnp.exp(scores - highest)
    row_total = jnp.sum(exponent, axis=-1, keepdims=True)
    weight_tensors = (exponent / row_total).astype(jnp.bfloat16)
    context = jnp.einsum(
        "hqk,khd->qhd", weight_tensors, value_block, preferred_element_type=jnp.float32
    )
    return (context.astype(jnp.bfloat16), (highest + jnp.log(row_total))[..., 0])


def attend_backward(inputs):
    queries, key_block, value_block, key_valid, log_total, grad_context = inputs
    head_scale = queries.shape[-1] ** (-0.5)
    scores = (
        jnp.einsum("qhd,khd->hqk", queries, key_block, preferred_element_type=jnp.float32)
        * head_scale
    )
    scores = jnp.where(key_valid[None, None, :], scores, -1e30)
    probs = jnp.exp(scores - log_total[..., None])
    grad_probs = jnp.einsum(
        "qhd,khd->hqk", grad_context, value_block, preferred_element_type=jnp.float32
    )
    row_inner = jnp.sum(probs * grad_probs, axis=-1, keepdims=True)
    grad_scores = (probs * (grad_probs - row_inner)).astype(jnp.bfloat16)
    probs_low = probs.astype(jnp.bfloat16)
    grad_queries = (
        jnp.einsum("hqk,khd->qhd", grad_scores, key_block, preferred_element_type=jnp.float32)
        * head_scale
    )
    grad_keys = (
        jnp.einsum("hqk,qhd->khd", grad_scores, queries, preferred_element_type=jnp.float32)
        * head_scale
    )
    grad_values = jnp.einsum(
        "hqk,qhd->khd", probs_low, grad_context, preferred_element_type=jnp.float32
    )
    return jnp.stack([grad_queries, grad_keys, grad_values], axis=1).astype(jnp.bfloat16)


def local_any(
    tokens,
    lengths,
    cotangent,
    w_qkv,
    b_query,
    b_value,
    w_out,
    b_out,
    first_gain,
    first_shift,
    w_up,
    b_up,
    w_down,
    b_down,
    second_gain,
    second_shift,
):
    lane_count = lax.axis_size("seq")
    seq_count, part_len, model_width = tokens.shape
    full_len = part_len * lane_count
    lane_width = model_width // lane_count
    head_size = HEAD_DIM
    heads_here = lane_width // head_size
    row_count = seq_count * part_len
    offset = lax.axis_index("seq") * part_len
    places = offset + jnp.arange(part_len, dtype=jnp.int32)
    length_row = lengths[0]
    row_live = (places[None, :] < length_row[:, None]).astype(jnp.float32).reshape(row_count, 1)
    key_valid = jnp.arange(full_len, dtype=jnp.int32)[None, :] < length_row[:, None]
    joined_bias = jnp.concatenate([b_query, jnp.zeros_like(b_query), b_value])
    tokens_flat = tokens.reshape(row_count, model_width)
    mixed = jnp.dot(tokens_flat, w_qkv, preferred_element_type=jnp.float32) + joined_bias
    qkv_heads = lax.all_to_all(
        mixed.astype(jnp.bfloat16).reshape(seq_count, part_len, 3, lane_count, lane_width),
        "seq",
        split_axis=3,
        concat_axis=1,
        tiled=True,
    )
    qkv_heads = qkv_heads.reshape(seq_count, full_len, 3, heads_here, head_size)
    context_heads, log_total = lax.map(
        attention_forward_pass,
        (qkv_heads[:, :, 0], qkv_heads[:, :, 1], qkv_heads[:, :, 2], key_valid),
    )
    context_heads = context_heads.reshape(seq_count, full_len, 1, lane_width)
    context_token_rows = lax.all_to_all(
        context_heads, "seq", split_axis=1, concat_axis=2, tiled=True
    ).reshape(row_count, model_width)
    branch = jnp.dot(context_token_rows, w_out, preferred_element_type=jnp.float32) + b_out
    normed_one, inverse_one = normalize(tokens_flat.astype(jnp.float32) + branch)
    hidden = normed_one * first_gain + first_shift
    hidden_low = hidden.astype(jnp.bfloat16)
    preactivation_input = jnp.dot(hidden_low, w_up, preferred_element_type=jnp.float32) + b_up
    active = jax.nn.gelu(preactivation_input, approximate=False).astype(jnp.bfloat16)
    ffn_out = jnp.dot(active, w_down, preferred_element_type=jnp.float32) + b_down
    normed_two, inverse_two = normalize(hidden + ffn_out)
    output_rows = (normed_two * second_gain + second_shift) * row_live
    output_tokens = output_rows.astype(jnp.bfloat16).reshape(seq_count, part_len, model_width)
    grad_out = cotangent.reshape(row_count, model_width).astype(jnp.float32) * row_live
    grad_second_gain = jnp.sum(grad_out * normed_two, axis=0)
    grad_second_shift = jnp.sum(grad_out, axis=0)
    d_sum_two = norm_backward(grad_out, normed_two, inverse_two, second_gain)
    d_ffn = d_sum_two.astype(jnp.bfloat16)
    grad_b_down = jnp.sum(d_ffn.astype(jnp.float32), axis=0)
    grad_w_down = contract_rows(active, d_ffn)
    d_active = times_transposed(d_ffn, w_down)
    gelu_slope = (
        0.5 * (1.0 + lax.erf(preactivation_input * ROOT_HALF))
        + preactivation_input
        * jnp.exp(-0.5 * preactivation_input * preactivation_input)
        * INV_ROOT_TWO_PI
    )
    d_pre = (d_active * gelu_slope).astype(jnp.bfloat16)
    grad_b_up = jnp.sum(d_pre.astype(jnp.float32), axis=0)
    grad_w_up = contract_rows(hidden_low, d_pre)
    d_hidden = d_sum_two + times_transposed(d_pre, w_up)
    grad_first_gain = jnp.sum(d_hidden * normed_one, axis=0)
    grad_first_shift = jnp.sum(d_hidden, axis=0)
    d_sum_one = norm_backward(d_hidden, normed_one, inverse_one, first_gain)
    d_branch = d_sum_one.astype(jnp.bfloat16)
    grad_b_out = jnp.sum(d_branch.astype(jnp.float32), axis=0)
    grad_w_out = contract_rows(context_token_rows, d_branch)
    d_context = times_transposed(d_branch, w_out).astype(jnp.bfloat16)
    d_context = d_context.reshape(seq_count, part_len, lane_count, lane_width)
    d_context_heads = lax.all_to_all(d_context, "seq", split_axis=2, concat_axis=1, tiled=True)
    d_context_heads = d_context_heads.reshape(seq_count, full_len, heads_here, head_size)
    d_qkv_heads = lax.map(
        attend_backward,
        (
            qkv_heads[:, :, 0],
            qkv_heads[:, :, 1],
            qkv_heads[:, :, 2],
            key_valid,
            log_total,
            d_context_heads,
        ),
    )
    d_qkv_heads = d_qkv_heads.reshape(seq_count, full_len, 3, 1, lane_width)
    d_qkv = lax.all_to_all(d_qkv_heads, "seq", split_axis=1, concat_axis=3, tiled=True).reshape(
        row_count, 3 * model_width
    )
    d_qkv_wide = d_qkv.astype(jnp.float32)
    grad_b_query = jnp.sum(d_qkv_wide[:, :model_width], axis=0)
    grad_b_value = jnp.sum(d_qkv_wide[:, 2 * model_width :], axis=0)
    grad_w_qkv = contract_rows(tokens_flat, d_qkv)
    grad_rows = d_sum_one + times_transposed(d_qkv, w_qkv)
    grad_tokens = grad_rows.astype(jnp.bfloat16).reshape(seq_count, part_len, model_width)
    matrices = (grad_w_qkv, grad_w_out, grad_w_up, grad_w_down)
    halfway = (
        lax.psum_scatter(matrices[0], "dp", scatter_dimension=0, tiled=True),
        lax.psum_scatter(matrices[1], "dp", scatter_dimension=0, tiled=True),
        lax.psum_scatter(matrices[2], "dp", scatter_dimension=0, tiled=True),
        lax.psum_scatter(matrices[3], "dp", scatter_dimension=0, tiled=True),
    )
    matrices = (
        lax.psum_scatter(
            halfway[0].astype(jnp.bfloat16), "seq", scatter_dimension=1, tiled=True
        ).astype(jnp.float32),
        lax.psum_scatter(
            halfway[1].astype(jnp.bfloat16), "seq", scatter_dimension=1, tiled=True
        ).astype(jnp.float32),
        lax.psum_scatter(
            halfway[2].astype(jnp.bfloat16), "seq", scatter_dimension=1, tiled=True
        ).astype(jnp.float32),
        lax.psum_scatter(
            halfway[3].astype(jnp.bfloat16), "seq", scatter_dimension=1, tiled=True
        ).astype(jnp.float32),
    )
    vectors = lax.psum(
        (
            grad_b_query,
            grad_b_value,
            grad_b_out,
            grad_first_gain,
            grad_first_shift,
            grad_b_up,
            grad_b_down,
            grad_second_gain,
            grad_second_shift,
        ),
        ("dp", "seq"),
    )
    return (
        output_tokens,
        grad_tokens,
        matrices[0],
        matrices[1],
        matrices[2],
        matrices[3],
        vectors[0],
        vectors[1],
        vectors[2],
        vectors[3],
        vectors[4],
        vectors[5],
        vectors[6],
        vectors[7],
        vectors[8],
    )


DOWN, UP, QKV = 0, 1, 2
BLOCKS = ((192, 384), (96, 768), (96, 768))
PLAN = (
    ((0, 0, 2), (0, 0, 1),),
    (),
    (),
    (),
    ((0, 0, 3), (0, 0, 0),),
    (),
    ((1, 0, 1), (1, 0, 2),),
    (),
    (),
    ((0, 1, 2), (0, 1, 1),),
    ((1, 0, 0), (1, 0, 3),),
    ((2, 0, 1), (2, 0, 2),),
    (),
    ((1, 1, 1), (1, 1, 2),),
    ((2, 0, 0), (0, 1, 3), (2, 0, 3), (2, 1, 1), (1, 1, 3), (0, 1, 0), (2, 1, 2), (2, 1, 3), (0, 2, 2), (0, 2, 1), (1, 1, 0), (1, 2, 1), (1, 2, 2), (0, 2, 3), (2, 1, 0), (0, 2, 0), (2, 2, 1), (2, 2, 2), (1, 2, 3), (1, 2, 0), (2, 2, 3), (2, 2, 0),),
)
X_FIRST = {(0, 0), (0, 1), (1, 1), (2, 0), (2, 1)}
ORDER_D = (2, 1, 3, 0)

B_QUERY, B_VALUE, B_OUT, FIRST_GAIN, FIRST_SHIFT, B_DOWN, SECOND_GAIN, SECOND_SHIFT, B_UP = range(9)

ROWS = 256
PART = 128
WIDTH = 768
STEP = 128


def place():
    row, lane = lax.axis_index("dp"), lax.axis_index("seq")
    return row // 2, row % 2, lane // 2, lane % 2


def device(z, y, x, core):
    return (z * 2 + y, x * 2 + core)


def remote(source, target, send, receive, where):
    return pltpu.make_async_remote_copy(
        src_ref=source,
        dst_ref=target,
        send_sem=send,
        recv_sem=receive,
        device_id=where,
        device_id_type=MESH_ID,
    )


def dot(left, right):
    return jnp.dot(left, right, preferred_element_type=F32)


def dot_t(left, right):
    return lax.dot_general(left, right, (((1,), (1,)), ((), ())), preferred_element_type=F32)


def fold(rows):
    return jnp.sum(rows.reshape(rows.shape[0] // 8, 8, rows.shape[1]), axis=0)


def mean(rows):
    return jnp.sum(rows, axis=-1, keepdims=True) * (1.0 / WIDTH)


def layer_kernel(
    tokens_in, lengths_in, cot_in, w_qkv_in, w_out_in, w_up_in, w_down_in,
    b_query_in, b_value_in, b_out_in, first_gain_in, first_shift_in, b_up_in, b_down_in, second_gain_in, second_shift_in,
    tokens_out, grad_out, down_out, up_out, qkv_out, vec_out,
    w_qkv, w_out, w_up, w_down, par, tok, cot, q3, k3, v3, bias, probs, hidden, xhat, rstd, low, slope, wide, total,
    dsum, dctx3, dkv_own, dkv_send, dkv_in, dq_t, dqkv_flat, out_rows, grad_rows,
    act, dpre, dffn_t, hid_t, tok_t, ctx_t, dqkv, dbr,
    sums_0, sums_1, sums_2, in1_0, in1_1, in1_2, in2_0, in2_1, in2_2, in3_0, in3_1, in3_2,
    vec_mine, vec_in,
    load, ex_send, ex_recv, core_send, core_recv, act_send, act_recv,
    send1, recv1, send2, recv2, send3, recv3, vec_send, vec_recv, vec_load,
    held_0, held_1, held_2, held_3, held_4, held_5, held_6, held_7, held_8,
):
    z, y, x, core = place()
    sums, in1, in2, in3 = (sums_0, sums_1, sums_2), (in1_0, in1_1, in1_2), (in2_0, in2_1, in2_2), (in3_0, in3_1, in3_2)
    at_core = device(z, y, x, 1 - core)
    at_x = device(z, y, 1 - x, core)
    at_y = device(z, 1 - y, x, core)
    at_z = [device((z + k) % 4, y, x, core) for k in (1, 2, 3)]

    loads = [pltpu.make_async_copy(tokens_in.at[x], tok.at[pl.ds(0, PART)], load.at[0])]
    for n, s in enumerate((1, 2, 0)):
        loads.append(
            pltpu.make_async_copy(
                w_qkv_in.at[:, pl.ds(WIDTH * s, WIDTH)], w_qkv.at[:, pl.ds(WIDTH * s, WIDTH)], load.at[1 + n]
            )
        )
    loads.append(pltpu.make_async_copy(cot_in.at[x], cot.at[pl.ds(0, PART)], load.at[4]))
    loads.append(pltpu.make_async_copy(w_out_in, w_out, load.at[5]))
    for t in range(4):
        loads.append(pltpu.make_async_copy(w_up_in.at[:, pl.ds(WIDTH * t, WIDTH)], w_up.at[t], load.at[6 + t]))
    for t in range(4):
        loads.append(pltpu.make_async_copy(w_down_in.at[pl.ds(WIDTH * t, WIDTH)], w_down.at[t], load.at[10 + t]))
    for copy in loads[0:4]:
        copy.start()

    vec_refs = {
        B_QUERY: (b_query_in, held_0), B_VALUE: (b_value_in, held_1), B_OUT: (b_out_in, held_2), FIRST_GAIN: (first_gain_in, held_3),
        FIRST_SHIFT: (first_shift_in, held_4), B_DOWN: (b_down_in, held_5), SECOND_GAIN: (second_gain_in, held_6),
        SECOND_SHIFT: (second_shift_in, held_7), B_UP: (b_up_in, held_8),
    }
    vec_loads = [
        pltpu.make_async_copy(source, held, vec_load.at[n]) for n, (source, held) in enumerate(vec_refs.values())
    ]
    for copy in vec_loads:
        copy.start()

    barrier = pltpu.get_barrier_semaphore()
    for where in [at_core, at_x, at_y] + at_z:
        pl.semaphore_signal(barrier, inc=1, device_id=where, device_id_type=MESH_ID)
    pl.semaphore_wait(barrier, 6)

    get_tok = remote(tokens_in.at[1 - x], tok.at[pl.ds(PART, PART)], ex_send.at[0], ex_recv.at[0], at_x)
    get_cot = remote(cot_in.at[1 - x], cot.at[pl.ds(PART, PART)], ex_send.at[1], ex_recv.at[1], at_x)
    get_tok.start()

    core_copies = []

    def to_core(source, target):
        n = len(core_copies)
        copy = remote(source, target, core_send.at[n], core_recv.at[n], at_core)
        copy.start()
        core_copies.append(copy)
        return copy

    for copy in vec_loads:
        copy.wait()
    for row, (_, held) in vec_refs.items():
        if row == B_UP:
            for t in range(4):
                par[B_UP + t : B_UP + t + 1, :] = held[WIDTH * t : WIDTH * (t + 1)].reshape(1, WIDTH)
        else:
            par[row : row + 1, :] = held[...].reshape(1, WIDTH)
    vec_mine[0] = jnp.zeros((16, WIDTH), F32)
    length = lengths_in[0, x]
    mine, across = 2 * x + core, 2 * (1 - x) + core
    theirs, theirs_across = 2 * x + 1 - core, 2 * (1 - x) + 1 - core

    def positions(shape, starts):
        n = lax.broadcasted_iota(jnp.int32, shape, 0)
        first = starts[-1] * PART
        for b in range(len(starts) - 2, -1, -1):
            first = jnp.where(n < PART * (b + 1), starts[b] * PART, first)
        return first + n % PART

    bias[...] = jnp.where(positions((512, ROWS), (mine, across, theirs, theirs_across)) < length, 0.0, -1e30)

    kv_copies = []
    for b in range(2):
        rows = slice(PART * b, PART * (b + 1))
        if b == 0:
            loads[0].wait()
        else:
            get_tok.wait_recv()
            get_cot.start()
        for n, s in enumerate((1, 2, 0)):
            if b == 0:
                loads[1 + n].wait()
            part = dot(tok[rows, :], w_qkv[:, WIDTH * s : WIDTH * (s + 1)])
            if s == 0:
                part = part + par[B_QUERY : B_QUERY + 1, :]
            if s == 2:
                part = part + par[B_VALUE : B_VALUE + 1, :]
            part = part.astype(BF16)
            if s == 0:
                part = part * jnp.asarray(0.125, BF16)
            held = (q3, k3, v3)[s]
            for j in range(6):
                held[j, rows, :] = part[:, 128 * j : 128 * (j + 1)]
            if s:
                kv_copies.append(
                    to_core(held.at[:, pl.ds(PART * b, PART)], held.at[:, pl.ds(ROWS + PART * b, PART)])
                )
        if b == 0:
            for copy in loads[5:14]:
                copy.start()
        else:
            loads[4].start()
    tok_t[:, 0:ROWS] = tok[...].T
    qkv_copies = [to_core(tok_t.at[:, pl.ds(0, ROWS)], tok_t.at[:, pl.ds(ROWS, ROWS)])]
    for copy in kv_copies:
        copy.wait_recv()

    low_half = lax.broadcasted_iota(jnp.int32, (ROWS, 128), 1) < 64

    def half_of(pair, h):
        zeros = jnp.zeros_like(pair)
        return jnp.where(low_half, pair, zeros) if h == 0 else jnp.where(low_half, zeros, pair)

    def attend(j, _):
        queries, keys = q3[j], k3[j]
        values_t = v3[j].T
        for h in range(2):
            scores = dot_t(keys, half_of(queries, h)) + bias[...]
            exponent = jnp.exp(scores - jnp.max(scores, axis=0, keepdims=True))
            weight = (exponent * (1.0 / jnp.sum(exponent, axis=0, keepdims=True))).astype(BF16)
            probs[2 * j + h] = weight
            ctx_t[pl.ds(pl.multiple_of(128 * j + 64 * h, 64), 64), 0:ROWS] = dot(values_t[64 * h : 64 * (h + 1)], weight).astype(BF16)
        return 0

    lax.fori_loop(0, 6, attend, 0, unroll=True)
    qkv_copies.append(to_core(ctx_t.at[:, pl.ds(0, ROWS)], ctx_t.at[:, pl.ds(ROWS, ROWS)]))

    loads[5].wait()
    wide[...] = dot(ctx_t[:, 0:ROWS].T, w_out[...])

    def first_norm(r, _):
        rows = pl.ds(pl.multiple_of(STEP * r, STEP), STEP)
        value = tok[rows, :].astype(F32) + wide[rows, :] + par[B_OUT : B_OUT + 1, :]
        center = value - mean(value)
        root = lax.rsqrt(mean(center * center) + EPSILON)
        normed = center * root
        out = normed * par[FIRST_GAIN : FIRST_GAIN + 1, :] + par[FIRST_SHIFT : FIRST_SHIFT + 1, :]
        xhat[rows, :] = normed
        rstd[rows, :] = root
        hidden[rows, :] = out
        low[rows, :] = out.astype(BF16)
        return 0

    lax.fori_loop(0, ROWS // STEP, first_norm, 0)
    hid_t[:, 0:ROWS] = low[...].T
    up_copies = [to_core(hid_t.at[:, pl.ds(0, ROWS)], hid_t.at[:, pl.ds(ROWS, ROWS)])]

    for n in range(6, 14):
        loads[n].wait()
    total[...] = jnp.zeros_like(total)

    def act_copy(t):
        return remote(act.at[t, pl.ds(0, ROWS)], act.at[t, pl.ds(ROWS, ROWS)], act_send.at[t], act_recv.at[t], at_core)

    for t in range(4):
        u = dot(low[...], w_up[t]) + par[B_UP + t : B_UP + t + 1, :]
        phi = 0.5 * (1.0 + lax.erf(u * ROOT_HALF))
        active = (u * phi).astype(BF16)
        act[t, 0:ROWS, :] = active
        slope[t] = phi + u * jnp.exp(-0.5 * u * u) * INV_ROOT_TWO_PI
        act_copy(t).start()
        total[...] += dot(active, w_down[t])

    loads[4].wait()
    get_cot.wait_recv()

    def second_norm(r, carry):
        rows = pl.ds(pl.multiple_of(STEP * r, STEP), STEP)
        value = hidden[rows, :] + (total[rows, :] + par[B_DOWN : B_DOWN + 1, :])
        center = value - mean(value)
        root = lax.rsqrt(mean(center * center) + EPSILON)
        normed = center * root
        n = lax.broadcasted_iota(jnp.int32, (STEP, 1), 0) + STEP * r
        live = jnp.where(jnp.where(n < PART, mine * PART + n, across * PART + n - PART) < length, 1.0, 0.0)
        out = (normed * par[SECOND_GAIN : SECOND_GAIN + 1, :] + par[SECOND_SHIFT : SECOND_SHIFT + 1, :]) * live
        out_rows[rows, :] = out.astype(BF16)
        grad = cot[rows, :].astype(F32) * live
        e = grad * par[SECOND_GAIN : SECOND_GAIN + 1, :]
        d = root * (e - mean(e) - normed * mean(e * normed))
        dsum[rows, :] = d
        d_low = d.astype(BF16)
        low[rows, :] = d_low
        gain, shift, down = carry
        return gain + fold(grad * normed), shift + fold(grad), down + fold(d_low.astype(F32))

    zero = jnp.zeros((8, WIDTH), F32)
    gain, shift, down = lax.fori_loop(0, ROWS // STEP, second_norm, (zero, zero, zero))

    def put(row, partial):
        vec_mine[0, row : row + 1, :] = jnp.sum(partial, axis=0, keepdims=True)

    put(SECOND_GAIN, gain)
    put(SECOND_SHIFT, shift)
    put(B_DOWN, down)
    out_local = pltpu.make_async_copy(out_rows.at[pl.ds(0, PART)], tokens_out.at[x], load.at[14])
    out_across = remote(out_rows.at[pl.ds(PART, PART)], tokens_out.at[x], ex_send.at[2], ex_recv.at[2], at_x)
    out_local.start()
    dffn_all = low[...].T
    for j in range(4):
        dffn_t[j, :, 0:ROWS] = dffn_all[192 * j : 192 * (j + 1), :]
    down_copies = []
    for j in (0, 2):
        there = j + 1 - core
        down_copies.append(to_core(dffn_t.at[there, :, pl.ds(0, ROWS)], dffn_t.at[there, :, pl.ds(ROWS, ROWS)]))

    def first(m, k):
        zk = (z + k) % 4
        if (m, k) in X_FIRST:
            return remote(sums[m].at[1 - x, zk], in1[m].at[zk], send1.at[m, k], recv1.at[m, k], at_x)
        return remote(sums[m].at[:, zk, 1 - y], in1[m].at[zk], send1.at[m, k], recv1.at[m, k], at_y)

    def second(m, k):
        zk = (z + k) % 4
        if (m, k) in X_FIRST:
            return remote(sums[m].at[x, zk, 1 - y], in2[m].at[zk], send2.at[m, k], recv2.at[m, k], at_y)
        return remote(sums[m].at[1 - x, zk, y], in2[m].at[zk], send2.at[m, k], recv2.at[m, k], at_x)

    def third(m, k):
        zk = (z + k) % 4
        return remote(sums[m].at[x, zk, y], in3[m].at[k - 1], send3.at[m, k], recv3.at[m, k], at_z[k - 1])

    def add_first(m, k):
        zk = (z + k) % 4
        if (m, k) in X_FIRST:
            sums[m][x, zk] = sums[m][x, zk] + in1[m][zk]
        else:
            for b in range(2):
                sums[m][b, zk, y] = sums[m][b, zk, y] + in1[m][zk, b]

    def add_second(m, k):
        zk = (z + k) % 4
        sums[m][x, zk, y] = sums[m][x, zk, y] + in2[m][zk]

    def at(point):
        for step, m, k in PLAN[point]:
            if step == 0:
                first(m, k).start()
            elif step == 1:
                first(m, k).wait_recv()
                add_first(m, k)
                second(m, k).start()
            else:
                second(m, k).wait_recv()
                add_second(m, k)
                if k:
                    third(m, k).start()

    total[...] = dsum[...]

    def feed_back(t):
        d_pre = (dot_t(low[...], w_down[t]) * slope[t]).astype(BF16)
        dpre[t, 0:ROWS, :] = d_pre
        vec_mine[0, pl.ds(B_UP + t, 1), :] = jnp.sum(fold(d_pre.astype(F32)), axis=0, keepdims=True)
        total[...] += dot_t(d_pre, w_up[t])

    for j in (0, 2):
        there = j + 1 - core
        feed_back(there)
        up_copies.append(to_core(dpre.at[there, pl.ds(0, ROWS)], dpre.at[there, pl.ds(ROWS, ROWS)]))

    for t in range(4):
        act_copy(t).wait_recv()
    for copy in down_copies:
        copy.wait_recv()
    left = jnp.concatenate([dffn_t[core], dffn_t[2 + core]], axis=0)
    for k in ORDER_D:
        t = (z + k) % 4
        part = dot(left, act[t]).astype(BF16)
        for b in range(2):
            for h in range(2):
                sums_0[b, t, h] = part[192 * b : 192 * (b + 1), 384 * h : 384 * (h + 1)]
        if (0, DOWN, k) in PLAN[0]:
            first(DOWN, k).start()
    for n, j in enumerate((0, 2)):
        feed_back(j + core)
        at(1 + n)
    for copy in up_copies:
        copy.wait_recv()
    for b in range(2):
        for n in range(3):
            part = dot(hid_t[...], dpre[2 * b + core, :, 256 * n : 256 * (n + 1)]).astype(BF16)
            sums_1[b, :, :, :, 256 * n : 256 * (n + 1)] = part.reshape(4, 2, 96, 256)
    at(3)

    def first_norm_back(r, carry):
        rows = pl.ds(pl.multiple_of(STEP * r, STEP), STEP)
        d_hidden, normed = total[rows, :], xhat[rows, :]
        e = d_hidden * par[FIRST_GAIN : FIRST_GAIN + 1, :]
        d = rstd[rows, :] * (e - mean(e) - normed * mean(e * normed))
        dsum[rows, :] = d
        d_low = d.astype(BF16)
        low[rows, :] = d_low
        gain, shift, out = carry
        return gain + fold(d_hidden * normed), shift + fold(d_hidden), out + fold(d_low.astype(F32))

    gain, shift, out = lax.fori_loop(0, ROWS // STEP, first_norm_back, (zero, zero, zero))
    put(FIRST_GAIN, gain)
    put(FIRST_SHIFT, shift)
    put(B_OUT, out)
    for j in range(4):
        dbr[j, 0:ROWS, :] = jnp.concatenate([jnp.zeros((ROWS, 64), BF16), low[:, 192 * j : 192 * (j + 1)]], axis=1)
    for j in (0, 2):
        there = j + 1 - core
        qkv_copies.append(to_core(dbr.at[there, pl.ds(0, ROWS)], dbr.at[there, pl.ds(ROWS, ROWS)]))
    d_context = dot_t(low[...], w_out[...]).astype(BF16)
    for j in range(6):
        dctx3[j] = d_context[:, 128 * j : 128 * (j + 1)]

    at(4)

    def attend_back(j, _):
        queries, keys, values, d_ctx = q3[j], k3[j], v3[j], dctx3[j]
        keys_t = keys.T
        d_keys = jnp.zeros((512, 128), F32)
        d_values = jnp.zeros((512, 128), F32)
        for h in range(2):
            d_head = half_of(d_ctx, h)
            weight = probs[2 * j + h]
            d_probs = dot_t(values, d_head)
            d_values = d_values + dot(weight, d_head)
            wide_weight = weight.astype(F32)
            inner = jnp.sum(wide_weight * d_probs, axis=0, keepdims=True)
            d_scores = (wide_weight * (d_probs - inner)).astype(BF16)
            d_keys = d_keys + dot(d_scores, half_of(queries, h))
            dq_t[pl.ds(pl.multiple_of(128 * j + 64 * h, 64), 64), :] = (dot(keys_t[64 * h : 64 * (h + 1)], d_scores) * 0.125).astype(BF16)
        dkv_own[0, j] = d_keys[0:ROWS]
        dkv_own[1, j] = d_values[0:ROWS]
        dkv_send[0, j] = d_keys[ROWS:].astype(BF16)
        dkv_send[1, j] = d_values[ROWS:].astype(BF16)
        return 0

    lax.fori_loop(0, 3, attend_back, 0, unroll=True)
    back_copies = [to_core(dkv_send.at[:, pl.ds(0, 3)], dkv_in.at[:, pl.ds(0, 3)])]
    at(5)
    lax.fori_loop(3, 6, attend_back, 0, unroll=True)
    back_copies.append(to_core(dkv_send.at[:, pl.ds(3, 3)], dkv_in.at[:, pl.ds(3, 3)]))
    at(6)
    d_queries = dq_t[...].T
    dqkv_flat[:, 0:WIDTH] = d_queries
    put(B_QUERY, fold(d_queries.astype(F32)))
    at(7)
    for copy in back_copies:
        copy.wait_recv()
    at(8)
    for j in range(6):
        for s in range(2):
            d = (dkv_own[s, j] + dkv_in[s, j].astype(F32)).astype(BF16)
            dqkv_flat[:, WIDTH * (1 + s) + 128 * j : WIDTH * (1 + s) + 128 * (j + 1)] = d
            if s:
                vec_mine[0, B_VALUE : B_VALUE + 1, 128 * j : 128 * (j + 1)] = jnp.sum(d.astype(F32), axis=0, keepdims=True)
    for j in range(4):
        dqkv[j, 0:ROWS, :] = jnp.concatenate(
            [dqkv_flat[:, 576 * j : 576 * (j + 1)], jnp.zeros((ROWS, 64), BF16)], axis=1
        )
    for j in (0, 2):
        there = j + 1 - core
        qkv_copies.append(to_core(dqkv.at[there, pl.ds(0, ROWS)], dqkv.at[there, pl.ds(ROWS, ROWS)]))
    vec_steps = [
        remote(vec_mine.at[s], vec_in.at[s], vec_send.at[s], vec_recv.at[s], w) for s, w in enumerate((at_core, at_x, at_y))
    ]
    vec_steps[0].start()
    at(9)

    for copy in qkv_copies:
        copy.wait_recv()
    at(10)
    for b in range(2):
        one = dot(tok_t[...], dqkv[2 * b + core])
        two = dot(ctx_t[...], dbr[2 * b + core])
        part = jnp.concatenate([one[:, 0:512], one[:, 512:640] + two[:, 0:128], two[:, 128:256]], axis=1).astype(BF16)
        sums_2[b] = part.reshape(4, 2, 96, WIDTH)
    at(11)
    vec_steps[0].wait_recv()
    vec_mine[1] = vec_mine[0] + vec_in[0]
    vec_steps[1].start()
    grad_rows[...] = (dsum[...] + dot_t(dqkv_flat[...], w_qkv[...])).astype(BF16)
    grad_local = pltpu.make_async_copy(grad_rows.at[pl.ds(0, PART)], grad_out.at[x], load.at[15])
    grad_across = remote(grad_rows.at[pl.ds(PART, PART)], grad_out.at[x], ex_send.at[3], ex_recv.at[3], at_x)
    grad_local.start()
    grad_across.start()
    out_across.start()
    at(12)
    vec_steps[1].wait_recv()
    vec_mine[2] = vec_mine[1] + vec_in[1]
    vec_steps[2].start()
    at(13)
    vec_steps[2].wait_recv()
    vec_mine[3] = vec_mine[2] + vec_in[2]
    vec_z = [
        remote(vec_mine.at[3], vec_in.at[3 + z], vec_send.at[2 + k], vec_recv.at[2 + k], at_z[k - 1])
        for k in (1, 2, 3)
    ]
    for copy in vec_z:
        copy.start()
    vec_in[3 + z] = vec_mine[3]
    at(14)
    for copy in vec_z:
        copy.wait_recv()
    vec_out[...] = (vec_in[3] + vec_in[4]) + (vec_in[5] + vec_in[6])
    for m, out in ((DOWN, down_out), (UP, up_out), (QKV, qkv_out)):
        for k in (1, 2, 3):
            third(m, k).wait_recv()
        block = sums[m][x, z, y].astype(F32)
        for k in range(3):
            block = block + in3[m][k].astype(F32)
        out[...] = block

    out_across.wait_recv()
    grad_across.wait_recv()
    out_local.wait()
    grad_local.wait()
    for copy in [get_tok, get_cot, out_across, grad_across] + core_copies + vec_steps + vec_z:
        copy.wait_send()
    for t in range(4):
        act_copy(t).wait_send()
    for m in (DOWN, UP, QKV):
        for k in range(4):
            first(m, k).wait_send()
            second(m, k).wait_send()
            if k:
                third(m, k).wait_send()


def finish_kernel(
    tokens_in, grad_in, down_in, up_in, joined_in, vec_in,
    tokens_out, grad_out, qkv_out, out_out, up_out, down_out,
    b_query, b_value, b_out, first_gain, first_shift, b_up, b_down, second_gain, second_shift,
):
    tokens_out[...] = tokens_in[...]
    grad_out[...] = grad_in[...]
    up_out[...] = up_in[...]
    qkv_out[...] = joined_in[:, 0:576]
    out_out[...] = joined_in[:, 576:WIDTH]
    down_out[...] = down_in[...]
    for row, ref in (
        (B_QUERY, b_query), (B_VALUE, b_value), (B_OUT, b_out), (FIRST_GAIN, first_gain), (FIRST_SHIFT, first_shift),
        (B_DOWN, b_down), (SECOND_GAIN, second_gain), (SECOND_SHIFT, second_shift),
    ):
        ref[...] = vec_in[row, :]
    for t in range(4):
        b_up[WIDTH * t : WIDTH * (t + 1)] = vec_in[B_UP + t, :]


def finish(out_tokens, grad_tokens, down, up, joined, vectors):
    vmem = pl.BlockSpec(memory_space=pltpu.VMEM)
    W = WIDTH
    shapes = [out_tokens.shape] * 2 + [(96, 576), (96, 192), up.shape, down.shape] + [(W,)] * 5 + [(4 * W,)] + [(W,)] * 3
    outs = pl.pallas_call(
        finish_kernel,
        name="finish",
        out_shape=tuple(jax.ShapeDtypeStruct(s, BF16 if n < 2 else F32) for n, s in enumerate(shapes)),
        in_specs=[vmem] * 6,
        out_specs=(vmem,) * 15,
    )(out_tokens, grad_tokens, down, up, joined, vectors)
    return outs[:5] + (outs[5].T,) + outs[6:]


def local(
    tokens, lengths, cotangent, w_qkv, b_query, b_value, w_out, b_out, first_gain, first_shift, w_up, b_up, w_down, b_down,
    second_gain, second_shift,
):
    vmem = pl.BlockSpec(memory_space=pltpu.VMEM)
    hbm = pl.BlockSpec(memory_space=pl.ANY)
    dma = pltpu.SemaphoreType.DMA
    B, W = pltpu.VMEM, WIDTH
    scratch = [
        B((W, 3 * W), BF16), B((W, W), BF16), B((4, W, W), BF16), B((4, W, W), BF16), B((16, W), F32),
        B((ROWS, W), BF16), B((ROWS, W), BF16),
        B((6, ROWS, 128), BF16), B((6, 512, 128), BF16), B((6, 512, 128), BF16),
        B((512, ROWS), F32), B((12, 512, ROWS), BF16),
        B((ROWS, W), F32), B((ROWS, W), F32), B((ROWS, 1), F32), B((ROWS, W), BF16),
        B((4, ROWS, W), F32), B((ROWS, W), F32), B((ROWS, W), F32), B((ROWS, W), F32),
        B((6, ROWS, 128), BF16), B((2, 6, ROWS, 128), F32), B((2, 6, ROWS, 128), BF16), B((2, 6, ROWS, 128), BF16),
        B((W, ROWS), BF16), B((ROWS, 3 * W), BF16), B((ROWS, W), BF16), B((ROWS, W), BF16),
        B((4, 512, W), BF16), B((4, 512, W), BF16), B((4, 192, 512), BF16),
        B((W, 512), BF16), B((W, 512), BF16), B((W, 512), BF16), B((4, 512, 640), BF16), B((4, 512, 256), BF16),
    ]
    scratch += [B((2, 4, 2) + block, BF16) for block in BLOCKS]
    scratch += [B((4, 2) + block, BF16) for block in BLOCKS]
    scratch += [B((4,) + block, BF16) for block in BLOCKS]
    scratch += [B((3,) + block, BF16) for block in BLOCKS]
    scratch += [B((4, 16, W), F32), B((7, 16, W), F32)]
    scratch += [dma((16,)), dma((4,)), dma((4,)), dma((24,)), dma((24,)), dma((4,)), dma((4,))]
    scratch += [dma((3, 4))] * 6 + [dma((6,)), dma((6,)), dma((9,))] + [B((W,), F32)] * 8 + [B((4 * W,), F32)]
    results = pl.pallas_call(
        layer_kernel,
        name="layer",
        out_shape=(
            jax.ShapeDtypeStruct(tokens.shape, BF16),
            jax.ShapeDtypeStruct(tokens.shape, BF16),
            jax.ShapeDtypeStruct(BLOCKS[DOWN], F32),
            jax.ShapeDtypeStruct(BLOCKS[UP], F32),
            jax.ShapeDtypeStruct(BLOCKS[QKV], F32),
            jax.ShapeDtypeStruct((16, W), F32),
        ),
        in_specs=[hbm, pl.BlockSpec(memory_space=pltpu.SMEM)] + [hbm] * 14,
        out_specs=(hbm, hbm) + (vmem,) * 4,
        scratch_shapes=scratch,
        compiler_params=pltpu.CompilerParams(
            collective_id=1, has_side_effects=True, vmem_limit_bytes=63 * 1024 * 1024
        ),
    )(
        tokens, lengths, cotangent, w_qkv, w_out, w_up, w_down,
        b_query, b_value, b_out, first_gain, first_shift, b_up, b_down, second_gain, second_shift,
    )
    return finish(*results)


def solution(mesh):
    in_specs = (
        P("dp", "seq", None),
        P("dp", None),
        P("dp", "seq", None),
        P(),
        P(),
        P(),
        P(),
        P(),
        P(),
        P(),
        P(),
        P(),
        P(),
        P(),
        P(),
        P(),
    )
    out_specs = (
        P("dp", "seq", None),
        P("dp", "seq", None),
        P("dp", "seq"),
        P("dp", "seq"),
        P("dp", "seq"),
        P("dp", "seq"),
        P(),
        P(),
        P(),
        P(),
        P(),
        P(),
        P(),
        P(),
        P(),
    )
    return jax.shard_map(
        local if dict(mesh.shape) == {"dp": 8, "seq": 4} else local_any, mesh=mesh, in_specs=in_specs, out_specs=out_specs, check_vma=False)
```

```python
import functools

import jax
import jax.numpy as jnp
from jax import lax
from jax.experimental import pallas as pl
from jax.experimental.pallas import tpu as pltpu
from jax.sharding import PartitionSpec as P

MESH_ID = pl.DeviceIdType.MESH
BF16 = jnp.bfloat16
F32 = jnp.float32

HEAD_DIM = 64


EPSILON = 1e-05
ROOT_HALF = 0.7071067811865476
INV_ROOT_TWO_PI = 0.3989422804014327


def contract_rows(left, right):
    return lax.dot_general(
        left, right, (((0,), (0,)), ((), ())), preferred_element_type=jnp.float32
    )


def times_transposed(left, weight_matrix):
    return lax.dot_general(
        left, weight_matrix, (((1,), (1,)), ((), ())), preferred_element_type=jnp.float32
    )


def normalize(value_rows):
    center = value_rows - jnp.mean(value_rows, axis=-1, keepdims=True)
    inverse_root = lax.rsqrt(jnp.mean(center * center, axis=-1, keepdims=True) + EPSILON)
    return (center * inverse_root, inverse_root)


def norm_backward(grad_out, normed, inverse_root, gain):
    scaled = grad_out * gain
    return inverse_root * (
        scaled
        - jnp.mean(scaled, axis=-1, keepdims=True)
        - normed * jnp.mean(scaled * normed, axis=-1, keepdims=True)
    )


def attention_forward_pass(inputs):
    queries, key_block, value_block, key_valid = inputs
    head_scale = queries.shape[-1] ** (-0.5)
    scores = (
        jnp.einsum("qhd,khd->hqk", queries, key_block, preferred_element_type=jnp.float32)
        * head_scale
    )
    scores = jnp.where(key_valid[None, None, :], scores, -1e30)
    highest = jnp.max(scores, axis=-1, keepdims=True)
    exponent = jnp.exp(scores - highest)
    row_total = jnp.sum(exponent, axis=-1, keepdims=True)
    weight_tensors = (exponent / row_total).astype(jnp.bfloat16)
    context = jnp.einsum(
        "hqk,khd->qhd", weight_tensors, value_block, preferred_element_type=jnp.float32
    )
    return (context.astype(jnp.bfloat16), (highest + jnp.log(row_total))[..., 0])


def attend_backward(inputs):
    queries, key_block, value_block, key_valid, log_total, grad_context = inputs
    head_scale = queries.shape[-1] ** (-0.5)
    scores = (
        jnp.einsum("qhd,khd->hqk", queries, key_block, preferred_element_type=jnp.float32)
        * head_scale
    )
    scores = jnp.where(key_valid[None, None, :], scores, -1e30)
    probs = jnp.exp(scores - log_total[..., None])
    grad_probs = jnp.einsum(
        "qhd,khd->hqk", grad_context, value_block, preferred_element_type=jnp.float32
    )
    row_inner = jnp.sum(probs * grad_probs, axis=-1, keepdims=True)
    grad_scores = (probs * (grad_probs - row_inner)).astype(jnp.bfloat16)
    probs_low = probs.astype(jnp.bfloat16)
    grad_queries = (
        jnp.einsum("hqk,khd->qhd", grad_scores, key_block, preferred_element_type=jnp.float32)
        * head_scale
    )
    grad_keys = (
        jnp.einsum("hqk,qhd->khd", grad_scores, queries, preferred_element_type=jnp.float32)
        * head_scale
    )
    grad_values = jnp.einsum(
        "hqk,qhd->khd", probs_low, grad_context, preferred_element_type=jnp.float32
    )
    return jnp.stack([grad_queries, grad_keys, grad_values], axis=1).astype(jnp.bfloat16)


def local_any(
    tokens,
    lengths,
    cotangent,
    w_qkv,
    b_query,
    b_value,
    w_out,
    b_out,
    first_gain,
    first_shift,
    w_up,
    b_up,
    w_down,
    b_down,
    second_gain,
    second_shift,
):
    lane_count = lax.axis_size("seq")
    seq_count, part_len, model_width = tokens.shape
    full_len = part_len * lane_count
    lane_width = model_width // lane_count
    head_size = HEAD_DIM
    heads_here = lane_width // head_size
    row_count = seq_count * part_len
    offset = lax.axis_index("seq") * part_len
    places = offset + jnp.arange(part_len, dtype=jnp.int32)
    length_row = lengths[0]
    row_live = (places[None, :] < length_row[:, None]).astype(jnp.float32).reshape(row_count, 1)
    key_valid = jnp.arange(full_len, dtype=jnp.int32)[None, :] < length_row[:, None]
    joined_bias = jnp.concatenate([b_query, jnp.zeros_like(b_query), b_value])
    tokens_flat = tokens.reshape(row_count, model_width)
    mixed = jnp.dot(tokens_flat, w_qkv, preferred_element_type=jnp.float32) + joined_bias
    qkv_heads = lax.all_to_all(
        mixed.astype(jnp.bfloat16).reshape(seq_count, part_len, 3, lane_count, lane_width),
        "seq",
        split_axis=3,
        concat_axis=1,
        tiled=True,
    )
    qkv_heads = qkv_heads.reshape(seq_count, full_len, 3, heads_here, head_size)
    context_heads, log_total = lax.map(
        attention_forward_pass,
        (qkv_heads[:, :, 0], qkv_heads[:, :, 1], qkv_heads[:, :, 2], key_valid),
    )
    context_heads = context_heads.reshape(seq_count, full_len, 1, lane_width)
    context_token_rows = lax.all_to_all(
        context_heads, "seq", split_axis=1, concat_axis=2, tiled=True
    ).reshape(row_count, model_width)
    branch = jnp.dot(context_token_rows, w_out, preferred_element_type=jnp.float32) + b_out
    normed_one, inverse_one = normalize(tokens_flat.astype(jnp.float32) + branch)
    hidden = normed_one * first_gain + first_shift
    hidden_low = hidden.astype(jnp.bfloat16)
    preactivation_input = jnp.dot(hidden_low, w_up, preferred_element_type=jnp.float32) + b_up
    active = jax.nn.gelu(preactivation_input, approximate=False).astype(jnp.bfloat16)
    ffn_out = jnp.dot(active, w_down, preferred_element_type=jnp.float32) + b_down
    normed_two, inverse_two = normalize(hidden + ffn_out)
    output_rows = (normed_two * second_gain + second_shift) * row_live
    output_tokens = output_rows.astype(jnp.bfloat16).reshape(seq_count, part_len, model_width)
    grad_out = cotangent.reshape(row_count, model_width).astype(jnp.float32) * row_live
    grad_second_gain = jnp.sum(grad_out * normed_two, axis=0)
    grad_second_shift = jnp.sum(grad_out, axis=0)
    d_sum_two = norm_backward(grad_out, normed_two, inverse_two, second_gain)
    d_ffn = d_sum_two.astype(jnp.bfloat16)
    grad_b_down = jnp.sum(d_ffn.astype(jnp.float32), axis=0)
    grad_w_down = contract_rows(active, d_ffn)
    d_active = times_transposed(d_ffn, w_down)
    gelu_slope = (
        0.5 * (1.0 + lax.erf(preactivation_input * ROOT_HALF))
        + preactivation_input
        * jnp.exp(-0.5 * preactivation_input * preactivation_input)
        * INV_ROOT_TWO_PI
    )
    d_pre = (d_active * gelu_slope).astype(jnp.bfloat16)
    grad_b_up = jnp.sum(d_pre.astype(jnp.float32), axis=0)
    grad_w_up = contract_rows(hidden_low, d_pre)
    d_hidden = d_sum_two + times_transposed(d_pre, w_up)
    grad_first_gain = jnp.sum(d_hidden * normed_one, axis=0)
    grad_first_shift = jnp.sum(d_hidden, axis=0)
    d_sum_one = norm_backward(d_hidden, normed_one, inverse_one, first_gain)
    d_branch = d_sum_one.astype(jnp.bfloat16)
    grad_b_out = jnp.sum(d_branch.astype(jnp.float32), axis=0)
    grad_w_out = contract_rows(context_token_rows, d_branch)
    d_context = times_transposed(d_branch, w_out).astype(jnp.bfloat16)
    d_context = d_context.reshape(seq_count, part_len, lane_count, lane_width)
    d_context_heads = lax.all_to_all(d_context, "seq", split_axis=2, concat_axis=1, tiled=True)
    d_context_heads = d_context_heads.reshape(seq_count, full_len, heads_here, head_size)
    d_qkv_heads = lax.map(
        attend_backward,
        (
            qkv_heads[:, :, 0],
            qkv_heads[:, :, 1],
            qkv_heads[:, :, 2],
            key_valid,
            log_total,
            d_context_heads,
        ),
    )
    d_qkv_heads = d_qkv_heads.reshape(seq_count, full_len, 3, 1, lane_width)
    d_qkv = lax.all_to_all(d_qkv_heads, "seq", split_axis=1, concat_axis=3, tiled=True).reshape(
        row_count, 3 * model_width
    )
    d_qkv_wide = d_qkv.astype(jnp.float32)
    grad_b_query = jnp.sum(d_qkv_wide[:, :model_width], axis=0)
    grad_b_value = jnp.sum(d_qkv_wide[:, 2 * model_width :], axis=0)
    grad_w_qkv = contract_rows(tokens_flat, d_qkv)
    grad_rows = d_sum_one + times_transposed(d_qkv, w_qkv)
    grad_tokens = grad_rows.astype(jnp.bfloat16).reshape(seq_count, part_len, model_width)
    matrices = (grad_w_qkv, grad_w_out, grad_w_up, grad_w_down)
    halfway = (
        lax.psum_scatter(matrices[0], "dp", scatter_dimension=0, tiled=True),
        lax.psum_scatter(matrices[1], "dp", scatter_dimension=0, tiled=True),
        lax.psum_scatter(matrices[2], "dp", scatter_dimension=0, tiled=True),
        lax.psum_scatter(matrices[3], "dp", scatter_dimension=0, tiled=True),
    )
    matrices = (
        lax.psum_scatter(
            halfway[0].astype(jnp.bfloat16), "seq", scatter_dimension=1, tiled=True
        ).astype(jnp.float32),
        lax.psum_scatter(
            halfway[1].astype(jnp.bfloat16), "seq", scatter_dimension=1, tiled=True
        ).astype(jnp.float32),
        lax.psum_scatter(
            halfway[2].astype(jnp.bfloat16), "seq", scatter_dimension=1, tiled=True
        ).astype(jnp.float32),
        lax.psum_scatter(
            halfway[3].astype(jnp.bfloat16), "seq", scatter_dimension=1, tiled=True
        ).astype(jnp.float32),
    )
    vectors = lax.psum(
        (
            grad_b_query,
            grad_b_value,
            grad_b_out,
            grad_first_gain,
            grad_first_shift,
            grad_b_up,
            grad_b_down,
            grad_second_gain,
            grad_second_shift,
        ),
        ("dp", "seq"),
    )
    return (
        output_tokens,
        grad_tokens,
        matrices[0],
        matrices[1],
        matrices[2],
        matrices[3],
        vectors[0],
        vectors[1],
        vectors[2],
        vectors[3],
        vectors[4],
        vectors[5],
        vectors[6],
        vectors[7],
        vectors[8],
    )


DOWN, UP, QKV, DOWN_Z = 0, 1, 2, 3
BLOCKS = ((96, 384), (96, 768), (96, 768), (96, 384))
PLAN = (
    ((0, 0, 3), (0, 0, 1), (0, 0, 2),),
    (),
    ((0, 0, 0),),
    ((0, 1, 3),),
    ((0, 1, 1), (0, 1, 2),),
    ((1, 0, 3), (1, 0, 1), (1, 3, 0),),
    ((1, 0, 2),),
    (),
    ((1, 0, 0), (1, 1, 3),),
    (),
    ((0, 1, 0),),
    ((0, 2, 3),),
    ((1, 1, 1), (1, 1, 2), (2, 0, 1), (2, 0, 3), (2, 3, 0),),
    ((2, 1, 3), (2, 0, 0),),
    ((2, 0, 2), (0, 2, 1), (1, 1, 0),),
    ((1, 2, 3), (2, 1, 2), (1, 2, 1), (0, 2, 2), (2, 1, 1), (2, 2, 3), (0, 2, 0), (3, 3, 0), (2, 1, 0), (1, 2, 2), (2, 2, 1), (2, 2, 2), (1, 2, 0), (4, 3, 0), (2, 2, 0),),
)
X_FIRST = {(0, 1), (1, 2), (1, 3), (2, 3)}
ORDER_D = (3, 1, 2, 0)

B_QUERY, B_VALUE, B_OUT, FIRST_GAIN, FIRST_SHIFT, B_DOWN, SECOND_GAIN, SECOND_SHIFT, B_UP = range(9)

ROWS = 256
TILE = 256
PART = 128
WIDTH = 768
STEP = 128


def place():
    row, lane = lax.axis_index("dp"), lax.axis_index("seq")
    return row // 2, row % 2, lane // 2, lane % 2


def device(z, y, x, core):
    return (z * 2 + y, x * 2 + core)


def remote(source, target, send, receive, where):
    return pltpu.make_async_remote_copy(
        src_ref=source,
        dst_ref=target,
        send_sem=send,
        recv_sem=receive,
        device_id=where,
        device_id_type=MESH_ID,
    )


def dot(left, right):
    return jnp.dot(left, right, preferred_element_type=F32)


def dot_t(left, right):
    return lax.dot_general(left, right, (((1,), (1,)), ((), ())), preferred_element_type=F32)


def fold(rows):
    return jnp.sum(rows.reshape(rows.shape[0] // 8, 8, rows.shape[1]), axis=0)


def mean(rows):
    return jnp.sum(rows, axis=-1, keepdims=True) * (1.0 / WIDTH)


def layer_kernel(
    tokens_in, lengths_in, cot_in, w_qkv_in, w_out_in, w_up_in, w_down_in,
    b_query_in, b_value_in, b_out_in, first_gain_in, first_shift_in, b_up_in, b_down_in, second_gain_in, second_shift_in,
    tokens_out, grad_out, down_out, up_out, qkv_out, vec_out,
    w_qkv, w_out, w_up, w_down, par, tok, cot, q3, k3, v3, bias, probs, hidden, xhat, rstd, low, slope, wide, total, held, turned, inverse, d_scores,
    dsum, dctx3, dkv_own, dkv_send, dkv_in, dq_t, dqkv_flat, out_rows, grad_rows,
    act, dpre, dffn_t, hid_t, tok_t, ctx_t, dqkv, dbr,
    sums_0, sums_1, sums_2, sums_z, in1_0, in1_1, in1_2, in2_0, in2_1, in2_2, in3_0, in3_1, in3_2, in1_z, in2_z, in3_z,
    vec_mine, vec_in,
    load, ex_send, ex_recv, core_send, core_recv, act_send, act_recv,
    send1, recv1, send2, recv2, send3, recv3, send_z, recv_z, vec_send, vec_recv, vec_load,
    held_0, held_1, held_2, held_3, held_4, held_5, held_6, held_7, held_8,
):
    z, y, x, core = place()
    sums, in1, in2, in3 = (sums_0, sums_1, sums_2), (in1_0, in1_1, in1_2), (in2_0, in2_1, in2_2), (in3_0, in3_1, in3_2)
    at_core = device(z, y, x, 1 - core)
    at_x = device(z, y, 1 - x, core)
    at_y = device(z, 1 - y, x, core)
    at_place = [z, z + 1 - 2 * (z % 2), (z + 2) % 4, 3 - z]
    at_z1 = device(at_place[1], y, x, core)
    at_z2 = device(at_place[2], y, x, core)

    loads = [pltpu.make_async_copy(tokens_in.at[x], tok.at[pl.ds(0, PART)], load.at[0])]
    for n, s in enumerate((1, 2, 0)):
        loads.append(
            pltpu.make_async_copy(
                w_qkv_in.at[:, pl.ds(WIDTH * s, WIDTH)], w_qkv.at[:, pl.ds(WIDTH * s, WIDTH)], load.at[1 + n]
            )
        )
    loads.append(pltpu.make_async_copy(cot_in.at[x], cot.at[pl.ds(0, PART)], load.at[4]))
    loads.append(pltpu.make_async_copy(w_out_in, w_out, load.at[5]))
    for t in range(4):
        loads.append(pltpu.make_async_copy(w_up_in.at[:, pl.ds(WIDTH * t, WIDTH)], w_up.at[t], load.at[6 + t]))
    for t in range(4):
        loads.append(pltpu.make_async_copy(w_down_in.at[pl.ds(WIDTH * t, WIDTH)], w_down.at[t], load.at[10 + t]))
    for copy in loads[0:4]:
        copy.start()

    vec_refs = {
        B_QUERY: (b_query_in, held_0), B_VALUE: (b_value_in, held_1), B_OUT: (b_out_in, held_2), FIRST_GAIN: (first_gain_in, held_3),
        FIRST_SHIFT: (first_shift_in, held_4), B_DOWN: (b_down_in, held_5), SECOND_GAIN: (second_gain_in, held_6),
        SECOND_SHIFT: (second_shift_in, held_7), B_UP: (b_up_in, held_8),
    }
    vec_loads = [
        pltpu.make_async_copy(source, vector, vec_load.at[n]) for n, (source, vector) in enumerate(vec_refs.values())
    ]
    for copy in vec_loads:
        copy.start()

    barrier = pltpu.get_barrier_semaphore()
    for where in (at_core, at_x, at_y, at_z1, at_z2):
        pl.semaphore_signal(barrier, inc=1, device_id=where, device_id_type=MESH_ID)
    pl.semaphore_wait(barrier, 5)

    get_tok = remote(tokens_in.at[1 - x], tok.at[pl.ds(PART, PART)], ex_send.at[0], ex_recv.at[0], at_x)
    get_cot = remote(cot_in.at[1 - x], cot.at[pl.ds(PART, PART)], ex_send.at[1], ex_recv.at[1], at_x)
    get_tok.start()

    core_copies = []

    def to_core(source, target):
        n = len(core_copies)
        copy = remote(source, target, core_send.at[n], core_recv.at[n], at_core)
        copy.start()
        core_copies.append(copy)
        return copy

    for copy in vec_loads:
        copy.wait()
    for row, (_, vector) in vec_refs.items():
        if row == B_UP:
            for t in range(4):
                par[B_UP + t : B_UP + t + 1, :] = vector[WIDTH * t : WIDTH * (t + 1)].reshape(1, WIDTH)
        else:
            par[row : row + 1, :] = vector[...].reshape(1, WIDTH)
    vec_mine[0] = jnp.zeros((16, WIDTH), F32)
    length = lengths_in[0, x]
    mine, across = 2 * x + core, 2 * (1 - x) + core
    theirs, theirs_across = 2 * x + 1 - core, 2 * (1 - x) + 1 - core

    def positions(shape, starts):
        n = lax.broadcasted_iota(jnp.int32, shape, 0)
        first = starts[-1] * PART
        for b in range(len(starts) - 2, -1, -1):
            first = jnp.where(n < PART * (b + 1), starts[b] * PART, first)
        return first + n % PART

    bias[...] = jnp.where(positions((512, ROWS), (mine, across, theirs, theirs_across)) < length, 0.0, -1e30)

    kv_copies = []
    for b in range(2):
        rows = slice(PART * b, PART * (b + 1))
        if b == 0:
            loads[0].wait()
        else:
            get_tok.wait_recv()
            get_cot.start()
            for copy in loads[4:14]:
                copy.start()
        for n, s in enumerate((1, 2, 0)):
            if b == 0:
                loads[1 + n].wait()
            part = dot(tok[rows, :], w_qkv[:, WIDTH * s : WIDTH * (s + 1)])
            if s == 0:
                part = part + par[B_QUERY : B_QUERY + 1, :]
            if s == 2:
                part = part + par[B_VALUE : B_VALUE + 1, :]
            part = part.astype(BF16)
            if s == 0:
                part = part * jnp.asarray(0.125, BF16)
            heads = (q3, k3, v3)[s]
            for j in range(6):
                heads[j, rows, :] = part[:, 128 * j : 128 * (j + 1)]
            if s:
                kv_copies.append(
                    to_core(heads.at[:, pl.ds(PART * b, PART)], heads.at[:, pl.ds(ROWS + PART * b, PART)])
                )
    tok_t[:, 0:ROWS] = tok[...].T
    qkv_copies = [to_core(tok_t.at[:, pl.ds(0, ROWS)], tok_t.at[:, pl.ds(ROWS, ROWS)])]
    for copy in kv_copies:
        copy.wait_recv()

    low_half = lax.broadcasted_iota(jnp.int32, (ROWS, 128), 1) < 64

    def half_of(pair, h):
        zeros = jnp.zeros_like(pair)
        return jnp.where(low_half, pair, zeros) if h == 0 else jnp.where(low_half, zeros, pair)

    for j in range(6):
        turned[j] = v3[j].T
    highest = {}

    def score(n):
        queries = half_of(q3[n // 2], n % 2)
        top = None
        for t in range(0, 512, TILE):
            scores = dot_t(k3[n // 2, t : t + TILE], queries) + bias[t : t + TILE, :]
            held[n % 2, t : t + TILE, :] = scores
            part = jnp.max(scores.reshape(TILE // 8, 8, ROWS), axis=0)
            top = part if top is None else jnp.maximum(top, part)
        highest[n] = jnp.max(top, axis=0, keepdims=True)

    def weigh(n):
        sums = None
        for t in range(0, 512, TILE):
            exponent = jnp.exp(held[n % 2, t : t + TILE, :] - highest[n])
            part = fold(exponent)
            sums = part if sums is None else sums + part
            probs[n, t : t + TILE, :] = exponent.astype(BF16)
        inverse[n : n + 1, :] = 1.0 / jnp.sum(sums, axis=0, keepdims=True)

    def gather(n):
        context = dot(turned[n // 2, 64 * (n % 2) : 64 * (n % 2 + 1)], probs[n]) * inverse[n : n + 1, :]
        ctx_t[64 * n : 64 * (n + 1), 0:ROWS] = context.astype(BF16)

    score(0)
    for n in range(12):
        if n < 11:
            score(n + 1)
        weigh(n)
        if n:
            gather(n - 1)
    gather(11)
    qkv_copies.append(to_core(ctx_t.at[:, pl.ds(0, ROWS)], ctx_t.at[:, pl.ds(ROWS, ROWS)]))

    loads[5].wait()
    wide[...] = dot(ctx_t[:, 0:ROWS].T, w_out[...])

    def first_norm(r, _):
        rows = pl.ds(pl.multiple_of(STEP * r, STEP), STEP)
        value = tok[rows, :].astype(F32) + wide[rows, :] + par[B_OUT : B_OUT + 1, :]
        center = value - mean(value)
        root = lax.rsqrt(mean(center * center) + EPSILON)
        normed = center * root
        out = normed * par[FIRST_GAIN : FIRST_GAIN + 1, :] + par[FIRST_SHIFT : FIRST_SHIFT + 1, :]
        xhat[rows, :] = normed
        rstd[rows, :] = root
        hidden[rows, :] = out
        low[rows, :] = out.astype(BF16)
        return 0

    lax.fori_loop(0, ROWS // STEP, first_norm, 0)
    hid_t[:, 0:ROWS] = low[...].T
    up_copies = [to_core(hid_t.at[:, pl.ds(0, ROWS)], hid_t.at[:, pl.ds(ROWS, ROWS)])]

    for n in range(6, 14):
        loads[n].wait()
    total[...] = jnp.zeros_like(total)

    def act_copy(t):
        return remote(act.at[t, pl.ds(0, ROWS)], act.at[t, pl.ds(ROWS, ROWS)], act_send.at[t], act_recv.at[t], at_core)

    for t in range(4):
        u = dot(low[...], w_up[t]) + par[B_UP + t : B_UP + t + 1, :]
        phi = 0.5 * (1.0 + lax.erf(u * ROOT_HALF))
        active = (u * phi).astype(BF16)
        act[t, 0:ROWS, :] = active
        slope[t] = phi + u * jnp.exp(-0.5 * u * u) * INV_ROOT_TWO_PI
        act_copy(t).start()
        total[...] += dot(active, w_down[t])

    loads[4].wait()
    get_cot.wait_recv()

    def second_norm(r, carry):
        rows = pl.ds(pl.multiple_of(STEP * r, STEP), STEP)
        value = hidden[rows, :] + (total[rows, :] + par[B_DOWN : B_DOWN + 1, :])
        center = value - mean(value)
        root = lax.rsqrt(mean(center * center) + EPSILON)
        normed = center * root
        n = lax.broadcasted_iota(jnp.int32, (STEP, 1), 0) + STEP * r
        live = jnp.where(jnp.where(n < PART, mine * PART + n, across * PART + n - PART) < length, 1.0, 0.0)
        out = (normed * par[SECOND_GAIN : SECOND_GAIN + 1, :] + par[SECOND_SHIFT : SECOND_SHIFT + 1, :]) * live
        out_rows[rows, :] = out.astype(BF16)
        grad = cot[rows, :].astype(F32) * live
        e = grad * par[SECOND_GAIN : SECOND_GAIN + 1, :]
        d = root * (e - mean(e) - normed * mean(e * normed))
        dsum[rows, :] = d
        d_low = d.astype(BF16)
        low[rows, :] = d_low
        gain, shift, down = carry
        return gain + fold(grad * normed), shift + fold(grad), down + fold(d_low.astype(F32))

    zero = jnp.zeros((8, WIDTH), F32)
    gain, shift, down = lax.fori_loop(0, ROWS // STEP, second_norm, (zero, zero, zero))

    def put(row, partial):
        vec_mine[0, row : row + 1, :] = jnp.sum(partial, axis=0, keepdims=True)

    put(SECOND_GAIN, gain)
    put(SECOND_SHIFT, shift)
    put(B_DOWN, down)
    out_local = pltpu.make_async_copy(out_rows.at[pl.ds(0, PART)], tokens_out.at[x], load.at[14])
    out_across = remote(out_rows.at[pl.ds(PART, PART)], tokens_out.at[x], ex_send.at[2], ex_recv.at[2], at_x)
    out_local.start()
    dffn_all = low[...].T
    for j in range(4):
        dffn_t[j, :, 0:ROWS] = dffn_all[192 * j : 192 * (j + 1), :]
    down_copies = []
    for j in (0, 2):
        there = j + 1 - core
        down_copies.append(to_core(dffn_t.at[there, :, pl.ds(0, ROWS)], dffn_t.at[there, :, pl.ds(ROWS, ROWS)]))

    def first(m, k):
        zk = at_place[k]
        if (m, k) in X_FIRST:
            return remote(sums[m].at[1 - x, zk], in1[m].at[zk], send1.at[m, k], recv1.at[m, k], at_x)
        return remote(sums[m].at[:, zk, 1 - y], in1[m].at[zk], send1.at[m, k], recv1.at[m, k], at_y)

    def second(m, k):
        zk = at_place[k]
        if (m, k) in X_FIRST:
            return remote(sums[m].at[x, zk, 1 - y], in2[m].at[zk], send2.at[m, k], recv2.at[m, k], at_y)
        return remote(sums[m].at[1 - x, zk, y], in2[m].at[zk], send2.at[m, k], recv2.at[m, k], at_x)

    def third(m, k):
        zk = at_place[k]
        slot, where = ((0, at_z1), (2, at_z2), (1, at_z1))[k - 1]
        return remote(sums[m].at[x, zk, y], in3[m].at[slot], send3.at[m, k], recv3.at[m, k], where)

    def add_first(m, k):
        zk = at_place[k]
        if (m, k) in X_FIRST:
            sums[m][x, zk] = sums[m][x, zk] + in1[m][zk]
        else:
            for b in range(2):
                sums[m][b, zk, y] = sums[m][b, zk, y] + in1[m][zk, b]

    def add_second(m, k):
        zk = at_place[k]
        block = sums[m][x, zk, y] + in2[m][zk]
        if k == 2:
            third(m, 3).wait_recv()
            block = block + in3[m][1]
        sums[m][x, zk, y] = block

    z_near = [
        remote(sums_z.at[:, at_place[k]], in1_z.at[n], send_z.at[n], recv_z.at[n], at_z1) for n, k in enumerate((1, 3))
    ]
    z_far = remote(sums_z.at[:, at_place[2]], in1_z.at[2], send_z.at[2], recv_z.at[2], at_z2)
    z_second = remote(sums_z.at[1 - x, z], in2_z, send_z.at[3], recv_z.at[3], at_x)
    z_third = remote(sums_z.at[x, z, 1 - y], in3_z, send_z.at[4], recv_z.at[4], at_y)

    def at_z_first(step):
        if step == 1:
            z_near[1].wait_recv()
            for b in range(2):
                sums_z[b, at_place[2]] = sums_z[b, at_place[2]] + in1_z[1, b]
            z_far.start()
        elif step == 2:
            z_near[0].wait_recv()
            z_far.wait_recv()
            for b in range(2):
                sums_z[b, z] = (sums_z[b, z].astype(F32) + in1_z[0, b].astype(F32) + in1_z[2, b].astype(F32)).astype(BF16)
            z_second.start()
        elif step == 3:
            z_second.wait_recv()
            sums_z[x, z] = sums_z[x, z] + in2_z[...]
            z_third.start()
        else:
            z_third.wait_recv()
            down_out[96:192, :] = sums_z[x, z, y].astype(F32) + in3_z[...].astype(F32)

    def at(point):
        for step, m, k in PLAN[point]:
            if m == DOWN_Z:
                at_z_first(step)
                continue
            if step == 0:
                first(m, k).start()
            elif step == 1:
                first(m, k).wait_recv()
                add_first(m, k)
                second(m, k).start()
            else:
                second(m, k).wait_recv()
                add_second(m, k)
                if k:
                    third(m, k).start()

    total[...] = dsum[...]

    def feed_back(t):
        d_pre = (dot_t(low[...], w_down[t]) * slope[t]).astype(BF16)
        dpre[t, 0:ROWS, :] = d_pre
        vec_mine[0, pl.ds(B_UP + t, 1), :] = jnp.sum(fold(d_pre.astype(F32)), axis=0, keepdims=True)
        total[...] += dot_t(d_pre, w_up[t])

    for j in (0, 2):
        there = j + 1 - core
        feed_back(there)
        up_copies.append(to_core(dpre.at[there, pl.ds(0, ROWS)], dpre.at[there, pl.ds(ROWS, ROWS)]))

    for t in range(4):
        act_copy(t).wait_recv()
    for copy in down_copies:
        copy.wait_recv()
    left = jnp.concatenate([dffn_t[core], dffn_t[2 + core]], axis=0)
    for k in ORDER_D:
        t = at_place[k]
        part = dot(left, act[t]).astype(BF16)
        for b in range(2):
            for h in range(2):
                sums_0[b, t, h] = part[192 * b : 192 * b + 96, 384 * h : 384 * (h + 1)]
                sums_z[b, t, h] = part[192 * b + 96 : 192 * (b + 1), 384 * h : 384 * (h + 1)]
        if k % 2:
            z_near[k // 2].start()
        if (0, DOWN, k) in PLAN[0]:
            first(DOWN, k).start()
    for n, j in enumerate((0, 2)):
        feed_back(j + core)
        at(1 + n)
    for copy in up_copies:
        copy.wait_recv()
    for b in range(2):
        for n in range(3):
            part = dot(hid_t[...], dpre[2 * b + core, :, 256 * n : 256 * (n + 1)]).astype(BF16)
            sums_1[b, :, :, :, 256 * n : 256 * (n + 1)] = part.reshape(4, 2, 96, 256)
    at(3)

    def first_norm_back(r, carry):
        rows = pl.ds(pl.multiple_of(STEP * r, STEP), STEP)
        d_hidden, normed = total[rows, :], xhat[rows, :]
        e = d_hidden * par[FIRST_GAIN : FIRST_GAIN + 1, :]
        d = rstd[rows, :] * (e - mean(e) - normed * mean(e * normed))
        dsum[rows, :] = d
        d_low = d.astype(BF16)
        low[rows, :] = d_low
        gain, shift, out = carry
        return gain + fold(d_hidden * normed), shift + fold(d_hidden), out + fold(d_low.astype(F32))

    gain, shift, out = lax.fori_loop(0, ROWS // STEP, first_norm_back, (zero, zero, zero))
    put(FIRST_GAIN, gain)
    put(FIRST_SHIFT, shift)
    put(B_OUT, out)
    for j in range(4):
        dbr[j, 0:ROWS, :] = jnp.concatenate([jnp.zeros((ROWS, 64), BF16), low[:, 192 * j : 192 * (j + 1)]], axis=1)
    for j in (0, 2):
        there = j + 1 - core
        qkv_copies.append(to_core(dbr.at[there, pl.ds(0, ROWS)], dbr.at[there, pl.ds(ROWS, ROWS)]))
    d_context = dot_t(low[...], w_out[...]).astype(BF16)
    for j in range(6):
        dctx3[j] = d_context[:, 128 * j : 128 * (j + 1)]

    at(4)

    for j in range(6):
        turned[j] = k3[j].T
    inverse_t = inverse[...].T
    inner, d_heads, partial_values, partial_keys = {}, {}, {}, {}

    def probs_back(n):
        d_head = (half_of(dctx3[n // 2], n % 2).astype(F32) * inverse_t[:, n : n + 1]).astype(BF16)
        sums = None
        for t in range(0, 512, TILE):
            d_probs = dot_t(v3[n // 2, t : t + TILE], d_head)
            held[n % 2, t : t + TILE, :] = d_probs
            part = fold(probs[n, t : t + TILE, :].astype(F32) * d_probs)
            sums = part if sums is None else sums + part
        inner[n] = jnp.sum(sums, axis=0, keepdims=True) * inverse[n : n + 1, :]
        partial_values[n] = dot(probs[n], d_head)

    def scores_back(n):
        for t in range(0, 512, TILE):
            d = probs[n, t : t + TILE, :].astype(F32) * (held[n % 2, t : t + TILE, :] - inner[n])
            d_scores[n % 2, t : t + TILE, :] = d.astype(BF16)

    def keys_back(n):
        j, h = n // 2, n % 2
        d_queries = dot(turned[j, 64 * h : 64 * (h + 1)], d_scores[h]) * 0.125
        dq_t[64 * n : 64 * (n + 1), :] = d_queries.astype(BF16)
        partial_keys[n] = dot(d_scores[h], half_of(q3[j], h))
        if h:
            for s, partial in enumerate((partial_keys, partial_values)):
                total_pair = partial[n - 1] + partial[n]
                dkv_own[s, j] = total_pair[0:ROWS]
                dkv_send[s, j] = total_pair[ROWS:].astype(BF16)

    def attend_back(start, stop):
        probs_back(start)
        for n in range(start, stop):
            if n < stop - 1:
                probs_back(n + 1)
            scores_back(n)
            if n > start:
                keys_back(n - 1)
        keys_back(stop - 1)

    attend_back(0, 6)
    back_copies = [to_core(dkv_send.at[:, pl.ds(0, 3)], dkv_in.at[:, pl.ds(0, 3)])]
    at(5)
    attend_back(6, 12)
    back_copies.append(to_core(dkv_send.at[:, pl.ds(3, 3)], dkv_in.at[:, pl.ds(3, 3)]))
    at(6)
    d_queries = dq_t[...].T
    dqkv_flat[:, 0:WIDTH] = d_queries
    put(B_QUERY, fold(d_queries.astype(F32)))
    at(7)
    for copy in back_copies:
        copy.wait_recv()
    at(8)
    for j in range(6):
        for s in range(2):
            d = (dkv_own[s, j] + dkv_in[s, j].astype(F32)).astype(BF16)
            dqkv_flat[:, WIDTH * (1 + s) + 128 * j : WIDTH * (1 + s) + 128 * (j + 1)] = d
            if s:
                vec_mine[0, B_VALUE : B_VALUE + 1, 128 * j : 128 * (j + 1)] = jnp.sum(d.astype(F32), axis=0, keepdims=True)
    for j in range(4):
        dqkv[j, 0:ROWS, :] = jnp.concatenate(
            [dqkv_flat[:, 576 * j : 576 * (j + 1)], jnp.zeros((ROWS, 64), BF16)], axis=1
        )
    for j in (0, 2):
        there = j + 1 - core
        qkv_copies.append(to_core(dqkv.at[there, pl.ds(0, ROWS)], dqkv.at[there, pl.ds(ROWS, ROWS)]))
    vec_steps = [
        remote(vec_mine.at[s], vec_in.at[s], vec_send.at[s], vec_recv.at[s], w)
        for s, w in enumerate((at_core, at_x, at_y, at_z1, at_z2))
    ]
    vec_steps[0].start()
    at(9)

    for copy in qkv_copies:
        copy.wait_recv()
    at(10)
    for b in range(2):
        one = dot(tok_t[...], dqkv[2 * b + core])
        two = dot(ctx_t[...], dbr[2 * b + core])
        part = jnp.concatenate([one[:, 0:512], one[:, 512:640] + two[:, 0:128], two[:, 128:256]], axis=1).astype(BF16)
        sums_2[b] = part.reshape(4, 2, 96, WIDTH)
    at(11)
    vec_steps[0].wait_recv()
    vec_mine[1] = vec_mine[0] + vec_in[0]
    vec_steps[1].start()
    grad_rows[...] = (dsum[...] + dot_t(dqkv_flat[...], w_qkv[...])).astype(BF16)
    grad_local = pltpu.make_async_copy(grad_rows.at[pl.ds(0, PART)], grad_out.at[x], load.at[15])
    grad_across = remote(grad_rows.at[pl.ds(PART, PART)], grad_out.at[x], ex_send.at[3], ex_recv.at[3], at_x)
    grad_local.start()
    grad_across.start()
    out_across.start()
    at(12)
    vec_steps[1].wait_recv()
    vec_mine[2] = vec_mine[1] + vec_in[1]
    vec_steps[2].start()
    at(13)
    vec_steps[2].wait_recv()
    vec_mine[3] = vec_mine[2] + vec_in[2]
    vec_steps[3].start()
    at(14)
    vec_steps[3].wait_recv()
    vec_mine[4] = vec_mine[3] + vec_in[3]
    vec_steps[4].start()
    at(15)
    vec_steps[4].wait_recv()
    vec_out[...] = vec_mine[4] + vec_in[4]
    for m, out in ((DOWN, down_out), (UP, up_out), (QKV, qkv_out)):
        third(m, 1).wait_recv()
        third(m, 2).wait_recv()
        block = sums[m][x, z, y].astype(F32) + in3[m][0].astype(F32) + in3[m][2].astype(F32)
        out[0 : BLOCKS[m][0], :] = block

    out_across.wait_recv()
    grad_across.wait_recv()
    out_local.wait()
    grad_local.wait()
    for copy in [get_tok, get_cot, out_across, grad_across] + core_copies + vec_steps:
        copy.wait_send()
    for t in range(4):
        act_copy(t).wait_send()
    for copy in z_near + [z_far, z_second, z_third]:
        copy.wait_send()
    for m in (DOWN, UP, QKV):
        for k in range(4):
            first(m, k).wait_send()
            second(m, k).wait_send()
            if k:
                third(m, k).wait_send()


def finish_kernel(
    tokens_in, grad_in, down_in, up_in, joined_in, vec_in,
    tokens_out, grad_out, qkv_out, out_out, up_out, down_out,
    b_query, b_value, b_out, first_gain, first_shift, b_up, b_down, second_gain, second_shift,
):
    tokens_out[...] = tokens_in[...]
    grad_out[...] = grad_in[...]
    up_out[...] = up_in[...]
    qkv_out[...] = joined_in[:, 0:576]
    out_out[...] = joined_in[:, 576:WIDTH]
    down_out[...] = down_in[...]
    for row, ref in (
        (B_QUERY, b_query), (B_VALUE, b_value), (B_OUT, b_out), (FIRST_GAIN, first_gain), (FIRST_SHIFT, first_shift),
        (B_DOWN, b_down), (SECOND_GAIN, second_gain), (SECOND_SHIFT, second_shift),
    ):
        ref[...] = vec_in[row, :]
    for t in range(4):
        b_up[WIDTH * t : WIDTH * (t + 1)] = vec_in[B_UP + t, :]


def finish(out_tokens, grad_tokens, down, up, joined, vectors):
    vmem = pl.BlockSpec(memory_space=pltpu.VMEM)
    W = WIDTH
    shapes = [out_tokens.shape] * 2 + [(96, 576), (96, 192), up.shape, down.shape] + [(W,)] * 5 + [(4 * W,)] + [(W,)] * 3
    outs = pl.pallas_call(
        finish_kernel,
        name="finish",
        out_shape=tuple(jax.ShapeDtypeStruct(s, BF16 if n < 2 else F32) for n, s in enumerate(shapes)),
        in_specs=[vmem] * 6,
        out_specs=(vmem,) * 15,
    )(out_tokens, grad_tokens, down, up, joined, vectors)
    return outs[:5] + (outs[5].T,) + outs[6:]


def local(
    tokens, lengths, cotangent, w_qkv, b_query, b_value, w_out, b_out, first_gain, first_shift, w_up, b_up, w_down, b_down,
    second_gain, second_shift,
):
    vmem = pl.BlockSpec(memory_space=pltpu.VMEM)
    hbm = pl.BlockSpec(memory_space=pl.ANY)
    dma = pltpu.SemaphoreType.DMA
    B, W = pltpu.VMEM, WIDTH
    scratch = [
        B((W, 3 * W), BF16), B((W, W), BF16), B((4, W, W), BF16), B((4, W, W), BF16), B((16, W), F32),
        B((ROWS, W), BF16), B((ROWS, W), BF16),
        B((6, ROWS, 128), BF16), B((6, 512, 128), BF16), B((6, 512, 128), BF16),
        B((512, ROWS), F32), B((12, 512, ROWS), BF16),
        B((ROWS, W), F32), B((ROWS, W), F32), B((ROWS, 1), F32), B((ROWS, W), BF16),
        B((4, ROWS, W), F32), B((ROWS, W), F32), B((ROWS, W), F32),
        B((2, 512, ROWS), F32), B((6, 128, 512), BF16), B((16, ROWS), F32), B((2, 512, ROWS), BF16), B((ROWS, W), F32),
        B((6, ROWS, 128), BF16), B((2, 6, ROWS, 128), F32), B((2, 6, ROWS, 128), BF16), B((2, 6, ROWS, 128), BF16),
        B((W, ROWS), BF16), B((ROWS, 3 * W), BF16), B((ROWS, W), BF16), B((ROWS, W), BF16),
        B((4, 512, W), BF16), B((4, 512, W), BF16), B((4, 192, 512), BF16),
        B((W, 512), BF16), B((W, 512), BF16), B((W, 512), BF16), B((4, 512, 640), BF16), B((4, 512, 256), BF16),
    ]
    scratch += [B((2, 4, 2) + block, BF16) for block in BLOCKS]
    scratch += [B((4, 2) + block, BF16) for block in BLOCKS[:DOWN_Z]]
    scratch += [B((4,) + block, BF16) for block in BLOCKS[:DOWN_Z]]
    scratch += [B((3,) + block, BF16) for block in BLOCKS[:DOWN_Z]]
    scratch += [B((3, 2, 2) + BLOCKS[DOWN_Z], BF16), B((2,) + BLOCKS[DOWN_Z], BF16), B(BLOCKS[DOWN_Z], BF16)]
    scratch += [B((5, 16, W), F32), B((5, 16, W), F32)]
    scratch += [dma((16,)), dma((4,)), dma((4,)), dma((24,)), dma((24,)), dma((4,)), dma((4,))]
    scratch += [dma((3, 4))] * 6 + [dma((5,)), dma((5,)), dma((5,)), dma((5,)), dma((9,))] + [B((W,), F32)] * 8 + [B((4 * W,), F32)]
    results = pl.pallas_call(
        layer_kernel,
        name="layer",
        out_shape=(
            jax.ShapeDtypeStruct(tokens.shape, BF16),
            jax.ShapeDtypeStruct(tokens.shape, BF16),
            jax.ShapeDtypeStruct((192, 384), F32),
            jax.ShapeDtypeStruct(BLOCKS[UP], F32),
            jax.ShapeDtypeStruct(BLOCKS[QKV], F32),
            jax.ShapeDtypeStruct((16, W), F32),
        ),
        in_specs=[hbm, pl.BlockSpec(memory_space=pltpu.SMEM)] + [hbm] * 14,
        out_specs=(hbm, hbm) + (vmem,) * 4,
        scratch_shapes=scratch,
        compiler_params=pltpu.CompilerParams(
            collective_id=1, has_side_effects=True, vmem_limit_bytes=63 * 1024 * 1024
        ),
    )(
        tokens, lengths, cotangent, w_qkv, w_out, w_up, w_down,
        b_query, b_value, b_out, first_gain, first_shift, b_up, b_down, second_gain, second_shift,
    )
    return finish(*results)


def solution(mesh):
    in_specs = (
        P("dp", "seq", None),
        P("dp", None),
        P("dp", "seq", None),
        P(),
        P(),
        P(),
        P(),
        P(),
        P(),
        P(),
        P(),
        P(),
        P(),
        P(),
        P(),
        P(),
    )
    out_specs = (
        P("dp", "seq", None),
        P("dp", "seq", None),
        P("dp", "seq"),
        P("dp", "seq"),
        P("dp", "seq"),
        P("dp", "seq"),
        P(),
        P(),
        P(),
        P(),
        P(),
        P(),
        P(),
        P(),
        P(),
    )
    return jax.shard_map(
        local if dict(mesh.shape) == {"dp": 8, "seq": 4} else local_any, mesh=mesh, in_specs=in_specs, out_specs=out_specs, check_vma=False)
```

```python
import functools

import jax
import jax.numpy as jnp
from jax import lax
from jax.experimental import pallas as pl
from jax.experimental.pallas import tpu as pltpu
from jax.sharding import PartitionSpec as P

MESH_ID = pl.DeviceIdType.MESH
BF16 = jnp.bfloat16
F32 = jnp.float32

HEAD_DIM = 64


EPSILON = 1e-05
ROOT_HALF = 0.7071067811865476
INV_ROOT_TWO_PI = 0.3989422804014327


def contract_rows(left, right):
    return lax.dot_general(
        left, right, (((0,), (0,)), ((), ())), preferred_element_type=jnp.float32
    )


def times_transposed(left, weight_matrix):
    return lax.dot_general(
        left, weight_matrix, (((1,), (1,)), ((), ())), preferred_element_type=jnp.float32
    )


def normalize(value_rows):
    center = value_rows - jnp.mean(value_rows, axis=-1, keepdims=True)
    inverse_root = lax.rsqrt(jnp.mean(center * center, axis=-1, keepdims=True) + EPSILON)
    return (center * inverse_root, inverse_root)


def norm_backward(grad_out, normed, inverse_root, gain):
    scaled = grad_out * gain
    return inverse_root * (
        scaled
        - jnp.mean(scaled, axis=-1, keepdims=True)
        - normed * jnp.mean(scaled * normed, axis=-1, keepdims=True)
    )


def attention_forward_pass(inputs):
    queries, key_block, value_block, key_valid = inputs
    head_scale = queries.shape[-1] ** (-0.5)
    scores = (
        jnp.einsum("qhd,khd->hqk", queries, key_block, preferred_element_type=jnp.float32)
        * head_scale
    )
    scores = jnp.where(key_valid[None, None, :], scores, -1e30)
    highest = jnp.max(scores, axis=-1, keepdims=True)
    exponent = jnp.exp(scores - highest)
    row_total = jnp.sum(exponent, axis=-1, keepdims=True)
    weight_tensors = (exponent / row_total).astype(jnp.bfloat16)
    context = jnp.einsum(
        "hqk,khd->qhd", weight_tensors, value_block, preferred_element_type=jnp.float32
    )
    return (context.astype(jnp.bfloat16), (highest + jnp.log(row_total))[..., 0])


def attend_backward(inputs):
    queries, key_block, value_block, key_valid, log_total, grad_context = inputs
    head_scale = queries.shape[-1] ** (-0.5)
    scores = (
        jnp.einsum("qhd,khd->hqk", queries, key_block, preferred_element_type=jnp.float32)
        * head_scale
    )
    scores = jnp.where(key_valid[None, None, :], scores, -1e30)
    probs = jnp.exp(scores - log_total[..., None])
    grad_probs = jnp.einsum(
        "qhd,khd->hqk", grad_context, value_block, preferred_element_type=jnp.float32
    )
    row_inner = jnp.sum(probs * grad_probs, axis=-1, keepdims=True)
    grad_scores = (probs * (grad_probs - row_inner)).astype(jnp.bfloat16)
    probs_low = probs.astype(jnp.bfloat16)
    grad_queries = (
        jnp.einsum("hqk,khd->qhd", grad_scores, key_block, preferred_element_type=jnp.float32)
        * head_scale
    )
    grad_keys = (
        jnp.einsum("hqk,qhd->khd", grad_scores, queries, preferred_element_type=jnp.float32)
        * head_scale
    )
    grad_values = jnp.einsum(
        "hqk,qhd->khd", probs_low, grad_context, preferred_element_type=jnp.float32
    )
    return jnp.stack([grad_queries, grad_keys, grad_values], axis=1).astype(jnp.bfloat16)


def local_any(
    tokens,
    lengths,
    cotangent,
    w_qkv,
    b_query,
    b_value,
    w_out,
    b_out,
    first_gain,
    first_shift,
    w_up,
    b_up,
    w_down,
    b_down,
    second_gain,
    second_shift,
):
    lane_count = lax.axis_size("seq")
    seq_count, part_len, model_width = tokens.shape
    full_len = part_len * lane_count
    lane_width = model_width // lane_count
    head_size = HEAD_DIM
    heads_here = lane_width // head_size
    row_count = seq_count * part_len
    offset = lax.axis_index("seq") * part_len
    places = offset + jnp.arange(part_len, dtype=jnp.int32)
    length_row = lengths[0]
    row_live = (places[None, :] < length_row[:, None]).astype(jnp.float32).reshape(row_count, 1)
    key_valid = jnp.arange(full_len, dtype=jnp.int32)[None, :] < length_row[:, None]
    joined_bias = jnp.concatenate([b_query, jnp.zeros_like(b_query), b_value])
    tokens_flat = tokens.reshape(row_count, model_width)
    mixed = jnp.dot(tokens_flat, w_qkv, preferred_element_type=jnp.float32) + joined_bias
    qkv_heads = lax.all_to_all(
        mixed.astype(jnp.bfloat16).reshape(seq_count, part_len, 3, lane_count, lane_width),
        "seq",
        split_axis=3,
        concat_axis=1,
        tiled=True,
    )
    qkv_heads = qkv_heads.reshape(seq_count, full_len, 3, heads_here, head_size)
    context_heads, log_total = lax.map(
        attention_forward_pass,
        (qkv_heads[:, :, 0], qkv_heads[:, :, 1], qkv_heads[:, :, 2], key_valid),
    )
    context_heads = context_heads.reshape(seq_count, full_len, 1, lane_width)
    context_token_rows = lax.all_to_all(
        context_heads, "seq", split_axis=1, concat_axis=2, tiled=True
    ).reshape(row_count, model_width)
    branch = jnp.dot(context_token_rows, w_out, preferred_element_type=jnp.float32) + b_out
    normed_one, inverse_one = normalize(tokens_flat.astype(jnp.float32) + branch)
    hidden = normed_one * first_gain + first_shift
    hidden_low = hidden.astype(jnp.bfloat16)
    preactivation_input = jnp.dot(hidden_low, w_up, preferred_element_type=jnp.float32) + b_up
    active = jax.nn.gelu(preactivation_input, approximate=False).astype(jnp.bfloat16)
    ffn_out = jnp.dot(active, w_down, preferred_element_type=jnp.float32) + b_down
    normed_two, inverse_two = normalize(hidden + ffn_out)
    output_rows = (normed_two * second_gain + second_shift) * row_live
    output_tokens = output_rows.astype(jnp.bfloat16).reshape(seq_count, part_len, model_width)
    grad_out = cotangent.reshape(row_count, model_width).astype(jnp.float32) * row_live
    grad_second_gain = jnp.sum(grad_out * normed_two, axis=0)
    grad_second_shift = jnp.sum(grad_out, axis=0)
    d_sum_two = norm_backward(grad_out, normed_two, inverse_two, second_gain)
    d_ffn = d_sum_two.astype(jnp.bfloat16)
    grad_b_down = jnp.sum(d_ffn.astype(jnp.float32), axis=0)
    grad_w_down = contract_rows(active, d_ffn)
    d_active = times_transposed(d_ffn, w_down)
    gelu_slope = (
        0.5 * (1.0 + lax.erf(preactivation_input * ROOT_HALF))
        + preactivation_input
        * jnp.exp(-0.5 * preactivation_input * preactivation_input)
        * INV_ROOT_TWO_PI
    )
    d_pre = (d_active * gelu_slope).astype(jnp.bfloat16)
    grad_b_up = jnp.sum(d_pre.astype(jnp.float32), axis=0)
    grad_w_up = contract_rows(hidden_low, d_pre)
    d_hidden = d_sum_two + times_transposed(d_pre, w_up)
    grad_first_gain = jnp.sum(d_hidden * normed_one, axis=0)
    grad_first_shift = jnp.sum(d_hidden, axis=0)
    d_sum_one = norm_backward(d_hidden, normed_one, inverse_one, first_gain)
    d_branch = d_sum_one.astype(jnp.bfloat16)
    grad_b_out = jnp.sum(d_branch.astype(jnp.float32), axis=0)
    grad_w_out = contract_rows(context_token_rows, d_branch)
    d_context = times_transposed(d_branch, w_out).astype(jnp.bfloat16)
    d_context = d_context.reshape(seq_count, part_len, lane_count, lane_width)
    d_context_heads = lax.all_to_all(d_context, "seq", split_axis=2, concat_axis=1, tiled=True)
    d_context_heads = d_context_heads.reshape(seq_count, full_len, heads_here, head_size)
    d_qkv_heads = lax.map(
        attend_backward,
        (
            qkv_heads[:, :, 0],
            qkv_heads[:, :, 1],
            qkv_heads[:, :, 2],
            key_valid,
            log_total,
            d_context_heads,
        ),
    )
    d_qkv_heads = d_qkv_heads.reshape(seq_count, full_len, 3, 1, lane_width)
    d_qkv = lax.all_to_all(d_qkv_heads, "seq", split_axis=1, concat_axis=3, tiled=True).reshape(
        row_count, 3 * model_width
    )
    d_qkv_wide = d_qkv.astype(jnp.float32)
    grad_b_query = jnp.sum(d_qkv_wide[:, :model_width], axis=0)
    grad_b_value = jnp.sum(d_qkv_wide[:, 2 * model_width :], axis=0)
    grad_w_qkv = contract_rows(tokens_flat, d_qkv)
    grad_rows = d_sum_one + times_transposed(d_qkv, w_qkv)
    grad_tokens = grad_rows.astype(jnp.bfloat16).reshape(seq_count, part_len, model_width)
    matrices = (grad_w_qkv, grad_w_out, grad_w_up, grad_w_down)
    halfway = (
        lax.psum_scatter(matrices[0], "dp", scatter_dimension=0, tiled=True),
        lax.psum_scatter(matrices[1], "dp", scatter_dimension=0, tiled=True),
        lax.psum_scatter(matrices[2], "dp", scatter_dimension=0, tiled=True),
        lax.psum_scatter(matrices[3], "dp", scatter_dimension=0, tiled=True),
    )
    matrices = (
        lax.psum_scatter(
            halfway[0].astype(jnp.bfloat16), "seq", scatter_dimension=1, tiled=True
        ).astype(jnp.float32),
        lax.psum_scatter(
            halfway[1].astype(jnp.bfloat16), "seq", scatter_dimension=1, tiled=True
        ).astype(jnp.float32),
        lax.psum_scatter(
            halfway[2].astype(jnp.bfloat16), "seq", scatter_dimension=1, tiled=True
        ).astype(jnp.float32),
        lax.psum_scatter(
            halfway[3].astype(jnp.bfloat16), "seq", scatter_dimension=1, tiled=True
        ).astype(jnp.float32),
    )
    vectors = lax.psum(
        (
            grad_b_query,
            grad_b_value,
            grad_b_out,
            grad_first_gain,
            grad_first_shift,
            grad_b_up,
            grad_b_down,
            grad_second_gain,
            grad_second_shift,
        ),
        ("dp", "seq"),
    )
    return (
        output_tokens,
        grad_tokens,
        matrices[0],
        matrices[1],
        matrices[2],
        matrices[3],
        vectors[0],
        vectors[1],
        vectors[2],
        vectors[3],
        vectors[4],
        vectors[5],
        vectors[6],
        vectors[7],
        vectors[8],
    )


DOWN, UP, QKV, DOWN_Z = 0, 1, 2, 3
SPLIT = 64
BLOCKS = ((SPLIT, 384), (96, 768), (96, 768), (192 - SPLIT, 384))
PLAN = (
    ((0, 0, 3), (0, 0, 2), (0, 0, 1), (0, 0, 0),),
    (),
    (),
    ((0, 1, 3), (0, 1, 2),),
    ((0, 1, 1), (0, 1, 0), (1, 0, 3), (1, 0, 0), (1, 0, 2),),
    ((1, 0, 1),),
    ((1, 3, 0),),
    ((1, 1, 2),),
    (),
    (),
    ((1, 1, 3),),
    ((0, 2, 3), (0, 2, 2), (1, 1, 0), (2, 0, 3),),
    ((1, 1, 1), (2, 0, 1), (2, 0, 0),),
    ((2, 1, 3), (2, 3, 0),),
    ((0, 2, 1), (2, 0, 2), (1, 2, 2),),
    ((1, 2, 3), (2, 1, 2), (2, 1, 1), (2, 1, 0), (0, 2, 0), (5, 1, 0), (3, 3, 0), (1, 2, 1), (2, 2, 3), (5, 0, 0), (2, 2, 2), (2, 2, 1), (1, 2, 0), (4, 3, 0),),
    ((2, 2, 0),),
)
X_FIRST = {(0, 0), (1, 0), (1, 2), (2, 2)}
ORDER_D = (3, 2, 1, 0)

B_QUERY, B_VALUE, B_OUT, FIRST_GAIN, FIRST_SHIFT, B_DOWN, SECOND_GAIN, SECOND_SHIFT, B_UP = range(9)

ROWS = 256
TILE = 256
PART = 128
WIDTH = 768
STEP = 128


def place():
    row, lane = lax.axis_index("dp"), lax.axis_index("seq")
    return row // 2, row % 2, lane // 2, lane % 2


def device(z, y, x, core):
    return (z * 2 + y, x * 2 + core)


def remote(source, target, send, receive, where):
    return pltpu.make_async_remote_copy(
        src_ref=source,
        dst_ref=target,
        send_sem=send,
        recv_sem=receive,
        device_id=where,
        device_id_type=MESH_ID,
    )


def dot(left, right):
    return jnp.dot(left, right, preferred_element_type=F32)


def dot_t(left, right):
    return lax.dot_general(left, right, (((1,), (1,)), ((), ())), preferred_element_type=F32)


def fold(rows):
    return jnp.sum(rows.reshape(rows.shape[0] // 8, 8, rows.shape[1]), axis=0)


def mean(rows):
    return jnp.sum(rows, axis=-1, keepdims=True) * (1.0 / WIDTH)


def layer_kernel(
    tokens_in, lengths_in, cot_in, w_qkv_in, w_out_in, w_up_in, w_down_in,
    b_query_in, b_value_in, b_out_in, first_gain_in, first_shift_in, b_up_in, b_down_in, second_gain_in, second_shift_in,
    tokens_out, grad_out, down_hbm, up_hbm, qkv_hbm, vec_hbm,
    w_qkv, w_out, w_up, w_down, par, tok, cot, q3, k3, v3, bias, probs, hidden, xhat, rstd, low, d_ffn, slope, wide, total, held, turned, inverse, d_scores,
    dsum, dctx3, dkv_own, dkv_send, dkv_in, dq_t, dqkv_flat, out_rows, grad_rows,
    act, dpre, dffn_t, hid_t, tok_t, ctx_t, dqkv, dbr,
    sums_0, sums_1, sums_2, sums_z, in1_0, in1_1, in1_2, in2_0, in2_1, in2_2, in3_0, in3_1, in3_2, in1_z, in2_z, in3_z,
    vec_mine, vec_in, down_out, up_out, qkv_out, vec_out,
    load, ex_send, ex_recv, core_send, core_recv, act_send, act_recv,
    send1, recv1, send2, recv2, send3, recv3, send_z, recv_z, vec_send, vec_recv, vec_load,
    held_0, held_1, held_2, held_3, held_4, held_5, held_6, held_7, held_8,
):
    z, y, x, core = place()
    sums, in1, in2, in3 = (sums_0, sums_1, sums_2), (in1_0, in1_1, in1_2), (in2_0, in2_1, in2_2), (in3_0, in3_1, in3_2)
    at_core = device(z, y, x, 1 - core)
    at_x = device(z, y, 1 - x, core)
    at_y = device(z, 1 - y, x, core)
    at_place = [z, z + 1 - 2 * (z % 2), (z + 2) % 4, 3 - z]
    at_z1 = device(at_place[1], y, x, core)
    at_z2 = device(at_place[2], y, x, core)

    loads = [pltpu.make_async_copy(tokens_in.at[x], tok.at[pl.ds(0, PART)], load.at[0])]
    for n, s in enumerate((1, 2, 0)):
        loads.append(
            pltpu.make_async_copy(
                w_qkv_in.at[:, pl.ds(WIDTH * s, WIDTH)], w_qkv.at[:, pl.ds(WIDTH * s, WIDTH)], load.at[1 + n]
            )
        )
    loads.append(pltpu.make_async_copy(cot_in.at[x], cot.at[pl.ds(0, PART)], load.at[4]))
    loads.append(pltpu.make_async_copy(w_out_in, w_out, load.at[5]))
    for t in range(4):
        loads.append(pltpu.make_async_copy(w_up_in.at[:, pl.ds(WIDTH * t, WIDTH)], w_up.at[t], load.at[6 + t]))
    for t in range(4):
        loads.append(pltpu.make_async_copy(w_down_in.at[pl.ds(WIDTH * t, WIDTH)], w_down.at[t], load.at[10 + t]))
    for copy in loads[0:4]:
        copy.start()

    vec_refs = {
        B_QUERY: (b_query_in, held_0), B_VALUE: (b_value_in, held_1), B_OUT: (b_out_in, held_2), FIRST_GAIN: (first_gain_in, held_3),
        FIRST_SHIFT: (first_shift_in, held_4), B_DOWN: (b_down_in, held_5), SECOND_GAIN: (second_gain_in, held_6),
        SECOND_SHIFT: (second_shift_in, held_7), B_UP: (b_up_in, held_8),
    }
    vec_loads = [
        pltpu.make_async_copy(source, vector, vec_load.at[n]) for n, (source, vector) in enumerate(vec_refs.values())
    ]
    for copy in vec_loads:
        copy.start()

    barrier = pltpu.get_barrier_semaphore()
    for where in (at_core, at_x, at_y, at_z1, at_z2):
        pl.semaphore_signal(barrier, inc=1, device_id=where, device_id_type=MESH_ID)
    pl.semaphore_wait(barrier, 5)

    get_tok = remote(tokens_in.at[1 - x], tok.at[pl.ds(PART, PART)], ex_send.at[0], ex_recv.at[0], at_x)
    get_cot = remote(cot_in.at[1 - x], cot.at[pl.ds(PART, PART)], ex_send.at[1], ex_recv.at[1], at_x)
    get_tok.start()

    core_copies = []

    def to_core(source, target):
        n = len(core_copies)
        copy = remote(source, target, core_send.at[n], core_recv.at[n], at_core)
        copy.start()
        core_copies.append(copy)
        return copy

    for copy in vec_loads:
        copy.wait()
    for row, (_, vector) in vec_refs.items():
        if row == B_UP:
            for t in range(4):
                par[B_UP + t : B_UP + t + 1, :] = vector[WIDTH * t : WIDTH * (t + 1)].reshape(1, WIDTH)
        else:
            par[row : row + 1, :] = vector[...].reshape(1, WIDTH)
    vec_mine[0] = jnp.zeros((16, WIDTH), F32)
    length = lengths_in[0, x]
    mine, across = 2 * x + core, 2 * (1 - x) + core
    theirs, theirs_across = 2 * x + 1 - core, 2 * (1 - x) + 1 - core

    def positions(shape, starts):
        n = lax.broadcasted_iota(jnp.int32, shape, 0)
        first = starts[-1] * PART
        for b in range(len(starts) - 2, -1, -1):
            first = jnp.where(n < PART * (b + 1), starts[b] * PART, first)
        return first + n % PART

    bias[...] = jnp.where(positions((512, ROWS), (mine, across, theirs, theirs_across)) < length, 0.0, -1e30)

    kv_copies = []
    for b in range(2):
        rows = slice(PART * b, PART * (b + 1))
        if b == 0:
            loads[0].wait()
        else:
            get_tok.wait_recv()
            get_cot.start()
            for copy in loads[4:14]:
                copy.start()
        for n, s in enumerate((1, 2, 0)):
            if b == 0:
                loads[1 + n].wait()
            part = dot(tok[rows, :], w_qkv[:, WIDTH * s : WIDTH * (s + 1)])
            if s == 0:
                part = part + par[B_QUERY : B_QUERY + 1, :]
            if s == 2:
                part = part + par[B_VALUE : B_VALUE + 1, :]
            part = part.astype(BF16)
            if s == 0:
                part = part * jnp.asarray(0.125, BF16)
            heads = (q3, k3, v3)[s]
            for j in range(6):
                heads[j, rows, :] = part[:, 128 * j : 128 * (j + 1)]
            if s:
                kv_copies.append(
                    to_core(heads.at[:, pl.ds(PART * b, PART)], heads.at[:, pl.ds(ROWS + PART * b, PART)])
                )
    tok_t[:, 0:ROWS] = tok[...].T
    qkv_copies = [to_core(tok_t.at[:, pl.ds(0, ROWS)], tok_t.at[:, pl.ds(ROWS, ROWS)])]
    for copy in kv_copies:
        copy.wait_recv()

    low_half = lax.broadcasted_iota(jnp.int32, (ROWS, 128), 1) < 64

    def half_of(pair, h):
        zeros = jnp.zeros_like(pair)
        return jnp.where(low_half, pair, zeros) if h == 0 else jnp.where(low_half, zeros, pair)

    for j in range(6):
        turned[j] = v3[j].T
    highest = {}

    def score(n):
        queries = half_of(q3[n // 2], n % 2)
        top = None
        for t in range(0, 512, TILE):
            scores = dot_t(k3[n // 2, t : t + TILE], queries) + bias[t : t + TILE, :]
            held[n % 2, t : t + TILE, :] = scores
            part = jnp.max(scores.reshape(TILE // 8, 8, ROWS), axis=0)
            top = part if top is None else jnp.maximum(top, part)
        highest[n] = jnp.max(top, axis=0, keepdims=True)

    def weigh(n):
        sums = None
        for t in range(0, 512, TILE):
            exponent = jnp.exp(held[n % 2, t : t + TILE, :] - highest[n])
            part = fold(exponent)
            sums = part if sums is None else sums + part
            probs[n, t : t + TILE, :] = exponent.astype(BF16)
        inverse[n : n + 1, :] = 1.0 / jnp.sum(sums, axis=0, keepdims=True)

    def gather(n):
        context = dot(turned[n // 2, 64 * (n % 2) : 64 * (n % 2 + 1)], probs[n]) * inverse[n : n + 1, :]
        ctx_t[64 * n : 64 * (n + 1), 0:ROWS] = context.astype(BF16)

    score(0)
    for n in range(12):
        if n < 11:
            score(n + 1)
        weigh(n)
        if n:
            gather(n - 1)
    gather(11)
    qkv_copies.append(to_core(ctx_t.at[:, pl.ds(0, ROWS)], ctx_t.at[:, pl.ds(ROWS, ROWS)]))

    loads[5].wait()
    wide[...] = dot(ctx_t[:, 0:ROWS].T, w_out[...])

    def first_norm(r, _):
        rows = pl.ds(pl.multiple_of(STEP * r, STEP), STEP)
        value = tok[rows, :].astype(F32) + wide[rows, :] + par[B_OUT : B_OUT + 1, :]
        center = value - mean(value)
        root = lax.rsqrt(mean(center * center) + EPSILON)
        normed = center * root
        out = normed * par[FIRST_GAIN : FIRST_GAIN + 1, :] + par[FIRST_SHIFT : FIRST_SHIFT + 1, :]
        xhat[rows, :] = normed
        rstd[rows, :] = root
        hidden[rows, :] = out
        low[rows, :] = out.astype(BF16)
        return 0

    lax.fori_loop(0, ROWS // STEP, first_norm, 0)
    up_copies = []

    for n in range(6, 14):
        loads[n].wait()

    def act_copy(t):
        return remote(act.at[t, pl.ds(0, ROWS)], act.at[t, pl.ds(ROWS, ROWS)], act_send.at[t], act_recv.at[t], at_core)

    for t in range(4):
        u = dot(low[...], w_up[t]) + par[B_UP + t : B_UP + t + 1, :]
        phi = 0.5 * (1.0 + lax.erf(u * ROOT_HALF))
        active = (u * phi).astype(BF16)
        act[t, 0:ROWS, :] = active
        slope[t] = phi + u * jnp.exp(-0.5 * u * u) * INV_ROOT_TWO_PI
        act_copy(t).start()
        product = dot(active, w_down[t])
        total[...] = total[...] + product if t else product

    loads[4].wait()
    get_cot.wait_recv()

    def live_rows(r):
        n = lax.broadcasted_iota(jnp.int32, (STEP, 1), 0) + STEP * r
        return jnp.where(jnp.where(n < PART, mine * PART + n, across * PART + n - PART) < length, 1.0, 0.0)

    def second_norm(r, _):
        rows = pl.ds(pl.multiple_of(STEP * r, STEP), STEP)
        value = hidden[rows, :] + (total[rows, :] + par[B_DOWN : B_DOWN + 1, :])
        center = value - mean(value)
        root = lax.rsqrt(mean(center * center) + EPSILON)
        normed = center * root
        wide[rows, :] = normed
        e = cot[rows, :].astype(F32) * live_rows(r) * par[SECOND_GAIN : SECOND_GAIN + 1, :]
        d = root * (e - mean(e) - normed * mean(e * normed))
        dsum[rows, :] = d
        d_ffn[rows, :] = d.astype(BF16)
        return 0

    lax.fori_loop(0, ROWS // STEP, second_norm, 0)

    def second_norm_rest(r, carry):
        rows = pl.ds(pl.multiple_of(STEP * r, STEP), STEP)
        live, normed = live_rows(r), wide[rows, :]
        out = (normed * par[SECOND_GAIN : SECOND_GAIN + 1, :] + par[SECOND_SHIFT : SECOND_SHIFT + 1, :]) * live
        out_rows[rows, :] = out.astype(BF16)
        grad = cot[rows, :].astype(F32) * live
        gain, shift, down = carry
        return gain + fold(grad * normed), shift + fold(grad), down + fold(d_ffn[rows, :].astype(F32))

    zero = jnp.zeros((8, WIDTH), F32)

    def put(row, partial):
        vec_mine[0, row : row + 1, :] = jnp.sum(partial, axis=0, keepdims=True)

    out_local = pltpu.make_async_copy(out_rows.at[pl.ds(0, PART)], tokens_out.at[x], load.at[14])
    out_across = remote(out_rows.at[pl.ds(PART, PART)], tokens_out.at[x], ex_send.at[2], ex_recv.at[2], at_x)
    dffn_all = d_ffn[...].T
    for j in range(4):
        dffn_t[j, :, 0:ROWS] = dffn_all[192 * j : 192 * (j + 1), :]
    down_copies = []
    for j in (0, 2):
        there = j + 1 - core
        down_copies.append(to_core(dffn_t.at[there, :, pl.ds(0, ROWS)], dffn_t.at[there, :, pl.ds(ROWS, ROWS)]))

    def first(m, k):
        zk = at_place[k]
        if (m, k) in X_FIRST:
            return remote(sums[m].at[1 - x, zk], in1[m].at[zk], send1.at[m, k], recv1.at[m, k], at_x)
        return remote(sums[m].at[:, zk, 1 - y], in1[m].at[zk], send1.at[m, k], recv1.at[m, k], at_y)

    def second(m, k):
        zk = at_place[k]
        if (m, k) in X_FIRST:
            return remote(sums[m].at[x, zk, 1 - y], in2[m].at[zk], send2.at[m, k], recv2.at[m, k], at_y)
        return remote(sums[m].at[1 - x, zk, y], in2[m].at[zk], send2.at[m, k], recv2.at[m, k], at_x)

    def third(m, k):
        zk = at_place[k]
        slot, where = ((0, at_z1), (2, at_z2), (1, at_z1))[k - 1]
        return remote(sums[m].at[x, zk, y], in3[m].at[slot], send3.at[m, k], recv3.at[m, k], where)

    def add_first(m, k):
        zk = at_place[k]
        if (m, k) in X_FIRST:
            sums[m][x, zk] = sums[m][x, zk] + in1[m][zk]
        else:
            for b in range(2):
                sums[m][b, zk, y] = sums[m][b, zk, y] + in1[m][zk, b]

    def add_second(m, k):
        zk = at_place[k]
        block = sums[m][x, zk, y] + in2[m][zk]
        if k == 2:
            third(m, 3).wait_recv()
            block = block + in3[m][1]
        sums[m][x, zk, y] = block

    z_near = [
        remote(sums_z.at[:, at_place[k]], in1_z.at[n], send_z.at[n], recv_z.at[n], at_z1) for n, k in enumerate((1, 3))
    ]
    z_far = remote(sums_z.at[:, at_place[2]], in1_z.at[2], send_z.at[2], recv_z.at[2], at_z2)
    z_second = remote(sums_z.at[1 - x, z], in2_z, send_z.at[3], recv_z.at[3], at_x)
    z_third = remote(sums_z.at[x, z, 1 - y], in3_z, send_z.at[4], recv_z.at[4], at_y)

    def at_z_first(step):
        if step == 1:
            z_near[1].wait_recv()
            for b in range(2):
                sums_z[b, at_place[2]] = sums_z[b, at_place[2]] + in1_z[1, b]
            z_far.start()
        elif step == 2:
            z_near[0].wait_recv()
            z_far.wait_recv()
            for b in range(2):
                sums_z[b, z] = (sums_z[b, z].astype(F32) + in1_z[0, b].astype(F32) + in1_z[2, b].astype(F32)).astype(BF16)
            z_second.start()
        elif step == 3:
            z_second.wait_recv()
            sums_z[x, z] = sums_z[x, z] + in2_z[...]
            z_third.start()
        else:
            z_third.wait_recv()
            down_out[SPLIT:192, :] = sums_z[x, z, y].astype(F32) + in3_z[...].astype(F32)

    def at(point):
        for step, m, k in PLAN[point]:
            if step == 5:
                (out_across, grad_across)[m].start()
                continue
            if m == DOWN_Z:
                at_z_first(step)
                continue
            if step == 0:
                first(m, k).start()
            elif step == 1:
                first(m, k).wait_recv()
                add_first(m, k)
                second(m, k).start()
            else:
                second(m, k).wait_recv()
                add_second(m, k)
                if k:
                    third(m, k).start()

    before = [dsum]

    def feed_back(t):
        d_pre = (dot_t(d_ffn[...], w_down[t]) * slope[t]).astype(BF16)
        dpre[t, 0:ROWS, :] = d_pre
        vec_mine[0, pl.ds(B_UP + t, 1), :] = jnp.sum(fold(d_pre.astype(F32)), axis=0, keepdims=True)
        total[...] = before[-1][...] + dot_t(d_pre, w_up[t])
        before.append(total)

    for j in (0, 2):
        there = j + 1 - core
        feed_back(there)
        up_copies.append(to_core(dpre.at[there, pl.ds(0, ROWS)], dpre.at[there, pl.ds(ROWS, ROWS)]))

    for t in range(4):
        act_copy(t).wait_recv()
    for copy in down_copies:
        copy.wait_recv()
    left = jnp.concatenate([dffn_t[core], dffn_t[2 + core]], axis=0)
    for k in ORDER_D:
        t = at_place[k]
        part = dot(left, act[t]).astype(BF16)
        for b in range(2):
            for h in range(2):
                sums_0[b, t, h] = part[192 * b : 192 * b + SPLIT, 384 * h : 384 * (h + 1)]
                sums_z[b, t, h] = part[192 * b + SPLIT : 192 * (b + 1), 384 * h : 384 * (h + 1)]
        if k % 2:
            z_near[k // 2].start()
        if (0, DOWN, k) in PLAN[0]:
            first(DOWN, k).start()
    hid_t[:, 0:ROWS] = low[...].T
    up_copies.append(to_core(hid_t.at[:, pl.ds(0, ROWS)], hid_t.at[:, pl.ds(ROWS, ROWS)]))
    for n, j in enumerate((0, 2)):
        feed_back(j + core)
        at(1 + n)
    for copy in up_copies:
        copy.wait_recv()
    for b in range(2):
        for n in range(3):
            part = dot(hid_t[...], dpre[2 * b + core, :, 256 * n : 256 * (n + 1)]).astype(BF16)
            sums_1[b, :, :, :, 256 * n : 256 * (n + 1)] = part.reshape(4, 2, 96, 256)
    at(3)
    gain, shift, down = lax.fori_loop(0, ROWS // STEP, second_norm_rest, (zero, zero, zero))
    put(SECOND_GAIN, gain)
    put(SECOND_SHIFT, shift)
    put(B_DOWN, down)
    out_local.start()

    def first_norm_back(r, carry):
        rows = pl.ds(pl.multiple_of(STEP * r, STEP), STEP)
        d_hidden, normed = total[rows, :], xhat[rows, :]
        e = d_hidden * par[FIRST_GAIN : FIRST_GAIN + 1, :]
        d = rstd[rows, :] * (e - mean(e) - normed * mean(e * normed))
        dsum[rows, :] = d
        d_low = d.astype(BF16)
        low[rows, :] = d_low
        gain, shift, out = carry
        return gain + fold(d_hidden * normed), shift + fold(d_hidden), out + fold(d_low.astype(F32))

    gain, shift, out = lax.fori_loop(0, ROWS // STEP, first_norm_back, (zero, zero, zero))
    put(FIRST_GAIN, gain)
    put(FIRST_SHIFT, shift)
    put(B_OUT, out)
    for j in range(4):
        dbr[j, 0:ROWS, :] = jnp.concatenate([jnp.zeros((ROWS, 64), BF16), low[:, 192 * j : 192 * (j + 1)]], axis=1)
    for j in (0, 2):
        there = j + 1 - core
        qkv_copies.append(to_core(dbr.at[there, pl.ds(0, ROWS)], dbr.at[there, pl.ds(ROWS, ROWS)]))
    d_context = dot_t(low[...], w_out[...]).astype(BF16)
    for j in range(6):
        dctx3[j] = d_context[:, 128 * j : 128 * (j + 1)]

    at(4)

    for j in range(6):
        turned[j] = k3[j].T
    inverse_t = inverse[...].T
    inner, d_heads, partial_values, partial_keys = {}, {}, {}, {}

    def probs_back(n):
        d_head = (half_of(dctx3[n // 2], n % 2).astype(F32) * inverse_t[:, n : n + 1]).astype(BF16)
        sums = None
        for t in range(0, 512, TILE):
            d_probs = dot_t(v3[n // 2, t : t + TILE], d_head)
            held[n % 2, t : t + TILE, :] = d_probs
            part = fold(probs[n, t : t + TILE, :].astype(F32) * d_probs)
            sums = part if sums is None else sums + part
        inner[n] = jnp.sum(sums, axis=0, keepdims=True) * inverse[n : n + 1, :]
        partial_values[n] = dot(probs[n], d_head)

    def scores_back(n):
        for t in range(0, 512, TILE):
            d = probs[n, t : t + TILE, :].astype(F32) * (held[n % 2, t : t + TILE, :] - inner[n])
            d_scores[n % 2, t : t + TILE, :] = d.astype(BF16)

    def keys_back(n):
        j, h = n // 2, n % 2
        d_queries = dot(turned[j, 64 * h : 64 * (h + 1)], d_scores[h]) * 0.125
        dq_t[64 * n : 64 * (n + 1), :] = d_queries.astype(BF16)
        partial_keys[n] = dot(d_scores[h], half_of(q3[j], h))
        if h:
            for s, partial in enumerate((partial_keys, partial_values)):
                total_pair = partial[n - 1] + partial[n]
                dkv_own[s, j] = total_pair[0:ROWS]
                dkv_send[s, j] = total_pair[ROWS:].astype(BF16)

    def attend_back(start, stop):
        probs_back(start)
        for n in range(start, stop):
            if n < stop - 1:
                probs_back(n + 1)
            scores_back(n)
            if n > start:
                keys_back(n - 1)
        keys_back(stop - 1)

    attend_back(0, 6)
    back_copies = [to_core(dkv_send.at[:, pl.ds(0, 3)], dkv_in.at[:, pl.ds(0, 3)])]
    at(5)
    attend_back(6, 12)
    back_copies.append(to_core(dkv_send.at[:, pl.ds(3, 3)], dkv_in.at[:, pl.ds(3, 3)]))
    at(6)
    d_queries = dq_t[...].T
    dqkv_flat[:, 0:WIDTH] = d_queries
    put(B_QUERY, fold(d_queries.astype(F32)))
    at(7)
    for copy in back_copies:
        copy.wait_recv()
    at(8)
    for j in range(6):
        for s in range(2):
            d = (dkv_own[s, j] + dkv_in[s, j].astype(F32)).astype(BF16)
            dqkv_flat[:, WIDTH * (1 + s) + 128 * j : WIDTH * (1 + s) + 128 * (j + 1)] = d
            if s:
                vec_mine[0, B_VALUE : B_VALUE + 1, 128 * j : 128 * (j + 1)] = jnp.sum(d.astype(F32), axis=0, keepdims=True)
    for j in range(4):
        dqkv[j, 0:ROWS, :] = jnp.concatenate(
            [dqkv_flat[:, 576 * j : 576 * (j + 1)], jnp.zeros((ROWS, 64), BF16)], axis=1
        )
    for j in (0, 2):
        there = j + 1 - core
        qkv_copies.append(to_core(dqkv.at[there, pl.ds(0, ROWS)], dqkv.at[there, pl.ds(ROWS, ROWS)]))
    vec_steps = [
        remote(vec_mine.at[s], vec_in.at[s], vec_send.at[s], vec_recv.at[s], w)
        for s, w in enumerate((at_core, at_x, at_y, at_z1, at_z2))
    ]
    vec_steps[0].start()
    at(9)

    for copy in qkv_copies:
        copy.wait_recv()
    at(10)
    for b in range(2):
        one = dot(tok_t[...], dqkv[2 * b + core])
        two = dot(ctx_t[...], dbr[2 * b + core])
        part = jnp.concatenate([one[:, 0:512], one[:, 512:640] + two[:, 0:128], two[:, 128:256]], axis=1).astype(BF16)
        sums_2[b] = part.reshape(4, 2, 96, WIDTH)
    at(11)
    vec_steps[0].wait_recv()
    vec_mine[1] = vec_mine[0] + vec_in[0]
    vec_steps[1].start()
    grad_rows[...] = (dsum[...] + dot_t(dqkv_flat[...], w_qkv[...])).astype(BF16)
    grad_local = pltpu.make_async_copy(grad_rows.at[pl.ds(0, PART)], grad_out.at[x], load.at[15])
    grad_across = remote(grad_rows.at[pl.ds(PART, PART)], grad_out.at[x], ex_send.at[3], ex_recv.at[3], at_x)
    grad_local.start()
    at(12)
    vec_steps[1].wait_recv()
    vec_mine[2] = vec_mine[1] + vec_in[1]
    vec_steps[2].start()
    at(13)
    vec_steps[2].wait_recv()
    vec_mine[3] = vec_mine[2] + vec_in[2]
    vec_steps[3].start()
    at(14)
    vec_steps[3].wait_recv()
    vec_mine[4] = vec_mine[3] + vec_in[3]
    vec_steps[4].start()
    at(15)
    vec_steps[4].wait_recv()
    vec_out[...] = vec_mine[4] + vec_in[4]
    results = [pltpu.make_async_copy(vec_out, vec_hbm, load.at[19])]
    results[0].start()

    def finish_block(m):
        out, target = ((down_out, down_hbm), (up_out, up_hbm), (qkv_out, qkv_hbm))[m]
        third(m, 1).wait_recv()
        third(m, 2).wait_recv()
        block = sums[m][x, z, y].astype(F32) + in3[m][0].astype(F32) + in3[m][2].astype(F32)
        out[0 : BLOCKS[m][0], :] = block
        results.append(pltpu.make_async_copy(out, target, load.at[16 + m]))
        results[-1].start()

    finish_block(DOWN)
    finish_block(UP)
    at(16)
    finish_block(QKV)

    out_across.wait_recv()
    grad_across.wait_recv()
    out_local.wait()
    grad_local.wait()
    for copy in results:
        copy.wait()
    for copy in [get_tok, get_cot, out_across, grad_across] + core_copies + vec_steps:
        copy.wait_send()
    for t in range(4):
        act_copy(t).wait_send()
    for copy in z_near + [z_far, z_second, z_third]:
        copy.wait_send()
    for m in (DOWN, UP, QKV):
        for k in range(4):
            first(m, k).wait_send()
            second(m, k).wait_send()
            if k:
                third(m, k).wait_send()


def finish_kernel(
    tokens_in, grad_in, down_in, up_in, joined_in, vec_in,
    tokens_out, grad_out, qkv_out, out_out, up_out, down_out,
    b_query, b_value, b_out, first_gain, first_shift, b_up, b_down, second_gain, second_shift,
    tokens, grad, down, up, joined, vec, qkv, out, vec_0, vec_1, vec_2, vec_3, vec_4, vec_5, vec_6, vec_7, vec_8, get, give,
):
    pairs = ((joined_in, joined), (vec_in, vec), (tokens_in, tokens), (grad_in, grad), (down_in, down), (up_in, up))
    gets = [pltpu.make_async_copy(source, held, get.at[n]) for n, (source, held) in enumerate(pairs)]
    for copy in gets:
        copy.start()
    gives = []

    def put(held, target):
        gives.append(pltpu.make_async_copy(held, target, give.at[len(gives)]))
        gives[-1].start()

    for n, (held, target) in ((2, (tokens, tokens_out)), (3, (grad, grad_out)), (4, (down, down_out)), (5, (up, up_out))):
        gets[n].wait()
        put(held, target)
    gets[0].wait()
    qkv[...] = joined[:, 0:576]
    put(qkv, qkv_out)
    out[...] = joined[:, 576:WIDTH]
    put(out, out_out)
    gets[1].wait()
    for row, held, target in (
        (B_QUERY, vec_0, b_query), (B_VALUE, vec_1, b_value), (B_OUT, vec_2, b_out), (FIRST_GAIN, vec_3, first_gain),
        (FIRST_SHIFT, vec_4, first_shift), (B_DOWN, vec_5, b_down), (SECOND_GAIN, vec_6, second_gain),
        (SECOND_SHIFT, vec_7, second_shift),
    ):
        held[...] = vec[row, :]
        put(held, target)
    for t in range(4):
        vec_8[WIDTH * t : WIDTH * (t + 1)] = vec[B_UP + t, :]
    put(vec_8, b_up)
    for copy in gives:
        copy.wait()


def finish(out_tokens, grad_tokens, down, up, joined, vectors):
    hbm = pl.BlockSpec(memory_space=pl.ANY)
    W = WIDTH
    shapes = [out_tokens.shape] * 2 + [(96, 576), (96, 192), up.shape, down.shape] + [(W,)] * 5 + [(4 * W,)] + [(W,)] * 3
    inputs = (out_tokens, grad_tokens, down, up, joined, vectors)
    scratch = [pltpu.VMEM(a.shape, a.dtype) for a in inputs] + [pltpu.VMEM((96, 576), F32), pltpu.VMEM((96, 192), F32)]
    scratch += [pltpu.VMEM((W,), F32)] * 8 + [pltpu.VMEM((4 * W,), F32)]
    outs = pl.pallas_call(
        finish_kernel,
        name="finish",
        out_shape=tuple(jax.ShapeDtypeStruct(s, BF16 if n < 2 else F32) for n, s in enumerate(shapes)),
        in_specs=[hbm] * 6,
        out_specs=(hbm,) * 15,
        scratch_shapes=scratch + [pltpu.SemaphoreType.DMA((6,)), pltpu.SemaphoreType.DMA((15,))],
    )(*inputs)
    return outs[:5] + (outs[5].T,) + outs[6:]


def local(
    tokens, lengths, cotangent, w_qkv, b_query, b_value, w_out, b_out, first_gain, first_shift, w_up, b_up, w_down, b_down,
    second_gain, second_shift,
):
    hbm = pl.BlockSpec(memory_space=pl.ANY)
    dma = pltpu.SemaphoreType.DMA
    B, W = pltpu.VMEM, WIDTH
    scratch = [
        B((W, 3 * W), BF16), B((W, W), BF16), B((4, W, W), BF16), B((4, W, W), BF16), B((16, W), F32),
        B((ROWS, W), BF16), B((ROWS, W), BF16),
        B((6, ROWS, 128), BF16), B((6, 512, 128), BF16), B((6, 512, 128), BF16),
        B((512, ROWS), F32), B((12, 512, ROWS), BF16),
        B((ROWS, W), F32), B((ROWS, W), F32), B((ROWS, 1), F32), B((ROWS, W), BF16), B((ROWS, W), BF16),
        B((4, ROWS, W), F32), B((ROWS, W), F32), B((ROWS, W), F32),
        B((2, 512, ROWS), F32), B((6, 128, 512), BF16), B((16, ROWS), F32), B((2, 512, ROWS), BF16), B((ROWS, W), F32),
        B((6, ROWS, 128), BF16), B((2, 6, ROWS, 128), F32), B((2, 6, ROWS, 128), BF16), B((2, 6, ROWS, 128), BF16),
        B((W, ROWS), BF16), B((ROWS, 3 * W), BF16), B((ROWS, W), BF16), B((ROWS, W), BF16),
        B((4, 512, W), BF16), B((4, 512, W), BF16), B((4, 192, 512), BF16),
        B((W, 512), BF16), B((W, 512), BF16), B((W, 512), BF16), B((4, 512, 640), BF16), B((4, 512, 256), BF16),
    ]
    scratch += [B((2, 4, 2) + block, BF16) for block in BLOCKS]
    scratch += [B((4, 2) + block, BF16) for block in BLOCKS[:DOWN_Z]]
    scratch += [B((4,) + block, BF16) for block in BLOCKS[:DOWN_Z]]
    scratch += [B((3,) + block, BF16) for block in BLOCKS[:DOWN_Z]]
    scratch += [B((3, 2, 2) + BLOCKS[DOWN_Z], BF16), B((2,) + BLOCKS[DOWN_Z], BF16), B(BLOCKS[DOWN_Z], BF16)]
    scratch += [B((5, 16, W), F32), B((5, 16, W), F32)]
    scratch += [B((192, 384), F32), B(BLOCKS[UP], F32), B(BLOCKS[QKV], F32), B((16, W), F32)]
    scratch += [dma((20,)), dma((4,)), dma((4,)), dma((24,)), dma((24,)), dma((4,)), dma((4,))]
    scratch += [dma((3, 4))] * 6 + [dma((5,)), dma((5,)), dma((5,)), dma((5,)), dma((9,))] + [B((W,), F32)] * 8 + [B((4 * W,), F32)]
    results = pl.pallas_call(
        layer_kernel,
        name="layer",
        out_shape=(
            jax.ShapeDtypeStruct(tokens.shape, BF16),
            jax.ShapeDtypeStruct(tokens.shape, BF16),
            jax.ShapeDtypeStruct((192, 384), F32),
            jax.ShapeDtypeStruct(BLOCKS[UP], F32),
            jax.ShapeDtypeStruct(BLOCKS[QKV], F32),
            jax.ShapeDtypeStruct((16, W), F32),
        ),
        in_specs=[hbm, pl.BlockSpec(memory_space=pltpu.SMEM)] + [hbm] * 14,
        out_specs=(hbm,) * 6,
        scratch_shapes=scratch,
        compiler_params=pltpu.CompilerParams(
            collective_id=1, has_side_effects=True, vmem_limit_bytes=63 * 1024 * 1024
        ),
    )(
        tokens, lengths, cotangent, w_qkv, w_out, w_up, w_down,
        b_query, b_value, b_out, first_gain, first_shift, b_up, b_down, second_gain, second_shift,
    )
    return finish(*results)


def solution(mesh):
    in_specs = (
        P("dp", "seq", None),
        P("dp", None),
        P("dp", "seq", None),
        P(),
        P(),
        P(),
        P(),
        P(),
        P(),
        P(),
        P(),
        P(),
        P(),
        P(),
        P(),
        P(),
    )
    out_specs = (
        P("dp", "seq", None),
        P("dp", "seq", None),
        P("dp", "seq"),
        P("dp", "seq"),
        P("dp", "seq"),
        P("dp", "seq"),
        P(),
        P(),
        P(),
        P(),
        P(),
        P(),
        P(),
        P(),
        P(),
    )
    return jax.shard_map(
        local if dict(mesh.shape) == {"dp": 8, "seq": 4} else local_any, mesh=mesh, in_specs=in_specs, out_specs=out_specs, check_vma=False)
```

```python
import functools

import jax
import jax.numpy as jnp
from jax import lax
from jax.experimental import pallas as pl
from jax.experimental.pallas import tpu as pltpu
from jax.sharding import PartitionSpec as P

MESH_ID = pl.DeviceIdType.MESH
BF16 = jnp.bfloat16
F32 = jnp.float32

HEAD_DIM = 64


EPSILON = 1e-05
ROOT_HALF = 0.7071067811865476
INV_ROOT_TWO_PI = 0.3989422804014327


def contract_rows(left, right):
    return lax.dot_general(
        left, right, (((0,), (0,)), ((), ())), preferred_element_type=jnp.float32
    )


def times_transposed(left, weight_matrix):
    return lax.dot_general(
        left, weight_matrix, (((1,), (1,)), ((), ())), preferred_element_type=jnp.float32
    )


def normalize(value_rows):
    center = value_rows - jnp.mean(value_rows, axis=-1, keepdims=True)
    inverse_root = lax.rsqrt(jnp.mean(center * center, axis=-1, keepdims=True) + EPSILON)
    return (center * inverse_root, inverse_root)


def norm_backward(grad_out, normed, inverse_root, gain):
    scaled = grad_out * gain
    return inverse_root * (
        scaled
        - jnp.mean(scaled, axis=-1, keepdims=True)
        - normed * jnp.mean(scaled * normed, axis=-1, keepdims=True)
    )


def attention_forward_pass(inputs):
    queries, key_block, value_block, key_valid = inputs
    head_scale = queries.shape[-1] ** (-0.5)
    scores = (
        jnp.einsum("qhd,khd->hqk", queries, key_block, preferred_element_type=jnp.float32)
        * head_scale
    )
    scores = jnp.where(key_valid[None, None, :], scores, -1e30)
    highest = jnp.max(scores, axis=-1, keepdims=True)
    exponent = jnp.exp(scores - highest)
    row_total = jnp.sum(exponent, axis=-1, keepdims=True)
    weight_tensors = (exponent / row_total).astype(jnp.bfloat16)
    context = jnp.einsum(
        "hqk,khd->qhd", weight_tensors, value_block, preferred_element_type=jnp.float32
    )
    return (context.astype(jnp.bfloat16), (highest + jnp.log(row_total))[..., 0])


def attend_backward(inputs):
    queries, key_block, value_block, key_valid, log_total, grad_context = inputs
    head_scale = queries.shape[-1] ** (-0.5)
    scores = (
        jnp.einsum("qhd,khd->hqk", queries, key_block, preferred_element_type=jnp.float32)
        * head_scale
    )
    scores = jnp.where(key_valid[None, None, :], scores, -1e30)
    probs = jnp.exp(scores - log_total[..., None])
    grad_probs = jnp.einsum(
        "qhd,khd->hqk", grad_context, value_block, preferred_element_type=jnp.float32
    )
    row_inner = jnp.sum(probs * grad_probs, axis=-1, keepdims=True)
    grad_scores = (probs * (grad_probs - row_inner)).astype(jnp.bfloat16)
    probs_low = probs.astype(jnp.bfloat16)
    grad_queries = (
        jnp.einsum("hqk,khd->qhd", grad_scores, key_block, preferred_element_type=jnp.float32)
        * head_scale
    )
    grad_keys = (
        jnp.einsum("hqk,qhd->khd", grad_scores, queries, preferred_element_type=jnp.float32)
        * head_scale
    )
    grad_values = jnp.einsum(
        "hqk,qhd->khd", probs_low, grad_context, preferred_element_type=jnp.float32
    )
    return jnp.stack([grad_queries, grad_keys, grad_values], axis=1).astype(jnp.bfloat16)


def local_any(
    tokens,
    lengths,
    cotangent,
    w_qkv,
    b_query,
    b_value,
    w_out,
    b_out,
    first_gain,
    first_shift,
    w_up,
    b_up,
    w_down,
    b_down,
    second_gain,
    second_shift,
):
    lane_count = lax.axis_size("seq")
    seq_count, part_len, model_width = tokens.shape
    full_len = part_len * lane_count
    lane_width = model_width // lane_count
    head_size = HEAD_DIM
    heads_here = lane_width // head_size
    row_count = seq_count * part_len
    offset = lax.axis_index("seq") * part_len
    places = offset + jnp.arange(part_len, dtype=jnp.int32)
    length_row = lengths[0]
    row_live = (places[None, :] < length_row[:, None]).astype(jnp.float32).reshape(row_count, 1)
    key_valid = jnp.arange(full_len, dtype=jnp.int32)[None, :] < length_row[:, None]
    joined_bias = jnp.concatenate([b_query, jnp.zeros_like(b_query), b_value])
    tokens_flat = tokens.reshape(row_count, model_width)
    mixed = jnp.dot(tokens_flat, w_qkv, preferred_element_type=jnp.float32) + joined_bias
    qkv_heads = lax.all_to_all(
        mixed.astype(jnp.bfloat16).reshape(seq_count, part_len, 3, lane_count, lane_width),
        "seq",
        split_axis=3,
        concat_axis=1,
        tiled=True,
    )
    qkv_heads = qkv_heads.reshape(seq_count, full_len, 3, heads_here, head_size)
    context_heads, log_total = lax.map(
        attention_forward_pass,
        (qkv_heads[:, :, 0], qkv_heads[:, :, 1], qkv_heads[:, :, 2], key_valid),
    )
    context_heads = context_heads.reshape(seq_count, full_len, 1, lane_width)
    context_token_rows = lax.all_to_all(
        context_heads, "seq", split_axis=1, concat_axis=2, tiled=True
    ).reshape(row_count, model_width)
    branch = jnp.dot(context_token_rows, w_out, preferred_element_type=jnp.float32) + b_out
    normed_one, inverse_one = normalize(tokens_flat.astype(jnp.float32) + branch)
    hidden = normed_one * first_gain + first_shift
    hidden_low = hidden.astype(jnp.bfloat16)
    preactivation_input = jnp.dot(hidden_low, w_up, preferred_element_type=jnp.float32) + b_up
    active = jax.nn.gelu(preactivation_input, approximate=False).astype(jnp.bfloat16)
    ffn_out = jnp.dot(active, w_down, preferred_element_type=jnp.float32) + b_down
    normed_two, inverse_two = normalize(hidden + ffn_out)
    output_rows = (normed_two * second_gain + second_shift) * row_live
    output_tokens = output_rows.astype(jnp.bfloat16).reshape(seq_count, part_len, model_width)
    grad_out = cotangent.reshape(row_count, model_width).astype(jnp.float32) * row_live
    grad_second_gain = jnp.sum(grad_out * normed_two, axis=0)
    grad_second_shift = jnp.sum(grad_out, axis=0)
    d_sum_two = norm_backward(grad_out, normed_two, inverse_two, second_gain)
    d_ffn = d_sum_two.astype(jnp.bfloat16)
    grad_b_down = jnp.sum(d_ffn.astype(jnp.float32), axis=0)
    grad_w_down = contract_rows(active, d_ffn)
    d_active = times_transposed(d_ffn, w_down)
    gelu_slope = (
        0.5 * (1.0 + lax.erf(preactivation_input * ROOT_HALF))
        + preactivation_input
        * jnp.exp(-0.5 * preactivation_input * preactivation_input)
        * INV_ROOT_TWO_PI
    )
    d_pre = (d_active * gelu_slope).astype(jnp.bfloat16)
    grad_b_up = jnp.sum(d_pre.astype(jnp.float32), axis=0)
    grad_w_up = contract_rows(hidden_low, d_pre)
    d_hidden = d_sum_two + times_transposed(d_pre, w_up)
    grad_first_gain = jnp.sum(d_hidden * normed_one, axis=0)
    grad_first_shift = jnp.sum(d_hidden, axis=0)
    d_sum_one = norm_backward(d_hidden, normed_one, inverse_one, first_gain)
    d_branch = d_sum_one.astype(jnp.bfloat16)
    grad_b_out = jnp.sum(d_branch.astype(jnp.float32), axis=0)
    grad_w_out = contract_rows(context_token_rows, d_branch)
    d_context = times_transposed(d_branch, w_out).astype(jnp.bfloat16)
    d_context = d_context.reshape(seq_count, part_len, lane_count, lane_width)
    d_context_heads = lax.all_to_all(d_context, "seq", split_axis=2, concat_axis=1, tiled=True)
    d_context_heads = d_context_heads.reshape(seq_count, full_len, heads_here, head_size)
    d_qkv_heads = lax.map(
        attend_backward,
        (
            qkv_heads[:, :, 0],
            qkv_heads[:, :, 1],
            qkv_heads[:, :, 2],
            key_valid,
            log_total,
            d_context_heads,
        ),
    )
    d_qkv_heads = d_qkv_heads.reshape(seq_count, full_len, 3, 1, lane_width)
    d_qkv = lax.all_to_all(d_qkv_heads, "seq", split_axis=1, concat_axis=3, tiled=True).reshape(
        row_count, 3 * model_width
    )
    d_qkv_wide = d_qkv.astype(jnp.float32)
    grad_b_query = jnp.sum(d_qkv_wide[:, :model_width], axis=0)
    grad_b_value = jnp.sum(d_qkv_wide[:, 2 * model_width :], axis=0)
    grad_w_qkv = contract_rows(tokens_flat, d_qkv)
    grad_rows = d_sum_one + times_transposed(d_qkv, w_qkv)
    grad_tokens = grad_rows.astype(jnp.bfloat16).reshape(seq_count, part_len, model_width)
    matrices = (grad_w_qkv, grad_w_out, grad_w_up, grad_w_down)
    halfway = (
        lax.psum_scatter(matrices[0], "dp", scatter_dimension=0, tiled=True),
        lax.psum_scatter(matrices[1], "dp", scatter_dimension=0, tiled=True),
        lax.psum_scatter(matrices[2], "dp", scatter_dimension=0, tiled=True),
        lax.psum_scatter(matrices[3], "dp", scatter_dimension=0, tiled=True),
    )
    matrices = (
        lax.psum_scatter(
            halfway[0].astype(jnp.bfloat16), "seq", scatter_dimension=1, tiled=True
        ).astype(jnp.float32),
        lax.psum_scatter(
            halfway[1].astype(jnp.bfloat16), "seq", scatter_dimension=1, tiled=True
        ).astype(jnp.float32),
        lax.psum_scatter(
            halfway[2].astype(jnp.bfloat16), "seq", scatter_dimension=1, tiled=True
        ).astype(jnp.float32),
        lax.psum_scatter(
            halfway[3].astype(jnp.bfloat16), "seq", scatter_dimension=1, tiled=True
        ).astype(jnp.float32),
    )
    vectors = lax.psum(
        (
            grad_b_query,
            grad_b_value,
            grad_b_out,
            grad_first_gain,
            grad_first_shift,
            grad_b_up,
            grad_b_down,
            grad_second_gain,
            grad_second_shift,
        ),
        ("dp", "seq"),
    )
    return (
        output_tokens,
        grad_tokens,
        matrices[0],
        matrices[1],
        matrices[2],
        matrices[3],
        vectors[0],
        vectors[1],
        vectors[2],
        vectors[3],
        vectors[4],
        vectors[5],
        vectors[6],
        vectors[7],
        vectors[8],
    )


DOWN, UP, QKV, DOWN_Z = 0, 1, 2, 3
SPLIT = 48
BLOCKS = ((SPLIT, 384), (96, 768), (96, 768), (192 - SPLIT, 384))
PLAN = (
    ((0, 0, 3), (0, 0, 2), (0, 0, 1), (0, 0, 0),),
    (),
    (),
    ((0, 1, 3), (0, 1, 2),),
    ((0, 1, 1), (0, 1, 0), (1, 0, 3), (1, 0, 0), (1, 0, 2),),
    ((1, 0, 1),),
    ((1, 3, 0),),
    ((1, 1, 2),),
    (),
    (),
    ((1, 1, 3),),
    ((0, 2, 3), (0, 2, 2), (1, 1, 0), (2, 0, 3),),
    ((1, 1, 1), (2, 0, 1), (2, 0, 0),),
    ((2, 1, 3), (2, 3, 0),),
    ((0, 2, 1), (2, 0, 2), (1, 2, 2),),
    ((1, 2, 3), (0, 2, 0), (2, 1, 2), (2, 1, 1), (2, 1, 0), (5, 1, 0), (3, 3, 0), (1, 2, 1), (2, 2, 3), (5, 0, 0), (2, 2, 2), (2, 2, 1), (1, 2, 0), (4, 3, 0),),
    ((2, 2, 0),),
)
X_FIRST = {(0, 0), (0, 1), (1, 0), (1, 2), (2, 2)}
ORDER_D = (3, 2, 1, 0)

B_QUERY, B_VALUE, B_OUT, FIRST_GAIN, FIRST_SHIFT, B_DOWN, SECOND_GAIN, SECOND_SHIFT, B_UP = range(9)

ROWS = 256
TILE = 256
PART = 128
WIDTH = 768
STEP = 128


def place():
    row, lane = lax.axis_index("dp"), lax.axis_index("seq")
    return row // 2, row % 2, lane // 2, lane % 2


def device(z, y, x, core):
    return (z * 2 + y, x * 2 + core)


def remote(source, target, send, receive, where):
    return pltpu.make_async_remote_copy(
        src_ref=source,
        dst_ref=target,
        send_sem=send,
        recv_sem=receive,
        device_id=where,
        device_id_type=MESH_ID,
    )


def dot(left, right):
    return jnp.dot(left, right, preferred_element_type=F32)


def dot_t(left, right):
    return lax.dot_general(left, right, (((1,), (1,)), ((), ())), preferred_element_type=F32)


def fold(rows):
    return jnp.sum(rows.reshape(rows.shape[0] // 8, 8, rows.shape[1]), axis=0)


def mean(rows):
    return jnp.sum(rows, axis=-1, keepdims=True) * (1.0 / WIDTH)


def layer_kernel(
    tokens_in, lengths_in, cot_in, w_qkv_in, w_out_in, w_up_in, w_down_in,
    b_query_in, b_value_in, b_out_in, first_gain_in, first_shift_in, b_up_in, b_down_in, second_gain_in, second_shift_in,
    tokens_out, grad_out, down_hbm, up_hbm, qkv_hbm, vec_hbm,
    w_qkv, w_out, w_up, w_down, par, tok, cot, q3, k3, v3, bias, probs, hidden, xhat, rstd, low, d_ffn, slope, wide, total, held, turned, inverse, d_scores,
    dsum, dctx3, dkv_own, dkv_send, dkv_in, dq_t, dqkv_flat, out_rows, grad_rows,
    act, dpre, dffn_t, hid_t, tok_t, ctx_t, dqkv, dbr,
    sums_0, sums_1, sums_2, sums_z, in1_0, in1_1, in1_2, in2_0, in2_1, in2_2, in3_0, in3_1, in3_2, in1_z, in2_z, in3_z,
    vec_mine, vec_in, down_out, up_out, qkv_out, vec_out,
    load, ex_send, ex_recv, core_send, core_recv, act_send, act_recv,
    send1, recv1, send2, recv2, send3, recv3, send_z, recv_z, vec_send, vec_recv, vec_load,
    held_0, held_1, held_2, held_3, held_4, held_5, held_6, held_7, held_8,
):
    z, y, x, core = place()
    sums, in1, in2, in3 = (sums_0, sums_1, sums_2), (in1_0, in1_1, in1_2), (in2_0, in2_1, in2_2), (in3_0, in3_1, in3_2)
    at_core = device(z, y, x, 1 - core)
    at_x = device(z, y, 1 - x, core)
    at_y = device(z, 1 - y, x, core)
    at_place = [z, z + 1 - 2 * (z % 2), (z + 2) % 4, 3 - z]
    at_z1 = device(at_place[1], y, x, core)
    at_z2 = device(at_place[2], y, x, core)

    loads = [pltpu.make_async_copy(tokens_in.at[x], tok.at[pl.ds(0, PART)], load.at[0])]
    for n, s in enumerate((1, 2, 0)):
        loads.append(
            pltpu.make_async_copy(
                w_qkv_in.at[:, pl.ds(WIDTH * s, WIDTH)], w_qkv.at[:, pl.ds(WIDTH * s, WIDTH)], load.at[1 + n]
            )
        )
    loads.append(pltpu.make_async_copy(cot_in.at[x], cot.at[pl.ds(0, PART)], load.at[4]))
    loads.append(pltpu.make_async_copy(w_out_in, w_out, load.at[5]))
    for t in range(4):
        loads.append(pltpu.make_async_copy(w_up_in.at[:, pl.ds(WIDTH * t, WIDTH)], w_up.at[t], load.at[6 + t]))
    for t in range(4):
        loads.append(pltpu.make_async_copy(w_down_in.at[pl.ds(WIDTH * t, WIDTH)], w_down.at[t], load.at[10 + t]))
    for copy in loads[0:4]:
        copy.start()

    vec_refs = {
        B_QUERY: (b_query_in, held_0), B_VALUE: (b_value_in, held_1), B_OUT: (b_out_in, held_2), FIRST_GAIN: (first_gain_in, held_3),
        FIRST_SHIFT: (first_shift_in, held_4), B_DOWN: (b_down_in, held_5), SECOND_GAIN: (second_gain_in, held_6),
        SECOND_SHIFT: (second_shift_in, held_7), B_UP: (b_up_in, held_8),
    }
    vec_loads = [
        pltpu.make_async_copy(source, vector, vec_load.at[n]) for n, (source, vector) in enumerate(vec_refs.values())
    ]
    for copy in vec_loads:
        copy.start()

    barrier = pltpu.get_barrier_semaphore()
    for where in (at_core, at_x, at_y, at_z1, at_z2):
        pl.semaphore_signal(barrier, inc=1, device_id=where, device_id_type=MESH_ID)
    pl.semaphore_wait(barrier, 5)

    get_tok = remote(tokens_in.at[1 - x], tok.at[pl.ds(PART, PART)], ex_send.at[0], ex_recv.at[0], at_x)
    get_cot = remote(cot_in.at[1 - x], cot.at[pl.ds(PART, PART)], ex_send.at[1], ex_recv.at[1], at_x)
    get_tok.start()

    core_copies = []

    def to_core(source, target):
        n = len(core_copies)
        copy = remote(source, target, core_send.at[n], core_recv.at[n], at_core)
        copy.start()
        core_copies.append(copy)
        return copy

    for copy in vec_loads:
        copy.wait()
    for row, (_, vector) in vec_refs.items():
        if row == B_UP:
            for t in range(4):
                par[B_UP + t : B_UP + t + 1, :] = vector[WIDTH * t : WIDTH * (t + 1)].reshape(1, WIDTH)
        else:
            par[row : row + 1, :] = vector[...].reshape(1, WIDTH)
    vec_mine[0] = jnp.zeros((16, WIDTH), F32)
    length = lengths_in[0, x]
    mine, across = 2 * x + core, 2 * (1 - x) + core
    theirs, theirs_across = 2 * x + 1 - core, 2 * (1 - x) + 1 - core

    def positions(shape, starts):
        n = lax.broadcasted_iota(jnp.int32, shape, 0)
        first = starts[-1] * PART
        for b in range(len(starts) - 2, -1, -1):
            first = jnp.where(n < PART * (b + 1), starts[b] * PART, first)
        return first + n % PART

    bias[...] = jnp.where(positions((512, ROWS), (mine, across, theirs, theirs_across)) < length, 0.0, -1e30)

    kv_copies = []
    for b in range(2):
        rows = slice(PART * b, PART * (b + 1))
        if b == 0:
            loads[0].wait()
        else:
            get_tok.wait_recv()
            get_cot.start()
            for copy in loads[4:14]:
                copy.start()
        for n, s in enumerate((1, 2, 0)):
            if b == 0:
                loads[1 + n].wait()
            part = dot(tok[rows, :], w_qkv[:, WIDTH * s : WIDTH * (s + 1)])
            if s == 0:
                part = part + par[B_QUERY : B_QUERY + 1, :]
            if s == 2:
                part = part + par[B_VALUE : B_VALUE + 1, :]
            part = part.astype(BF16)
            if s == 0:
                part = part * jnp.asarray(0.125, BF16)
            heads = (q3, k3, v3)[s]
            for j in range(6):
                heads[j, rows, :] = part[:, 128 * j : 128 * (j + 1)]
            if s:
                kv_copies.append(
                    to_core(heads.at[:, pl.ds(PART * b, PART)], heads.at[:, pl.ds(ROWS + PART * b, PART)])
                )
    tok_t[:, 0:ROWS] = tok[...].T
    qkv_copies = [to_core(tok_t.at[:, pl.ds(0, ROWS)], tok_t.at[:, pl.ds(ROWS, ROWS)])]
    for copy in kv_copies:
        copy.wait_recv()

    low_half = lax.broadcasted_iota(jnp.int32, (ROWS, 128), 1) < 64

    def half_of(pair, h):
        zeros = jnp.zeros_like(pair)
        return jnp.where(low_half, pair, zeros) if h == 0 else jnp.where(low_half, zeros, pair)

    for j in range(6):
        turned[j] = v3[j].T
    highest = {}

    def score(n):
        queries = half_of(q3[n // 2], n % 2)
        top = None
        for t in range(0, 512, TILE):
            scores = dot_t(k3[n // 2, t : t + TILE], queries) + bias[t : t + TILE, :]
            held[n % 2, t : t + TILE, :] = scores
            part = jnp.max(scores.reshape(TILE // 8, 8, ROWS), axis=0)
            top = part if top is None else jnp.maximum(top, part)
        highest[n] = jnp.max(top, axis=0, keepdims=True)

    def weigh(n):
        sums = None
        for t in range(0, 512, TILE):
            exponent = jnp.exp(held[n % 2, t : t + TILE, :] - highest[n])
            part = fold(exponent)
            sums = part if sums is None else sums + part
            probs[n, t : t + TILE, :] = exponent.astype(BF16)
        inverse[n : n + 1, :] = 1.0 / jnp.sum(sums, axis=0, keepdims=True)

    def gather(n):
        context = dot(turned[n // 2, 64 * (n % 2) : 64 * (n % 2 + 1)], probs[n]) * inverse[n : n + 1, :]
        ctx_t[64 * n : 64 * (n + 1), 0:ROWS] = context.astype(BF16)

    score(0)
    for n in range(12):
        if n < 11:
            score(n + 1)
        weigh(n)
        if n:
            gather(n - 1)
    gather(11)
    qkv_copies.append(to_core(ctx_t.at[:, pl.ds(0, ROWS)], ctx_t.at[:, pl.ds(ROWS, ROWS)]))

    loads[5].wait()
    wide[...] = dot(ctx_t[:, 0:ROWS].T, w_out[...])

    def first_norm(r, _):
        rows = pl.ds(pl.multiple_of(STEP * r, STEP), STEP)
        value = tok[rows, :].astype(F32) + wide[rows, :] + par[B_OUT : B_OUT + 1, :]
        center = value - mean(value)
        root = lax.rsqrt(mean(center * center) + EPSILON)
        normed = center * root
        out = normed * par[FIRST_GAIN : FIRST_GAIN + 1, :] + par[FIRST_SHIFT : FIRST_SHIFT + 1, :]
        xhat[rows, :] = normed
        rstd[rows, :] = root
        hidden[rows, :] = out
        low[rows, :] = out.astype(BF16)
        return 0

    lax.fori_loop(0, ROWS // STEP, first_norm, 0)
    up_copies = []

    for n in range(6, 14):
        loads[n].wait()

    def act_copy(t):
        return remote(act.at[t, pl.ds(0, ROWS)], act.at[t, pl.ds(ROWS, ROWS)], act_send.at[t], act_recv.at[t], at_core)

    for t in range(4):
        u = dot(low[...], w_up[t]) + par[B_UP + t : B_UP + t + 1, :]
        phi = 0.5 * (1.0 + lax.erf(u * ROOT_HALF))
        active = (u * phi).astype(BF16)
        act[t, 0:ROWS, :] = active
        slope[t] = phi + u * jnp.exp(-0.5 * u * u) * INV_ROOT_TWO_PI
        act_copy(t).start()
        product = dot(active, w_down[t])
        total[...] = total[...] + product if t else product

    loads[4].wait()
    get_cot.wait_recv()

    def live_rows(r):
        n = lax.broadcasted_iota(jnp.int32, (STEP, 1), 0) + STEP * r
        return jnp.where(jnp.where(n < PART, mine * PART + n, across * PART + n - PART) < length, 1.0, 0.0)

    def second_norm(r, _):
        rows = pl.ds(pl.multiple_of(STEP * r, STEP), STEP)
        value = hidden[rows, :] + (total[rows, :] + par[B_DOWN : B_DOWN + 1, :])
        center = value - mean(value)
        root = lax.rsqrt(mean(center * center) + EPSILON)
        normed = center * root
        wide[rows, :] = normed
        e = cot[rows, :].astype(F32) * live_rows(r) * par[SECOND_GAIN : SECOND_GAIN + 1, :]
        d = root * (e - mean(e) - normed * mean(e * normed))
        dsum[rows, :] = d
        d_ffn[rows, :] = d.astype(BF16)
        return 0

    lax.fori_loop(0, ROWS // STEP, second_norm, 0)

    def second_norm_rest(r, carry):
        rows = pl.ds(pl.multiple_of(STEP * r, STEP), STEP)
        live, normed = live_rows(r), wide[rows, :]
        out = (normed * par[SECOND_GAIN : SECOND_GAIN + 1, :] + par[SECOND_SHIFT : SECOND_SHIFT + 1, :]) * live
        out_rows[rows, :] = out.astype(BF16)
        grad = cot[rows, :].astype(F32) * live
        gain, shift, down = carry
        return gain + fold(grad * normed), shift + fold(grad), down + fold(d_ffn[rows, :].astype(F32))

    zero = jnp.zeros((8, WIDTH), F32)

    def put(row, partial):
        vec_mine[0, row : row + 1, :] = jnp.sum(partial, axis=0, keepdims=True)

    out_local = pltpu.make_async_copy(out_rows.at[pl.ds(0, PART)], tokens_out.at[x], load.at[14])
    out_across = remote(out_rows.at[pl.ds(PART, PART)], tokens_out.at[x], ex_send.at[2], ex_recv.at[2], at_x)
    dffn_all = d_ffn[...].T
    for j in range(4):
        dffn_t[j, :, 0:ROWS] = dffn_all[192 * j : 192 * (j + 1), :]
    down_copies = []
    for j in (0, 2):
        there = j + 1 - core
        down_copies.append(to_core(dffn_t.at[there, :, pl.ds(0, ROWS)], dffn_t.at[there, :, pl.ds(ROWS, ROWS)]))

    def first(m, k):
        zk = at_place[k]
        if (m, k) in X_FIRST:
            return remote(sums[m].at[1 - x, zk], in1[m].at[zk], send1.at[m, k], recv1.at[m, k], at_x)
        return remote(sums[m].at[:, zk, 1 - y], in1[m].at[zk], send1.at[m, k], recv1.at[m, k], at_y)

    def second(m, k):
        zk = at_place[k]
        if (m, k) in X_FIRST:
            return remote(sums[m].at[x, zk, 1 - y], in2[m].at[zk], send2.at[m, k], recv2.at[m, k], at_y)
        return remote(sums[m].at[1 - x, zk, y], in2[m].at[zk], send2.at[m, k], recv2.at[m, k], at_x)

    def third(m, k):
        zk = at_place[k]
        slot, where = ((0, at_z1), (2, at_z2), (1, at_z1))[k - 1]
        return remote(sums[m].at[x, zk, y], in3[m].at[slot], send3.at[m, k], recv3.at[m, k], where)

    def add_first(m, k):
        zk = at_place[k]
        if (m, k) in X_FIRST:
            sums[m][x, zk] = sums[m][x, zk] + in1[m][zk]
        else:
            for b in range(2):
                sums[m][b, zk, y] = sums[m][b, zk, y] + in1[m][zk, b]

    def add_second(m, k):
        zk = at_place[k]
        block = sums[m][x, zk, y] + in2[m][zk]
        if k == 2:
            third(m, 3).wait_recv()
            block = block + in3[m][1]
        sums[m][x, zk, y] = block

    z_near = [
        remote(sums_z.at[:, at_place[k]], in1_z.at[n], send_z.at[n], recv_z.at[n], at_z1) for n, k in enumerate((1, 3))
    ]
    z_far = remote(sums_z.at[:, at_place[2]], in1_z.at[2], send_z.at[2], recv_z.at[2], at_z2)
    z_second = remote(sums_z.at[1 - x, z], in2_z, send_z.at[3], recv_z.at[3], at_x)
    z_third = remote(sums_z.at[x, z, 1 - y], in3_z, send_z.at[4], recv_z.at[4], at_y)

    def at_z_first(step):
        if step == 1:
            z_near[1].wait_recv()
            for b in range(2):
                sums_z[b, at_place[2]] = sums_z[b, at_place[2]] + in1_z[1, b]
            z_far.start()
        elif step == 2:
            z_near[0].wait_recv()
            z_far.wait_recv()
            for b in range(2):
                sums_z[b, z] = (sums_z[b, z].astype(F32) + in1_z[0, b].astype(F32) + in1_z[2, b].astype(F32)).astype(BF16)
            z_second.start()
        elif step == 3:
            z_second.wait_recv()
            sums_z[x, z] = sums_z[x, z] + in2_z[...]
            z_third.start()
        else:
            z_third.wait_recv()
            down_out[SPLIT:192, :] = sums_z[x, z, y].astype(F32) + in3_z[...].astype(F32)

    def at(point):
        for step, m, k in PLAN[point]:
            if step == 5:
                (out_across, grad_across)[m].start()
                continue
            if m == DOWN_Z:
                at_z_first(step)
                continue
            if step == 0:
                first(m, k).start()
            elif step == 1:
                first(m, k).wait_recv()
                add_first(m, k)
                second(m, k).start()
            else:
                second(m, k).wait_recv()
                add_second(m, k)
                if k:
                    third(m, k).start()

    before = [dsum]

    def feed_back(t):
        d_pre = (dot_t(d_ffn[...], w_down[t]) * slope[t]).astype(BF16)
        dpre[t, 0:ROWS, :] = d_pre
        vec_mine[0, pl.ds(B_UP + t, 1), :] = jnp.sum(fold(d_pre.astype(F32)), axis=0, keepdims=True)
        total[...] = before[-1][...] + dot_t(d_pre, w_up[t])
        before.append(total)

    for j in (0, 2):
        there = j + 1 - core
        feed_back(there)
        up_copies.append(to_core(dpre.at[there, pl.ds(0, ROWS)], dpre.at[there, pl.ds(ROWS, ROWS)]))

    for t in range(4):
        act_copy(t).wait_recv()
    for copy in down_copies:
        copy.wait_recv()
    left = jnp.concatenate([dffn_t[core], dffn_t[2 + core]], axis=0)
    for k in ORDER_D:
        t = at_place[k]
        part = dot(left, act[t]).astype(BF16)
        for b in range(2):
            for h in range(2):
                sums_0[b, t, h] = part[192 * b : 192 * b + SPLIT, 384 * h : 384 * (h + 1)]
                sums_z[b, t, h] = part[192 * b + SPLIT : 192 * (b + 1), 384 * h : 384 * (h + 1)]
        if k % 2:
            z_near[k // 2].start()
        if (0, DOWN, k) in PLAN[0]:
            first(DOWN, k).start()
    hid_t[:, 0:ROWS] = low[...].T
    up_copies.append(to_core(hid_t.at[:, pl.ds(0, ROWS)], hid_t.at[:, pl.ds(ROWS, ROWS)]))
    for n, j in enumerate((0, 2)):
        feed_back(j + core)
        at(1 + n)
    for copy in up_copies:
        copy.wait_recv()
    for b in range(2):
        for n in range(3):
            part = dot(hid_t[...], dpre[2 * b + core, :, 256 * n : 256 * (n + 1)]).astype(BF16)
            sums_1[b, :, :, :, 256 * n : 256 * (n + 1)] = part.reshape(4, 2, 96, 256)
    at(3)
    gain, shift, down = lax.fori_loop(0, ROWS // STEP, second_norm_rest, (zero, zero, zero))
    put(SECOND_GAIN, gain)
    put(SECOND_SHIFT, shift)
    put(B_DOWN, down)
    out_local.start()

    def first_norm_back(r, carry):
        rows = pl.ds(pl.multiple_of(STEP * r, STEP), STEP)
        d_hidden, normed = total[rows, :], xhat[rows, :]
        e = d_hidden * par[FIRST_GAIN : FIRST_GAIN + 1, :]
        d = rstd[rows, :] * (e - mean(e) - normed * mean(e * normed))
        dsum[rows, :] = d
        d_low = d.astype(BF16)
        low[rows, :] = d_low
        gain, shift, out = carry
        return gain + fold(d_hidden * normed), shift + fold(d_hidden), out + fold(d_low.astype(F32))

    gain, shift, out = lax.fori_loop(0, ROWS // STEP, first_norm_back, (zero, zero, zero))
    put(FIRST_GAIN, gain)
    put(FIRST_SHIFT, shift)
    put(B_OUT, out)
    for j in range(4):
        dbr[j, 0:ROWS, :] = jnp.concatenate([jnp.zeros((ROWS, 64), BF16), low[:, 192 * j : 192 * (j + 1)]], axis=1)
    for j in (0, 2):
        there = j + 1 - core
        qkv_copies.append(to_core(dbr.at[there, pl.ds(0, ROWS)], dbr.at[there, pl.ds(ROWS, ROWS)]))
    d_context = dot_t(low[...], w_out[...]).astype(BF16)
    for j in range(6):
        dctx3[j] = d_context[:, 128 * j : 128 * (j + 1)]

    at(4)

    for j in range(6):
        turned[j] = k3[j].T
    inverse_t = inverse[...].T
    inner, d_heads, partial_values, partial_keys = {}, {}, {}, {}

    def probs_back(n):
        d_head = (half_of(dctx3[n // 2], n % 2).astype(F32) * inverse_t[:, n : n + 1]).astype(BF16)
        sums = None
        for t in range(0, 512, TILE):
            d_probs = dot_t(v3[n // 2, t : t + TILE], d_head)
            held[n % 2, t : t + TILE, :] = d_probs
            part = fold(probs[n, t : t + TILE, :].astype(F32) * d_probs)
            sums = part if sums is None else sums + part
        inner[n] = jnp.sum(sums, axis=0, keepdims=True) * inverse[n : n + 1, :]
        partial_values[n] = dot(probs[n], d_head)

    def scores_back(n):
        for t in range(0, 512, TILE):
            d = probs[n, t : t + TILE, :].astype(F32) * (held[n % 2, t : t + TILE, :] - inner[n])
            d_scores[n % 2, t : t + TILE, :] = d.astype(BF16)

    def keys_back(n):
        j, h = n // 2, n % 2
        d_queries = dot(turned[j, 64 * h : 64 * (h + 1)], d_scores[h]) * 0.125
        dq_t[64 * n : 64 * (n + 1), :] = d_queries.astype(BF16)
        partial_keys[n] = dot(d_scores[h], half_of(q3[j], h))
        if h:
            for s, partial in enumerate((partial_keys, partial_values)):
                total_pair = partial[n - 1] + partial[n]
                dkv_own[s, j] = total_pair[0:ROWS]
                dkv_send[s, j] = total_pair[ROWS:].astype(BF16)

    def attend_back(start, stop):
        probs_back(start)
        for n in range(start, stop):
            if n < stop - 1:
                probs_back(n + 1)
            scores_back(n)
            if n > start:
                keys_back(n - 1)
        keys_back(stop - 1)

    attend_back(0, 6)
    back_copies = [to_core(dkv_send.at[:, pl.ds(0, 3)], dkv_in.at[:, pl.ds(0, 3)])]
    at(5)
    attend_back(6, 12)
    back_copies.append(to_core(dkv_send.at[:, pl.ds(3, 3)], dkv_in.at[:, pl.ds(3, 3)]))
    at(6)
    d_queries = dq_t[...].T
    dqkv_flat[:, 0:WIDTH] = d_queries
    put(B_QUERY, fold(d_queries.astype(F32)))
    at(7)
    for copy in back_copies:
        copy.wait_recv()
    at(8)
    for j in range(6):
        for s in range(2):
            d = (dkv_own[s, j] + dkv_in[s, j].astype(F32)).astype(BF16)
            dqkv_flat[:, WIDTH * (1 + s) + 128 * j : WIDTH * (1 + s) + 128 * (j + 1)] = d
            if s:
                vec_mine[0, B_VALUE : B_VALUE + 1, 128 * j : 128 * (j + 1)] = jnp.sum(d.astype(F32), axis=0, keepdims=True)
    for j in range(4):
        dqkv[j, 0:ROWS, :] = jnp.concatenate(
            [dqkv_flat[:, 576 * j : 576 * (j + 1)], jnp.zeros((ROWS, 64), BF16)], axis=1
        )
    for j in (0, 2):
        there = j + 1 - core
        qkv_copies.append(to_core(dqkv.at[there, pl.ds(0, ROWS)], dqkv.at[there, pl.ds(ROWS, ROWS)]))
    vec_steps = [
        remote(vec_mine.at[s], vec_in.at[s], vec_send.at[s], vec_recv.at[s], w)
        for s, w in enumerate((at_core, at_x, at_y, at_z1, at_z2))
    ]
    vec_steps[0].start()
    at(9)

    for copy in qkv_copies:
        copy.wait_recv()
    at(10)
    for b in range(2):
        one = dot(tok_t[...], dqkv[2 * b + core])
        two = dot(ctx_t[...], dbr[2 * b + core])
        part = jnp.concatenate([one[:, 0:512], one[:, 512:640] + two[:, 0:128], two[:, 128:256]], axis=1).astype(BF16)
        sums_2[b] = part.reshape(4, 2, 96, WIDTH)
    at(11)
    vec_steps[0].wait_recv()
    vec_mine[1] = vec_mine[0] + vec_in[0]
    vec_steps[1].start()
    grad_rows[...] = (dsum[...] + dot_t(dqkv_flat[...], w_qkv[...])).astype(BF16)
    grad_local = pltpu.make_async_copy(grad_rows.at[pl.ds(0, PART)], grad_out.at[x], load.at[15])
    grad_across = remote(grad_rows.at[pl.ds(PART, PART)], grad_out.at[x], ex_send.at[3], ex_recv.at[3], at_x)
    grad_local.start()
    at(12)
    vec_steps[1].wait_recv()
    vec_mine[2] = vec_mine[1] + vec_in[1]
    vec_steps[2].start()
    at(13)
    vec_steps[2].wait_recv()
    vec_mine[3] = vec_mine[2] + vec_in[2]
    vec_steps[3].start()
    at(14)
    vec_steps[3].wait_recv()
    vec_mine[4] = vec_mine[3] + vec_in[3]
    vec_steps[4].start()
    at(15)
    vec_steps[4].wait_recv()
    vec_out[...] = vec_mine[4] + vec_in[4]
    results = [pltpu.make_async_copy(vec_out, vec_hbm, load.at[19])]
    results[0].start()

    def finish_block(m):
        out, target = ((down_out, down_hbm), (up_out, up_hbm), (qkv_out, qkv_hbm))[m]
        third(m, 1).wait_recv()
        third(m, 2).wait_recv()
        block = sums[m][x, z, y].astype(F32) + in3[m][0].astype(F32) + in3[m][2].astype(F32)
        out[0 : BLOCKS[m][0], :] = block
        results.append(pltpu.make_async_copy(out, target, load.at[16 + m]))
        results[-1].start()

    finish_block(DOWN)
    finish_block(UP)
    at(16)
    finish_block(QKV)

    out_across.wait_recv()
    grad_across.wait_recv()
    out_local.wait()
    grad_local.wait()
    for copy in results:
        copy.wait()
    for copy in [get_tok, get_cot, out_across, grad_across] + core_copies + vec_steps:
        copy.wait_send()
    for t in range(4):
        act_copy(t).wait_send()
    for copy in z_near + [z_far, z_second, z_third]:
        copy.wait_send()
    for m in (DOWN, UP, QKV):
        for k in range(4):
            first(m, k).wait_send()
            second(m, k).wait_send()
            if k:
                third(m, k).wait_send()


def finish_kernel(
    tokens_in, grad_in, down_in, up_in, joined_in, vec_in,
    tokens_out, grad_out, qkv_out, out_out, up_out, down_out,
    b_query, b_value, b_out, first_gain, first_shift, b_up, b_down, second_gain, second_shift,
    tokens, grad, down, up, joined, vec, qkv, out, vec_0, vec_1, vec_2, vec_3, vec_4, vec_5, vec_6, vec_7, vec_8, get, give,
):
    pairs = ((joined_in, joined), (vec_in, vec), (tokens_in, tokens), (grad_in, grad), (down_in, down), (up_in, up))
    gets = [pltpu.make_async_copy(source, held, get.at[n]) for n, (source, held) in enumerate(pairs)]
    for copy in gets:
        copy.start()
    gives = []

    def put(held, target):
        gives.append(pltpu.make_async_copy(held, target, give.at[len(gives)]))
        gives[-1].start()

    for n, (held, target) in ((2, (tokens, tokens_out)), (3, (grad, grad_out)), (4, (down, down_out)), (5, (up, up_out))):
        gets[n].wait()
        put(held, target)
    gets[0].wait()
    qkv[...] = joined[:, 0:576]
    put(qkv, qkv_out)
    out[...] = joined[:, 576:WIDTH]
    put(out, out_out)
    gets[1].wait()
    for row, held, target in (
        (B_QUERY, vec_0, b_query), (B_VALUE, vec_1, b_value), (B_OUT, vec_2, b_out), (FIRST_GAIN, vec_3, first_gain),
        (FIRST_SHIFT, vec_4, first_shift), (B_DOWN, vec_5, b_down), (SECOND_GAIN, vec_6, second_gain),
        (SECOND_SHIFT, vec_7, second_shift),
    ):
        held[...] = vec[row, :]
        put(held, target)
    for t in range(4):
        vec_8[WIDTH * t : WIDTH * (t + 1)] = vec[B_UP + t, :]
    put(vec_8, b_up)
    for copy in gives:
        copy.wait()


def finish(out_tokens, grad_tokens, down, up, joined, vectors):
    hbm = pl.BlockSpec(memory_space=pl.ANY)
    W = WIDTH
    shapes = [out_tokens.shape] * 2 + [(96, 576), (96, 192), up.shape, down.shape] + [(W,)] * 5 + [(4 * W,)] + [(W,)] * 3
    inputs = (out_tokens, grad_tokens, down, up, joined, vectors)
    scratch = [pltpu.VMEM(a.shape, a.dtype) for a in inputs] + [pltpu.VMEM((96, 576), F32), pltpu.VMEM((96, 192), F32)]
    scratch += [pltpu.VMEM((W,), F32)] * 8 + [pltpu.VMEM((4 * W,), F32)]
    outs = pl.pallas_call(
        finish_kernel,
        name="finish",
        out_shape=tuple(jax.ShapeDtypeStruct(s, BF16 if n < 2 else F32) for n, s in enumerate(shapes)),
        in_specs=[hbm] * 6,
        out_specs=(hbm,) * 15,
        scratch_shapes=scratch + [pltpu.SemaphoreType.DMA((6,)), pltpu.SemaphoreType.DMA((15,))],
    )(*inputs)
    return outs[:5] + (outs[5].T,) + outs[6:]


def local(
    tokens, lengths, cotangent, w_qkv, b_query, b_value, w_out, b_out, first_gain, first_shift, w_up, b_up, w_down, b_down,
    second_gain, second_shift,
):
    hbm = pl.BlockSpec(memory_space=pl.ANY)
    dma = pltpu.SemaphoreType.DMA
    B, W = pltpu.VMEM, WIDTH
    scratch = [
        B((W, 3 * W), BF16), B((W, W), BF16), B((4, W, W), BF16), B((4, W, W), BF16), B((16, W), F32),
        B((ROWS, W), BF16), B((ROWS, W), BF16),
        B((6, ROWS, 128), BF16), B((6, 512, 128), BF16), B((6, 512, 128), BF16),
        B((512, ROWS), F32), B((12, 512, ROWS), BF16),
        B((ROWS, W), F32), B((ROWS, W), F32), B((ROWS, 1), F32), B((ROWS, W), BF16), B((ROWS, W), BF16),
        B((4, ROWS, W), F32), B((ROWS, W), F32), B((ROWS, W), F32),
        B((2, 512, ROWS), F32), B((6, 128, 512), BF16), B((16, ROWS), F32), B((2, 512, ROWS), BF16), B((ROWS, W), F32),
        B((6, ROWS, 128), BF16), B((2, 6, ROWS, 128), F32), B((2, 6, ROWS, 128), BF16), B((2, 6, ROWS, 128), BF16),
        B((W, ROWS), BF16), B((ROWS, 3 * W), BF16), B((ROWS, W), BF16), B((ROWS, W), BF16),
        B((4, 512, W), BF16), B((4, 512, W), BF16), B((4, 192, 512), BF16),
        B((W, 512), BF16), B((W, 512), BF16), B((W, 512), BF16), B((4, 512, 640), BF16), B((4, 512, 256), BF16),
    ]
    scratch += [B((2, 4, 2) + block, BF16) for block in BLOCKS]
    scratch += [B((4, 2) + block, BF16) for block in BLOCKS[:DOWN_Z]]
    scratch += [B((4,) + block, BF16) for block in BLOCKS[:DOWN_Z]]
    scratch += [B((3,) + block, BF16) for block in BLOCKS[:DOWN_Z]]
    scratch += [B((3, 2, 2) + BLOCKS[DOWN_Z], BF16), B((2,) + BLOCKS[DOWN_Z], BF16), B(BLOCKS[DOWN_Z], BF16)]
    scratch += [B((5, 16, W), F32), B((5, 16, W), F32)]
    scratch += [B((192, 384), F32), B(BLOCKS[UP], F32), B(BLOCKS[QKV], F32), B((16, W), F32)]
    scratch += [dma((20,)), dma((4,)), dma((4,)), dma((24,)), dma((24,)), dma((4,)), dma((4,))]
    scratch += [dma((3, 4))] * 6 + [dma((5,)), dma((5,)), dma((5,)), dma((5,)), dma((9,))] + [B((W,), F32)] * 8 + [B((4 * W,), F32)]
    results = pl.pallas_call(
        layer_kernel,
        name="layer",
        out_shape=(
            jax.ShapeDtypeStruct(tokens.shape, BF16),
            jax.ShapeDtypeStruct(tokens.shape, BF16),
            jax.ShapeDtypeStruct((192, 384), F32),
            jax.ShapeDtypeStruct(BLOCKS[UP], F32),
            jax.ShapeDtypeStruct(BLOCKS[QKV], F32),
            jax.ShapeDtypeStruct((16, W), F32),
        ),
        in_specs=[hbm, pl.BlockSpec(memory_space=pltpu.SMEM)] + [hbm] * 14,
        out_specs=(hbm,) * 6,
        scratch_shapes=scratch,
        compiler_params=pltpu.CompilerParams(
            collective_id=1, has_side_effects=True, vmem_limit_bytes=63 * 1024 * 1024
        ),
    )(
        tokens, lengths, cotangent, w_qkv, w_out, w_up, w_down,
        b_query, b_value, b_out, first_gain, first_shift, b_up, b_down, second_gain, second_shift,
    )
    return finish(*results)


def solution(mesh):
    in_specs = (
        P("dp", "seq", None),
        P("dp", None),
        P("dp", "seq", None),
        P(),
        P(),
        P(),
        P(),
        P(),
        P(),
        P(),
        P(),
        P(),
        P(),
        P(),
        P(),
        P(),
    )
    out_specs = (
        P("dp", "seq", None),
        P("dp", "seq", None),
        P("dp", "seq"),
        P("dp", "seq"),
        P("dp", "seq"),
        P("dp", "seq"),
        P(),
        P(),
        P(),
        P(),
        P(),
        P(),
        P(),
        P(),
        P(),
    )
    return jax.shard_map(
        local if dict(mesh.shape) == {"dp": 8, "seq": 4} else local_any, mesh=mesh, in_specs=in_specs, out_specs=out_specs, check_vma=False)
```

```python
import functools

import jax
import jax.numpy as jnp
from jax import lax
from jax.experimental import pallas as pl
from jax.experimental.pallas import tpu as pltpu
from jax.sharding import PartitionSpec as P

MESH_ID = pl.DeviceIdType.MESH
BF16 = jnp.bfloat16
F32 = jnp.float32

HEAD_DIM = 64


EPSILON = 1e-05
ROOT_HALF = 0.7071067811865476
INV_ROOT_TWO_PI = 0.3989422804014327


def contract_rows(left, right):
    return lax.dot_general(
        left, right, (((0,), (0,)), ((), ())), preferred_element_type=jnp.float32
    )


def times_transposed(left, weight_matrix):
    return lax.dot_general(
        left, weight_matrix, (((1,), (1,)), ((), ())), preferred_element_type=jnp.float32
    )


def normalize(value_rows):
    center = value_rows - jnp.mean(value_rows, axis=-1, keepdims=True)
    inverse_root = lax.rsqrt(jnp.mean(center * center, axis=-1, keepdims=True) + EPSILON)
    return (center * inverse_root, inverse_root)


def norm_backward(grad_out, normed, inverse_root, gain):
    scaled = grad_out * gain
    return inverse_root * (
        scaled
        - jnp.mean(scaled, axis=-1, keepdims=True)
        - normed * jnp.mean(scaled * normed, axis=-1, keepdims=True)
    )


def attention_forward_pass(inputs):
    queries, key_block, value_block, key_valid = inputs
    head_scale = queries.shape[-1] ** (-0.5)
    scores = (
        jnp.einsum("qhd,khd->hqk", queries, key_block, preferred_element_type=jnp.float32)
        * head_scale
    )
    scores = jnp.where(key_valid[None, None, :], scores, -1e30)
    highest = jnp.max(scores, axis=-1, keepdims=True)
    exponent = jnp.exp(scores - highest)
    row_total = jnp.sum(exponent, axis=-1, keepdims=True)
    weight_tensors = (exponent / row_total).astype(jnp.bfloat16)
    context = jnp.einsum(
        "hqk,khd->qhd", weight_tensors, value_block, preferred_element_type=jnp.float32
    )
    return (context.astype(jnp.bfloat16), (highest + jnp.log(row_total))[..., 0])


def attend_backward(inputs):
    queries, key_block, value_block, key_valid, log_total, grad_context = inputs
    head_scale = queries.shape[-1] ** (-0.5)
    scores = (
        jnp.einsum("qhd,khd->hqk", queries, key_block, preferred_element_type=jnp.float32)
        * head_scale
    )
    scores = jnp.where(key_valid[None, None, :], scores, -1e30)
    probs = jnp.exp(scores - log_total[..., None])
    grad_probs = jnp.einsum(
        "qhd,khd->hqk", grad_context, value_block, preferred_element_type=jnp.float32
    )
    row_inner = jnp.sum(probs * grad_probs, axis=-1, keepdims=True)
    grad_scores = (probs * (grad_probs - row_inner)).astype(jnp.bfloat16)
    probs_low = probs.astype(jnp.bfloat16)
    grad_queries = (
        jnp.einsum("hqk,khd->qhd", grad_scores, key_block, preferred_element_type=jnp.float32)
        * head_scale
    )
    grad_keys = (
        jnp.einsum("hqk,qhd->khd", grad_scores, queries, preferred_element_type=jnp.float32)
        * head_scale
    )
    grad_values = jnp.einsum(
        "hqk,qhd->khd", probs_low, grad_context, preferred_element_type=jnp.float32
    )
    return jnp.stack([grad_queries, grad_keys, grad_values], axis=1).astype(jnp.bfloat16)


def local_any(
    tokens,
    lengths,
    cotangent,
    w_qkv,
    b_query,
    b_value,
    w_out,
    b_out,
    first_gain,
    first_shift,
    w_up,
    b_up,
    w_down,
    b_down,
    second_gain,
    second_shift,
):
    lane_count = lax.axis_size("seq")
    seq_count, part_len, model_width = tokens.shape
    full_len = part_len * lane_count
    lane_width = model_width // lane_count
    head_size = HEAD_DIM
    heads_here = lane_width // head_size
    row_count = seq_count * part_len
    offset = lax.axis_index("seq") * part_len
    places = offset + jnp.arange(part_len, dtype=jnp.int32)
    length_row = lengths[0]
    row_live = (places[None, :] < length_row[:, None]).astype(jnp.float32).reshape(row_count, 1)
    key_valid = jnp.arange(full_len, dtype=jnp.int32)[None, :] < length_row[:, None]
    joined_bias = jnp.concatenate([b_query, jnp.zeros_like(b_query), b_value])
    tokens_flat = tokens.reshape(row_count, model_width)
    mixed = jnp.dot(tokens_flat, w_qkv, preferred_element_type=jnp.float32) + joined_bias
    qkv_heads = lax.all_to_all(
        mixed.astype(jnp.bfloat16).reshape(seq_count, part_len, 3, lane_count, lane_width),
        "seq",
        split_axis=3,
        concat_axis=1,
        tiled=True,
    )
    qkv_heads = qkv_heads.reshape(seq_count, full_len, 3, heads_here, head_size)
    context_heads, log_total = lax.map(
        attention_forward_pass,
        (qkv_heads[:, :, 0], qkv_heads[:, :, 1], qkv_heads[:, :, 2], key_valid),
    )
    context_heads = context_heads.reshape(seq_count, full_len, 1, lane_width)
    context_token_rows = lax.all_to_all(
        context_heads, "seq", split_axis=1, concat_axis=2, tiled=True
    ).reshape(row_count, model_width)
    branch = jnp.dot(context_token_rows, w_out, preferred_element_type=jnp.float32) + b_out
    normed_one, inverse_one = normalize(tokens_flat.astype(jnp.float32) + branch)
    hidden = normed_one * first_gain + first_shift
    hidden_low = hidden.astype(jnp.bfloat16)
    preactivation_input = jnp.dot(hidden_low, w_up, preferred_element_type=jnp.float32) + b_up
    active = jax.nn.gelu(preactivation_input, approximate=False).astype(jnp.bfloat16)
    ffn_out = jnp.dot(active, w_down, preferred_element_type=jnp.float32) + b_down
    normed_two, inverse_two = normalize(hidden + ffn_out)
    output_rows = (normed_two * second_gain + second_shift) * row_live
    output_tokens = output_rows.astype(jnp.bfloat16).reshape(seq_count, part_len, model_width)
    grad_out = cotangent.reshape(row_count, model_width).astype(jnp.float32) * row_live
    grad_second_gain = jnp.sum(grad_out * normed_two, axis=0)
    grad_second_shift = jnp.sum(grad_out, axis=0)
    d_sum_two = norm_backward(grad_out, normed_two, inverse_two, second_gain)
    d_ffn = d_sum_two.astype(jnp.bfloat16)
    grad_b_down = jnp.sum(d_ffn.astype(jnp.float32), axis=0)
    grad_w_down = contract_rows(active, d_ffn)
    d_active = times_transposed(d_ffn, w_down)
    gelu_slope = (
        0.5 * (1.0 + lax.erf(preactivation_input * ROOT_HALF))
        + preactivation_input
        * jnp.exp(-0.5 * preactivation_input * preactivation_input)
        * INV_ROOT_TWO_PI
    )
    d_pre = (d_active * gelu_slope).astype(jnp.bfloat16)
    grad_b_up = jnp.sum(d_pre.astype(jnp.float32), axis=0)
    grad_w_up = contract_rows(hidden_low, d_pre)
    d_hidden = d_sum_two + times_transposed(d_pre, w_up)
    grad_first_gain = jnp.sum(d_hidden * normed_one, axis=0)
    grad_first_shift = jnp.sum(d_hidden, axis=0)
    d_sum_one = norm_backward(d_hidden, normed_one, inverse_one, first_gain)
    d_branch = d_sum_one.astype(jnp.bfloat16)
    grad_b_out = jnp.sum(d_branch.astype(jnp.float32), axis=0)
    grad_w_out = contract_rows(context_token_rows, d_branch)
    d_context = times_transposed(d_branch, w_out).astype(jnp.bfloat16)
    d_context = d_context.reshape(seq_count, part_len, lane_count, lane_width)
    d_context_heads = lax.all_to_all(d_context, "seq", split_axis=2, concat_axis=1, tiled=True)
    d_context_heads = d_context_heads.reshape(seq_count, full_len, heads_here, head_size)
    d_qkv_heads = lax.map(
        attend_backward,
        (
            qkv_heads[:, :, 0],
            qkv_heads[:, :, 1],
            qkv_heads[:, :, 2],
            key_valid,
            log_total,
            d_context_heads,
        ),
    )
    d_qkv_heads = d_qkv_heads.reshape(seq_count, full_len, 3, 1, lane_width)
    d_qkv = lax.all_to_all(d_qkv_heads, "seq", split_axis=1, concat_axis=3, tiled=True).reshape(
        row_count, 3 * model_width
    )
    d_qkv_wide = d_qkv.astype(jnp.float32)
    grad_b_query = jnp.sum(d_qkv_wide[:, :model_width], axis=0)
    grad_b_value = jnp.sum(d_qkv_wide[:, 2 * model_width :], axis=0)
    grad_w_qkv = contract_rows(tokens_flat, d_qkv)
    grad_rows = d_sum_one + times_transposed(d_qkv, w_qkv)
    grad_tokens = grad_rows.astype(jnp.bfloat16).reshape(seq_count, part_len, model_width)
    matrices = (grad_w_qkv, grad_w_out, grad_w_up, grad_w_down)
    halfway = (
        lax.psum_scatter(matrices[0], "dp", scatter_dimension=0, tiled=True),
        lax.psum_scatter(matrices[1], "dp", scatter_dimension=0, tiled=True),
        lax.psum_scatter(matrices[2], "dp", scatter_dimension=0, tiled=True),
        lax.psum_scatter(matrices[3], "dp", scatter_dimension=0, tiled=True),
    )
    matrices = (
        lax.psum_scatter(
            halfway[0].astype(jnp.bfloat16), "seq", scatter_dimension=1, tiled=True
        ).astype(jnp.float32),
        lax.psum_scatter(
            halfway[1].astype(jnp.bfloat16), "seq", scatter_dimension=1, tiled=True
        ).astype(jnp.float32),
        lax.psum_scatter(
            halfway[2].astype(jnp.bfloat16), "seq", scatter_dimension=1, tiled=True
        ).astype(jnp.float32),
        lax.psum_scatter(
            halfway[3].astype(jnp.bfloat16), "seq", scatter_dimension=1, tiled=True
        ).astype(jnp.float32),
    )
    vectors = lax.psum(
        (
            grad_b_query,
            grad_b_value,
            grad_b_out,
            grad_first_gain,
            grad_first_shift,
            grad_b_up,
            grad_b_down,
            grad_second_gain,
            grad_second_shift,
        ),
        ("dp", "seq"),
    )
    return (
        output_tokens,
        grad_tokens,
        matrices[0],
        matrices[1],
        matrices[2],
        matrices[3],
        vectors[0],
        vectors[1],
        vectors[2],
        vectors[3],
        vectors[4],
        vectors[5],
        vectors[6],
        vectors[7],
        vectors[8],
    )


DOWN, UP, QKV, DOWN_Z = 0, 1, 2, 3
SPLIT = 48
BLOCKS = ((SPLIT, 384), (96, 768), (96, 768), (192 - SPLIT, 384))
PLAN = (
    ((0, 0, 3), (0, 0, 2), (0, 0, 1), (0, 0, 0),),
    (),
    (),
    ((0, 1, 3), (0, 1, 2),),
    ((0, 1, 1), (0, 1, 0), (1, 0, 3), (1, 0, 0), (1, 0, 2),),
    ((1, 0, 1),),
    ((1, 3, 0),),
    ((1, 1, 2),),
    (),
    (),
    ((1, 1, 3),),
    ((0, 2, 3), (0, 2, 2), (1, 1, 0), (2, 0, 3),),
    ((1, 1, 1), (2, 0, 1), (2, 0, 0),),
    ((2, 1, 3), (2, 3, 0),),
    ((0, 2, 1), (2, 0, 2), (1, 2, 2),),
    ((1, 2, 3), (0, 2, 0), (2, 1, 2), (2, 1, 1), (2, 1, 0), (5, 1, 0), (3, 3, 0), (1, 2, 1), (2, 2, 3), (5, 0, 0), (2, 2, 2), (2, 2, 1), (1, 2, 0), (4, 3, 0),),
    ((2, 2, 0),),
)
X_FIRST = {(0, 0), (0, 1), (1, 0), (1, 2), (2, 2)}
ORDER_D = (3, 2, 1, 0)

B_QUERY, B_VALUE, B_OUT, FIRST_GAIN, FIRST_SHIFT, B_DOWN, SECOND_GAIN, SECOND_SHIFT, B_UP = range(9)

ROWS = 256
TILE = 256
PART = 128
WIDTH = 768
STEP = 128


def place():
    row, lane = lax.axis_index("dp"), lax.axis_index("seq")
    return row // 2, row % 2, lane // 2, lane % 2


def device(z, y, x, core):
    return (z * 2 + y, x * 2 + core)


def remote(source, target, send, receive, where):
    return pltpu.make_async_remote_copy(
        src_ref=source,
        dst_ref=target,
        send_sem=send,
        recv_sem=receive,
        device_id=where,
        device_id_type=MESH_ID,
    )


def dot(left, right):
    return jnp.dot(left, right, preferred_element_type=F32)


def dot_t(left, right):
    return lax.dot_general(left, right, (((1,), (1,)), ((), ())), preferred_element_type=F32)


def fold(rows):
    return jnp.sum(rows.reshape(rows.shape[0] // 8, 8, rows.shape[1]), axis=0)


def mean(rows):
    return jnp.sum(rows, axis=-1, keepdims=True) * (1.0 / WIDTH)


def layer_kernel(
    tokens_in, lengths_in, cot_in, w_qkv_in, w_out_in, w_up_in, w_down_in,
    b_query_in, b_value_in, b_out_in, first_gain_in, first_shift_in, b_up_in, b_down_in, second_gain_in, second_shift_in,
    tokens_out, grad_out, down_hbm, up_hbm, qkv_hbm, vec_hbm,
    w_qkv, w_out, w_up, w_down, par, tok, cot, q3, k3, v3, bias, probs, hidden, xhat, rstd, low, d_ffn, slope, wide, total, held, turned, inverse, d_scores,
    dsum, dctx3, dkv_own, dkv_send, dkv_in, dq_t, dqkv_flat, out_rows, grad_rows,
    act, dpre, dffn_t, hid_t, tok_t, ctx_t, dqkv, dbr,
    sums_0, sums_1, sums_2, sums_z, in1_0, in1_1, in1_2, in2_0, in2_1, in2_2, in3_0, in3_1, in3_2, in1_z, in2_z, in3_z,
    vec_mine, vec_in, down_out, up_out, qkv_out, vec_out,
    load, ex_send, ex_recv, core_send, core_recv, act_send, act_recv,
    send1, recv1, send2, recv2, send3, recv3, send_z, recv_z, vec_send, vec_recv, vec_load,
    held_0, held_1, held_2, held_3, held_4, held_5, held_6, held_7, held_8,
):
    z, y, x, core = place()
    sums, in1, in2, in3 = (sums_0, sums_1, sums_2), (in1_0, in1_1, in1_2), (in2_0, in2_1, in2_2), (in3_0, in3_1, in3_2)
    at_core = device(z, y, x, 1 - core)
    at_x = device(z, y, 1 - x, core)
    at_y = device(z, 1 - y, x, core)
    at_place = [z, z + 1 - 2 * (z % 2), (z + 2) % 4, 3 - z]
    at_z1 = device(at_place[1], y, x, core)
    at_z2 = device(at_place[2], y, x, core)

    loads = [pltpu.make_async_copy(tokens_in.at[x], tok.at[pl.ds(0, PART)], load.at[0])]
    for n, s in enumerate((1, 2, 0)):
        loads.append(
            pltpu.make_async_copy(
                w_qkv_in.at[:, pl.ds(WIDTH * s, WIDTH)], w_qkv.at[:, pl.ds(WIDTH * s, WIDTH)], load.at[1 + n]
            )
        )
    loads.append(pltpu.make_async_copy(cot_in.at[x], cot.at[pl.ds(0, PART)], load.at[4]))
    loads.append(pltpu.make_async_copy(w_out_in, w_out, load.at[5]))
    for t in range(4):
        loads.append(pltpu.make_async_copy(w_up_in.at[:, pl.ds(WIDTH * t, WIDTH)], w_up.at[t], load.at[6 + t]))
    for t in range(4):
        loads.append(pltpu.make_async_copy(w_down_in.at[pl.ds(WIDTH * t, WIDTH)], w_down.at[t], load.at[10 + t]))
    for copy in loads[0:4]:
        copy.start()

    vec_refs = {
        B_QUERY: (b_query_in, held_0), B_VALUE: (b_value_in, held_1), B_OUT: (b_out_in, held_2), FIRST_GAIN: (first_gain_in, held_3),
        FIRST_SHIFT: (first_shift_in, held_4), B_DOWN: (b_down_in, held_5), SECOND_GAIN: (second_gain_in, held_6),
        SECOND_SHIFT: (second_shift_in, held_7), B_UP: (b_up_in, held_8),
    }
    vec_loads = [
        pltpu.make_async_copy(source, vector, vec_load.at[n]) for n, (source, vector) in enumerate(vec_refs.values())
    ]
    for copy in vec_loads:
        copy.start()

    barrier = pltpu.get_barrier_semaphore()
    for where in (at_core, at_x, at_y, at_z1, at_z2):
        pl.semaphore_signal(barrier, inc=1, device_id=where, device_id_type=MESH_ID)
    pl.semaphore_wait(barrier, 5)

    get_tok = remote(tokens_in.at[1 - x], tok.at[pl.ds(PART, PART)], ex_send.at[0], ex_recv.at[0], at_x)
    get_cot = remote(cot_in.at[1 - x], cot.at[pl.ds(PART, PART)], ex_send.at[1], ex_recv.at[1], at_x)
    get_tok.start()

    core_copies = []

    def to_core(source, target):
        n = len(core_copies)
        copy = remote(source, target, core_send.at[n], core_recv.at[n], at_core)
        copy.start()
        core_copies.append(copy)
        return copy

    for copy in vec_loads:
        copy.wait()
    for row, (_, vector) in vec_refs.items():
        if row == B_UP:
            for t in range(4):
                par[B_UP + t : B_UP + t + 1, :] = vector[WIDTH * t : WIDTH * (t + 1)].reshape(1, WIDTH)
        else:
            par[row : row + 1, :] = vector[...].reshape(1, WIDTH)
    vec_mine[0] = jnp.zeros((16, WIDTH), F32)
    length = lengths_in[0, x]
    mine, across = 2 * x + core, 2 * (1 - x) + core
    theirs, theirs_across = 2 * x + 1 - core, 2 * (1 - x) + 1 - core

    def positions(shape, starts):
        n = lax.broadcasted_iota(jnp.int32, shape, 0)
        first = starts[-1] * PART
        for b in range(len(starts) - 2, -1, -1):
            first = jnp.where(n < PART * (b + 1), starts[b] * PART, first)
        return first + n % PART

    bias[...] = jnp.where(positions((512, ROWS), (mine, across, theirs, theirs_across)) < length, 0.0, -1e30)

    kv_copies = []
    for b in range(2):
        rows = slice(PART * b, PART * (b + 1))
        if b == 0:
            loads[0].wait()
        else:
            get_tok.wait_recv()
            get_cot.start()
            for copy in loads[4:14]:
                copy.start()
        for n, s in enumerate((1, 2, 0)):
            if b == 0:
                loads[1 + n].wait()
            part = dot(tok[rows, :], w_qkv[:, WIDTH * s : WIDTH * (s + 1)])
            if s == 0:
                part = part + par[B_QUERY : B_QUERY + 1, :]
            if s == 2:
                part = part + par[B_VALUE : B_VALUE + 1, :]
            part = part.astype(BF16)
            if s == 0:
                part = part * jnp.asarray(0.125, BF16)
            heads = (q3, k3, v3)[s]
            for j in range(6):
                heads[j, rows, :] = part[:, 128 * j : 128 * (j + 1)]
            if s:
                kv_copies.append(
                    to_core(heads.at[:, pl.ds(PART * b, PART)], heads.at[:, pl.ds(ROWS + PART * b, PART)])
                )
    tok_t[:, 0:ROWS] = tok[...].T
    qkv_copies = [to_core(tok_t.at[:, pl.ds(0, ROWS)], tok_t.at[:, pl.ds(ROWS, ROWS)])]
    for copy in kv_copies:
        copy.wait_recv()

    low_half = lax.broadcasted_iota(jnp.int32, (ROWS, 128), 1) < 64

    def half_of(pair, h):
        zeros = jnp.zeros_like(pair)
        return jnp.where(low_half, pair, zeros) if h == 0 else jnp.where(low_half, zeros, pair)

    for j in range(6):
        turned[j] = v3[j].T
    highest = {}

    def score(n):
        queries = half_of(q3[n // 2], n % 2)
        top = None
        for t in range(0, 512, TILE):
            scores = dot_t(k3[n // 2, t : t + TILE], queries) + bias[t : t + TILE, :]
            held[n % 2, t : t + TILE, :] = scores
            part = jnp.max(scores.reshape(TILE // 8, 8, ROWS), axis=0)
            top = part if top is None else jnp.maximum(top, part)
        highest[n] = jnp.max(top, axis=0, keepdims=True)

    def weigh(n):
        sums = None
        for t in range(0, 512, TILE):
            exponent = jnp.exp(held[n % 2, t : t + TILE, :] - highest[n])
            part = fold(exponent)
            sums = part if sums is None else sums + part
            probs[n, t : t + TILE, :] = exponent.astype(BF16)
        inverse[n : n + 1, :] = 1.0 / jnp.sum(sums, axis=0, keepdims=True)

    def gather(n):
        context = dot(turned[n // 2, 64 * (n % 2) : 64 * (n % 2 + 1)], probs[n]) * inverse[n : n + 1, :]
        ctx_t[64 * n : 64 * (n + 1), 0:ROWS] = context.astype(BF16)

    score(0)
    for n in range(12):
        if n < 11:
            score(n + 1)
        weigh(n)
        if n:
            gather(n - 1)
    gather(11)
    qkv_copies.append(to_core(ctx_t.at[:, pl.ds(0, ROWS)], ctx_t.at[:, pl.ds(ROWS, ROWS)]))

    loads[5].wait()

    def first_norm(r):
        rows = pl.ds(STEP * r, STEP)
        branch = dot(ctx_t[:, STEP * r : STEP * (r + 1)].T, w_out[...]) + par[B_OUT : B_OUT + 1, :]
        value = tok[rows, :].astype(F32) + branch
        center = value - mean(value)
        root = lax.rsqrt(mean(center * center) + EPSILON)
        normed = center * root
        out = normed * par[FIRST_GAIN : FIRST_GAIN + 1, :] + par[FIRST_SHIFT : FIRST_SHIFT + 1, :]
        xhat[rows, :] = normed
        rstd[rows, :] = root
        hidden[rows, :] = out
        low[rows, :] = out.astype(BF16)
        return 0

    for r in range(ROWS // STEP):
        first_norm(r)
    up_copies = []

    for n in range(6, 14):
        loads[n].wait()

    def act_copy(t):
        return remote(act.at[t, pl.ds(0, ROWS)], act.at[t, pl.ds(ROWS, ROWS)], act_send.at[t], act_recv.at[t], at_core)

    for t in range(4):
        u = dot(low[...], w_up[t]) + par[B_UP + t : B_UP + t + 1, :]
        phi = 0.5 * (1.0 + lax.erf(u * ROOT_HALF))
        active = (u * phi).astype(BF16)
        act[t, 0:ROWS, :] = active
        slope[t] = phi + u * jnp.exp(-0.5 * u * u) * INV_ROOT_TWO_PI
        act_copy(t).start()
        product = dot(active, w_down[t])
        total[...] = total[...] + product if t else product

    loads[4].wait()
    get_cot.wait_recv()

    def live_rows(r):
        n = lax.broadcasted_iota(jnp.int32, (STEP, 1), 0) + STEP * r
        return jnp.where(jnp.where(n < PART, mine * PART + n, across * PART + n - PART) < length, 1.0, 0.0)

    def second_norm(r):
        rows = pl.ds(STEP * r, STEP)
        value = hidden[rows, :] + (total[rows, :] + par[B_DOWN : B_DOWN + 1, :])
        center = value - mean(value)
        root = lax.rsqrt(mean(center * center) + EPSILON)
        normed = center * root
        wide[rows, :] = normed
        e = cot[rows, :].astype(F32) * live_rows(r) * par[SECOND_GAIN : SECOND_GAIN + 1, :]
        d = root * (e - mean(e) - normed * mean(e * normed))
        dsum[rows, :] = d
        d_ffn[rows, :] = d.astype(BF16)
        return 0

    for r in range(ROWS // STEP):
        second_norm(r)

    def second_norm_rest(r, carry):
        rows = pl.ds(pl.multiple_of(STEP * r, STEP), STEP)
        live, normed = live_rows(r), wide[rows, :]
        out = (normed * par[SECOND_GAIN : SECOND_GAIN + 1, :] + par[SECOND_SHIFT : SECOND_SHIFT + 1, :]) * live
        out_rows[rows, :] = out.astype(BF16)
        grad = cot[rows, :].astype(F32) * live
        gain, shift, down = carry
        return gain + fold(grad * normed), shift + fold(grad), down + fold(d_ffn[rows, :].astype(F32))

    zero = jnp.zeros((8, WIDTH), F32)

    def put(row, partial):
        vec_mine[0, row : row + 1, :] = jnp.sum(partial, axis=0, keepdims=True)

    out_local = pltpu.make_async_copy(out_rows.at[pl.ds(0, PART)], tokens_out.at[x], load.at[14])
    out_across = remote(out_rows.at[pl.ds(PART, PART)], tokens_out.at[x], ex_send.at[2], ex_recv.at[2], at_x)
    dffn_all = d_ffn[...].T
    for j in range(4):
        dffn_t[j, :, 0:ROWS] = dffn_all[192 * j : 192 * (j + 1), :]
    down_copies = []
    for j in (0, 2):
        there = j + 1 - core
        down_copies.append(to_core(dffn_t.at[there, :, pl.ds(0, ROWS)], dffn_t.at[there, :, pl.ds(ROWS, ROWS)]))

    def first(m, k):
        zk = at_place[k]
        if (m, k) in X_FIRST:
            return remote(sums[m].at[1 - x, zk], in1[m].at[zk], send1.at[m, k], recv1.at[m, k], at_x)
        return remote(sums[m].at[:, zk, 1 - y], in1[m].at[zk], send1.at[m, k], recv1.at[m, k], at_y)

    def second(m, k):
        zk = at_place[k]
        if (m, k) in X_FIRST:
            return remote(sums[m].at[x, zk, 1 - y], in2[m].at[zk], send2.at[m, k], recv2.at[m, k], at_y)
        return remote(sums[m].at[1 - x, zk, y], in2[m].at[zk], send2.at[m, k], recv2.at[m, k], at_x)

    def third(m, k):
        zk = at_place[k]
        slot, where = ((0, at_z1), (2, at_z2), (1, at_z1))[k - 1]
        return remote(sums[m].at[x, zk, y], in3[m].at[slot], send3.at[m, k], recv3.at[m, k], where)

    def add_first(m, k):
        zk = at_place[k]
        if (m, k) in X_FIRST:
            sums[m][x, zk] = sums[m][x, zk] + in1[m][zk]
        else:
            for b in range(2):
                sums[m][b, zk, y] = sums[m][b, zk, y] + in1[m][zk, b]

    def add_second(m, k):
        zk = at_place[k]
        block = sums[m][x, zk, y] + in2[m][zk]
        if k == 2:
            third(m, 3).wait_recv()
            block = block + in3[m][1]
        sums[m][x, zk, y] = block

    z_near = [
        remote(sums_z.at[:, at_place[k]], in1_z.at[n], send_z.at[n], recv_z.at[n], at_z1) for n, k in enumerate((1, 3))
    ]
    z_far = remote(sums_z.at[:, at_place[2]], in1_z.at[2], send_z.at[2], recv_z.at[2], at_z2)
    z_second = remote(sums_z.at[1 - x, z], in2_z, send_z.at[3], recv_z.at[3], at_x)
    z_third = remote(sums_z.at[x, z, 1 - y], in3_z, send_z.at[4], recv_z.at[4], at_y)

    def at_z_first(step):
        if step == 1:
            z_near[1].wait_recv()
            for b in range(2):
                sums_z[b, at_place[2]] = sums_z[b, at_place[2]] + in1_z[1, b]
            z_far.start()
        elif step == 2:
            z_near[0].wait_recv()
            z_far.wait_recv()
            for b in range(2):
                sums_z[b, z] = (sums_z[b, z].astype(F32) + in1_z[0, b].astype(F32) + in1_z[2, b].astype(F32)).astype(BF16)
            z_second.start()
        elif step == 3:
            z_second.wait_recv()
            sums_z[x, z] = sums_z[x, z] + in2_z[...]
            z_third.start()
        else:
            z_third.wait_recv()
            down_out[SPLIT:192, :] = sums_z[x, z, y].astype(F32) + in3_z[...].astype(F32)

    def at(point):
        for step, m, k in PLAN[point]:
            if step == 5:
                (out_across, grad_across)[m].start()
                continue
            if m == DOWN_Z:
                at_z_first(step)
                continue
            if step == 0:
                first(m, k).start()
            elif step == 1:
                first(m, k).wait_recv()
                add_first(m, k)
                second(m, k).start()
            else:
                second(m, k).wait_recv()
                add_second(m, k)
                if k:
                    third(m, k).start()

    before = [dsum]

    def feed_back(t):
        d_pre = (dot_t(d_ffn[...], w_down[t]) * slope[t]).astype(BF16)
        dpre[t, 0:ROWS, :] = d_pre
        vec_mine[0, pl.ds(B_UP + t, 1), :] = jnp.sum(fold(d_pre.astype(F32)), axis=0, keepdims=True)
        total[...] = before[-1][...] + dot_t(d_pre, w_up[t])
        before.append(total)

    for j in (0, 2):
        there = j + 1 - core
        feed_back(there)
        up_copies.append(to_core(dpre.at[there, pl.ds(0, ROWS)], dpre.at[there, pl.ds(ROWS, ROWS)]))

    for t in range(4):
        act_copy(t).wait_recv()
    for copy in down_copies:
        copy.wait_recv()
    left = jnp.concatenate([dffn_t[core], dffn_t[2 + core]], axis=0)
    for k in ORDER_D:
        t = at_place[k]
        part = dot(left, act[t]).astype(BF16)
        for b in range(2):
            for h in range(2):
                sums_0[b, t, h] = part[192 * b : 192 * b + SPLIT, 384 * h : 384 * (h + 1)]
                sums_z[b, t, h] = part[192 * b + SPLIT : 192 * (b + 1), 384 * h : 384 * (h + 1)]
        if k % 2:
            z_near[k // 2].start()
        if (0, DOWN, k) in PLAN[0]:
            first(DOWN, k).start()
    hid_t[:, 0:ROWS] = low[...].T
    up_copies.append(to_core(hid_t.at[:, pl.ds(0, ROWS)], hid_t.at[:, pl.ds(ROWS, ROWS)]))
    for n, j in enumerate((0, 2)):
        feed_back(j + core)
        at(1 + n)
    for copy in up_copies:
        copy.wait_recv()
    for b in range(2):
        for n in range(3):
            part = dot(hid_t[...], dpre[2 * b + core, :, 256 * n : 256 * (n + 1)]).astype(BF16)
            sums_1[b, :, :, :, 256 * n : 256 * (n + 1)] = part.reshape(4, 2, 96, 256)
    at(3)
    gain, shift, down = lax.fori_loop(0, ROWS // STEP, second_norm_rest, (zero, zero, zero))
    put(SECOND_GAIN, gain)
    put(SECOND_SHIFT, shift)
    put(B_DOWN, down)
    out_local.start()

    def first_norm_back(r, carry):
        rows = pl.ds(pl.multiple_of(STEP * r, STEP), STEP)
        d_hidden, normed = total[rows, :], xhat[rows, :]
        e = d_hidden * par[FIRST_GAIN : FIRST_GAIN + 1, :]
        d = rstd[rows, :] * (e - mean(e) - normed * mean(e * normed))
        dsum[rows, :] = d
        d_low = d.astype(BF16)
        low[rows, :] = d_low
        gain, shift, out = carry
        return gain + fold(d_hidden * normed), shift + fold(d_hidden), out + fold(d_low.astype(F32))

    gain, shift, out = lax.fori_loop(0, ROWS // STEP, first_norm_back, (zero, zero, zero))
    put(FIRST_GAIN, gain)
    put(FIRST_SHIFT, shift)
    put(B_OUT, out)
    for j in range(4):
        dbr[j, 0:ROWS, :] = jnp.concatenate([jnp.zeros((ROWS, 64), BF16), low[:, 192 * j : 192 * (j + 1)]], axis=1)
    for j in (0, 2):
        there = j + 1 - core
        qkv_copies.append(to_core(dbr.at[there, pl.ds(0, ROWS)], dbr.at[there, pl.ds(ROWS, ROWS)]))
    d_context = dot_t(low[...], w_out[...]).astype(BF16)
    for j in range(6):
        dctx3[j] = d_context[:, 128 * j : 128 * (j + 1)]

    at(4)

    for j in range(6):
        turned[j] = k3[j].T
    inverse_t = inverse[...].T
    inner, d_heads, partial_values, partial_keys = {}, {}, {}, {}

    def probs_back(n):
        d_head = (half_of(dctx3[n // 2], n % 2).astype(F32) * inverse_t[:, n : n + 1]).astype(BF16)
        sums = None
        for t in range(0, 512, TILE):
            d_probs = dot_t(v3[n // 2, t : t + TILE], d_head)
            held[n % 2, t : t + TILE, :] = d_probs
            part = fold(probs[n, t : t + TILE, :].astype(F32) * d_probs)
            sums = part if sums is None else sums + part
        inner[n] = jnp.sum(sums, axis=0, keepdims=True) * inverse[n : n + 1, :]
        partial_values[n] = dot(probs[n], d_head)

    def scores_back(n):
        for t in range(0, 512, TILE):
            d = probs[n, t : t + TILE, :].astype(F32) * (held[n % 2, t : t + TILE, :] - inner[n])
            d_scores[n % 2, t : t + TILE, :] = d.astype(BF16)

    def keys_back(n):
        j, h = n // 2, n % 2
        d_queries = dot(turned[j, 64 * h : 64 * (h + 1)], d_scores[h]) * 0.125
        dq_t[64 * n : 64 * (n + 1), :] = d_queries.astype(BF16)
        partial_keys[n] = dot(d_scores[h], half_of(q3[j], h))
        if h:
            for s, partial in enumerate((partial_keys, partial_values)):
                total_pair = partial[n - 1] + partial[n]
                dkv_own[s, j] = total_pair[0:ROWS]
                dkv_send[s, j] = total_pair[ROWS:].astype(BF16)

    def attend_back(start, stop):
        probs_back(start)
        for n in range(start, stop):
            if n < stop - 1:
                probs_back(n + 1)
            scores_back(n)
            if n > start:
                keys_back(n - 1)
        keys_back(stop - 1)

    attend_back(0, 6)
    back_copies = [to_core(dkv_send.at[:, pl.ds(0, 3)], dkv_in.at[:, pl.ds(0, 3)])]
    at(5)
    attend_back(6, 12)
    back_copies.append(to_core(dkv_send.at[:, pl.ds(3, 3)], dkv_in.at[:, pl.ds(3, 3)]))
    at(6)
    d_queries = dq_t[...].T
    dqkv_flat[:, 0:WIDTH] = d_queries
    put(B_QUERY, fold(d_queries.astype(F32)))
    at(7)
    for copy in back_copies:
        copy.wait_recv()
    at(8)
    for j in range(6):
        for s in range(2):
            d = (dkv_own[s, j] + dkv_in[s, j].astype(F32)).astype(BF16)
            dqkv_flat[:, WIDTH * (1 + s) + 128 * j : WIDTH * (1 + s) + 128 * (j + 1)] = d
            if s:
                vec_mine[0, B_VALUE : B_VALUE + 1, 128 * j : 128 * (j + 1)] = jnp.sum(d.astype(F32), axis=0, keepdims=True)
    for j in range(4):
        dqkv[j, 0:ROWS, :] = jnp.concatenate(
            [dqkv_flat[:, 576 * j : 576 * (j + 1)], jnp.zeros((ROWS, 64), BF16)], axis=1
        )
    for j in (0, 2):
        there = j + 1 - core
        qkv_copies.append(to_core(dqkv.at[there, pl.ds(0, ROWS)], dqkv.at[there, pl.ds(ROWS, ROWS)]))
    vec_steps = [
        remote(vec_mine.at[s], vec_in.at[s], vec_send.at[s], vec_recv.at[s], w)
        for s, w in enumerate((at_core, at_x, at_y, at_z1, at_z2))
    ]
    vec_steps[0].start()
    at(9)

    for copy in qkv_copies:
        copy.wait_recv()
    at(10)
    for b in range(2):
        one = dot(tok_t[...], dqkv[2 * b + core])
        two = dot(ctx_t[...], dbr[2 * b + core])
        part = jnp.concatenate([one[:, 0:512], one[:, 512:640] + two[:, 0:128], two[:, 128:256]], axis=1).astype(BF16)
        sums_2[b] = part.reshape(4, 2, 96, WIDTH)
    at(11)
    vec_steps[0].wait_recv()
    vec_mine[1] = vec_mine[0] + vec_in[0]
    vec_steps[1].start()
    grad_rows[...] = (dsum[...] + dot_t(dqkv_flat[...], w_qkv[...])).astype(BF16)
    grad_local = pltpu.make_async_copy(grad_rows.at[pl.ds(0, PART)], grad_out.at[x], load.at[15])
    grad_across = remote(grad_rows.at[pl.ds(PART, PART)], grad_out.at[x], ex_send.at[3], ex_recv.at[3], at_x)
    grad_local.start()
    at(12)
    vec_steps[1].wait_recv()
    vec_mine[2] = vec_mine[1] + vec_in[1]
    vec_steps[2].start()
    at(13)
    vec_steps[2].wait_recv()
    vec_mine[3] = vec_mine[2] + vec_in[2]
    vec_steps[3].start()
    at(14)
    vec_steps[3].wait_recv()
    vec_mine[4] = vec_mine[3] + vec_in[3]
    vec_steps[4].start()
    at(15)
    vec_steps[4].wait_recv()
    vec_out[...] = vec_mine[4] + vec_in[4]
    results = [pltpu.make_async_copy(vec_out, vec_hbm, load.at[19])]
    results[0].start()

    def finish_block(m):
        out, target = ((down_out, down_hbm), (up_out, up_hbm), (qkv_out, qkv_hbm))[m]
        third(m, 1).wait_recv()
        third(m, 2).wait_recv()
        block = sums[m][x, z, y].astype(F32) + in3[m][0].astype(F32) + in3[m][2].astype(F32)
        out[0 : BLOCKS[m][0], :] = block
        results.append(pltpu.make_async_copy(out, target, load.at[16 + m]))
        results[-1].start()

    finish_block(DOWN)
    finish_block(UP)
    at(16)
    finish_block(QKV)

    out_across.wait_recv()
    grad_across.wait_recv()
    out_local.wait()
    grad_local.wait()
    for copy in results:
        copy.wait()
    for copy in [get_tok, get_cot, out_across, grad_across] + core_copies + vec_steps:
        copy.wait_send()
    for t in range(4):
        act_copy(t).wait_send()
    for copy in z_near + [z_far, z_second, z_third]:
        copy.wait_send()
    for m in (DOWN, UP, QKV):
        for k in range(4):
            first(m, k).wait_send()
            second(m, k).wait_send()
            if k:
                third(m, k).wait_send()


def finish_kernel(
    tokens_in, grad_in, down_in, up_in, joined_in, vec_in,
    tokens_out, grad_out, qkv_out, out_out, up_out, down_out,
    b_query, b_value, b_out, first_gain, first_shift, b_up, b_down, second_gain, second_shift,
    tokens, grad, down, up, joined, vec, qkv, out, vec_0, vec_1, vec_2, vec_3, vec_4, vec_5, vec_6, vec_7, vec_8, get, give,
):
    pairs = ((joined_in, joined), (vec_in, vec), (tokens_in, tokens), (grad_in, grad), (down_in, down), (up_in, up))
    gets = [pltpu.make_async_copy(source, held, get.at[n]) for n, (source, held) in enumerate(pairs)]
    for copy in gets:
        copy.start()
    gives = []

    def put(held, target):
        gives.append(pltpu.make_async_copy(held, target, give.at[len(gives)]))
        gives[-1].start()

    for n, (held, target) in ((2, (tokens, tokens_out)), (3, (grad, grad_out)), (4, (down, down_out)), (5, (up, up_out))):
        gets[n].wait()
        put(held, target)
    gets[0].wait()
    qkv[...] = joined[:, 0:576]
    put(qkv, qkv_out)
    out[...] = joined[:, 576:WIDTH]
    put(out, out_out)
    gets[1].wait()
    for row, held, target in (
        (B_QUERY, vec_0, b_query), (B_VALUE, vec_1, b_value), (B_OUT, vec_2, b_out), (FIRST_GAIN, vec_3, first_gain),
        (FIRST_SHIFT, vec_4, first_shift), (B_DOWN, vec_5, b_down), (SECOND_GAIN, vec_6, second_gain),
        (SECOND_SHIFT, vec_7, second_shift),
    ):
        held[...] = vec[row, :]
        put(held, target)
    for t in range(4):
        vec_8[WIDTH * t : WIDTH * (t + 1)] = vec[B_UP + t, :]
    put(vec_8, b_up)
    for copy in gives:
        copy.wait()


def finish(out_tokens, grad_tokens, down, up, joined, vectors):
    hbm = pl.BlockSpec(memory_space=pl.ANY)
    W = WIDTH
    shapes = [out_tokens.shape] * 2 + [(96, 576), (96, 192), up.shape, down.shape] + [(W,)] * 5 + [(4 * W,)] + [(W,)] * 3
    inputs = (out_tokens, grad_tokens, down, up, joined, vectors)
    scratch = [pltpu.VMEM(a.shape, a.dtype) for a in inputs] + [pltpu.VMEM((96, 576), F32), pltpu.VMEM((96, 192), F32)]
    scratch += [pltpu.VMEM((W,), F32)] * 8 + [pltpu.VMEM((4 * W,), F32)]
    outs = pl.pallas_call(
        finish_kernel,
        name="finish",
        out_shape=tuple(jax.ShapeDtypeStruct(s, BF16 if n < 2 else F32) for n, s in enumerate(shapes)),
        in_specs=[hbm] * 6,
        out_specs=(hbm,) * 15,
        scratch_shapes=scratch + [pltpu.SemaphoreType.DMA((6,)), pltpu.SemaphoreType.DMA((15,))],
    )(*inputs)
    return outs[:5] + (outs[5].T,) + outs[6:]


def local(
    tokens, lengths, cotangent, w_qkv, b_query, b_value, w_out, b_out, first_gain, first_shift, w_up, b_up, w_down, b_down,
    second_gain, second_shift,
):
    hbm = pl.BlockSpec(memory_space=pl.ANY)
    dma = pltpu.SemaphoreType.DMA
    B, W = pltpu.VMEM, WIDTH
    scratch = [
        B((W, 3 * W), BF16), B((W, W), BF16), B((4, W, W), BF16), B((4, W, W), BF16), B((16, W), F32),
        B((ROWS, W), BF16), B((ROWS, W), BF16),
        B((6, ROWS, 128), BF16), B((6, 512, 128), BF16), B((6, 512, 128), BF16),
        B((512, ROWS), F32), B((12, 512, ROWS), BF16),
        B((ROWS, W), F32), B((ROWS, W), F32), B((ROWS, 1), F32), B((ROWS, W), BF16), B((ROWS, W), BF16),
        B((4, ROWS, W), F32), B((ROWS, W), F32), B((ROWS, W), F32),
        B((2, 512, ROWS), F32), B((6, 128, 512), BF16), B((16, ROWS), F32), B((2, 512, ROWS), BF16), B((ROWS, W), F32),
        B((6, ROWS, 128), BF16), B((2, 6, ROWS, 128), F32), B((2, 6, ROWS, 128), BF16), B((2, 6, ROWS, 128), BF16),
        B((W, ROWS), BF16), B((ROWS, 3 * W), BF16), B((ROWS, W), BF16), B((ROWS, W), BF16),
        B((4, 512, W), BF16), B((4, 512, W), BF16), B((4, 192, 512), BF16),
        B((W, 512), BF16), B((W, 512), BF16), B((W, 512), BF16), B((4, 512, 640), BF16), B((4, 512, 256), BF16),
    ]
    scratch += [B((2, 4, 2) + block, BF16) for block in BLOCKS]
    scratch += [B((4, 2) + block, BF16) for block in BLOCKS[:DOWN_Z]]
    scratch += [B((4,) + block, BF16) for block in BLOCKS[:DOWN_Z]]
    scratch += [B((3,) + block, BF16) for block in BLOCKS[:DOWN_Z]]
    scratch += [B((3, 2, 2) + BLOCKS[DOWN_Z], BF16), B((2,) + BLOCKS[DOWN_Z], BF16), B(BLOCKS[DOWN_Z], BF16)]
    scratch += [B((5, 16, W), F32), B((5, 16, W), F32)]
    scratch += [B((192, 384), F32), B(BLOCKS[UP], F32), B(BLOCKS[QKV], F32), B((16, W), F32)]
    scratch += [dma((20,)), dma((4,)), dma((4,)), dma((24,)), dma((24,)), dma((4,)), dma((4,))]
    scratch += [dma((3, 4))] * 6 + [dma((5,)), dma((5,)), dma((5,)), dma((5,)), dma((9,))] + [B((W,), F32)] * 8 + [B((4 * W,), F32)]
    results = pl.pallas_call(
        layer_kernel,
        name="layer",
        out_shape=(
            jax.ShapeDtypeStruct(tokens.shape, BF16),
            jax.ShapeDtypeStruct(tokens.shape, BF16),
            jax.ShapeDtypeStruct((192, 384), F32),
            jax.ShapeDtypeStruct(BLOCKS[UP], F32),
            jax.ShapeDtypeStruct(BLOCKS[QKV], F32),
            jax.ShapeDtypeStruct((16, W), F32),
        ),
        in_specs=[hbm, pl.BlockSpec(memory_space=pltpu.SMEM)] + [hbm] * 14,
        out_specs=(hbm,) * 6,
        scratch_shapes=scratch,
        compiler_params=pltpu.CompilerParams(
            collective_id=1, has_side_effects=True, vmem_limit_bytes=63 * 1024 * 1024
        ),
    )(
        tokens, lengths, cotangent, w_qkv, w_out, w_up, w_down,
        b_query, b_value, b_out, first_gain, first_shift, b_up, b_down, second_gain, second_shift,
    )
    return finish(*results)


def solution(mesh):
    in_specs = (
        P("dp", "seq", None),
        P("dp", None),
        P("dp", "seq", None),
        P(),
        P(),
        P(),
        P(),
        P(),
        P(),
        P(),
        P(),
        P(),
        P(),
        P(),
        P(),
        P(),
    )
    out_specs = (
        P("dp", "seq", None),
        P("dp", "seq", None),
        P("dp", "seq"),
        P("dp", "seq"),
        P("dp", "seq"),
        P("dp", "seq"),
        P(),
        P(),
        P(),
        P(),
        P(),
        P(),
        P(),
        P(),
        P(),
    )
    return jax.shard_map(
        local if dict(mesh.shape) == {"dp": 8, "seq": 4} else local_any, mesh=mesh, in_specs=in_specs, out_specs=out_specs, check_vma=False)
```
